32 devices in a mesh: docs: 32 (over z, y, x, core), pb: 1.
Axes of the slice: x: 2, y: 2, z: 4, core: 2. Of those that a mesh axis runs over, the one named last changes fastest.
Arguments:
- queries: bfloat16 [1024, 32, 128], P('docs', 'pb'), may hold values from -0.1875 to 0.1875
- documents: bfloat16 [4096, 64, 128], P('docs'), may hold values from -1.75 to 1.75
- lengths: int32 [4096], P('docs'), may hold values from 1 to 64
- pattern: int32 [8, 32], replicated, may hold values from 0 to 1
Outputs:
- scores: float32 [32, 32, 4096], P(None, 'pb', 'docs')
The draws below stay inside these ranges and needn't reach their ends.
All inputs are finite; a program needn't handle non-finite values.
Results may differ from the reference program's by a relative error of at most 0.0003.
Values may be sent and summed in bfloat16 or wider, within the bound.
No kernel may reach another device: no remote copies, remote signals or barrier semaphores. Data moves between devices by JAX's collectives and lax.ppermute only.
A program may use at most 64 MiB of HBM per device.

```python
import jax
import jax.numpy as jnp
from jax import lax

DIM = 128
QTOK = 32
DTOK = 64
BLOCK = 128
QBLK = 8
NQ = 1024
QROW = 32
DBLK = 32
NDOC = 4096


def draw_pattern(key, part):
    level_key, roll_key = jax.random.split(key)
    levels = jax.random.randint(level_key, (1, DBLK), 0, 5)
    dice_rolls = jax.random.randint(roll_key, (QBLK, DBLK), 0, 16)
    return (dice_rolls < levels).astype(jnp.int32)


def touch_ends(entries, stream_key, low, high):
    longest = entries.shape.index(max(entries.shape))
    spots = []
    for shift in (0, 1):
        where = [jax.random.randint(jax.random.fold_in(stream_key, axis), (), 0, length) for axis, length in enumerate(entries.shape)]
        where[longest] = (where[longest] + shift) % entries.shape[longest]
        spots.append(tuple(where))
    return entries.at[spots[0]].set(low).at[spots[1]].set(high)


def block_scale(rng, extent, shards, low, top_value):
    def one(dim, blocks):
        steps = jax.random.uniform(jax.random.fold_in(jax.random.fold_in(rng, 6), dim), (blocks,), jnp.float32, low / len(shards), top_value / len(shards))
        return jnp.repeat(jnp.exp(steps), extent[dim] // blocks).reshape((-1,) + (1,) * (len(extent) - dim - 1))

    loudness = one(*shards[0])
    for cut in shards[1:]:
        loudness = loudness * one(*cut)
    return loudness


def scatter_about(stream_key, shape, scale, bound, cuts=(), kind=jnp.bfloat16):
    array = scale * jax.random.normal(stream_key, shape, jnp.float32)
    if cuts:
        array = array * block_scale(stream_key, shape, cuts, -0.22, 0.18)
    return jnp.clip(array, -bound, bound).astype(kind)


def setup_inputs(seed: int = 0) -> dict:
    streams_of = jax.random.split(jax.random.key(seed), 5)
    queries = scatter_about(streams_of[0], (NQ, QTOK, DIM), 0.03, 0.1875, ((0, 32),))
    documents = scatter_about(streams_of[1], (NDOC, DTOK, DIM), 0.3, 1.75, ((0, 32),))
    lengths = touch_ends(jax.random.randint(streams_of[2], (NDOC,), 1, DTOK + 1), jax.random.fold_in(streams_of[2], 1), 1, DTOK).astype(jnp.int32)
    pattern = draw_pattern(jax.random.fold_in(streams_of[4], 71), 0)
    return {"queries": queries, "documents": documents, "lengths": lengths, "pattern": pattern}


def block_scores(query_block, doc_block, doc_lengths):
    qcount, tcount, width_dim = query_block.shape
    dcount, dtokens, _ = doc_block.shape
    group_size = min(16, dcount)
    doc_groups = doc_block.reshape(dcount // group_size, group_size * dtokens, width_dim)
    len_groups = doc_lengths.reshape(dcount // group_size, group_size)
    positions = jnp.arange(dtokens, dtype=jnp.int32)
    query_wide = query_block.astype(jnp.float32)

    def one_group(operands):
        doc_rows, limits = operands
        similar = jnp.einsum('qtc,gc->qtg', query_wide, doc_rows.astype(jnp.float32))
        is_valid = (positions[None, :] < limits[:, None]).reshape(group_size * dtokens)
        similar = jnp.where(is_valid[None, None, :], similar, -1e30)
        maxima = jnp.max(similar.reshape(qcount, tcount, group_size, dtokens), axis=3)
        return jnp.sum(maxima, axis=1)

    pieces = lax.map(one_group, (doc_groups, len_groups))
    return jnp.transpose(pieces, (1, 0, 2)).reshape(qcount, dcount)


def reference(queries, documents, lengths, pattern):
    query_blocks = queries.reshape(QBLK, BLOCK, QTOK, DIM)
    doc_blocks = documents.reshape(DBLK, BLOCK, DTOK, DIM)
    len_blocks = lengths.reshape(DBLK, BLOCK)

    def per_query(operands):
        query_block, flag_row = operands

        def per_doc(inner):
            doc_block, doc_lengths, flag = inner

            def active():
                return block_scores(query_block, doc_block, doc_lengths)

            def empty():
                return jnp.zeros((BLOCK, BLOCK), jnp.float32)

            return lax.cond(flag > 0, active, empty)

        return lax.map(per_doc, (doc_blocks, len_blocks, flag_row))

    result = lax.map(per_query, (query_blocks, pattern))
    return jnp.transpose(result, (0, 2, 1, 3)).reshape(NQ // QROW, QROW, NDOC)
```

```python
import functools

import jax
import jax.numpy as jnp
from jax import lax
from jax.experimental import pallas as pl
from jax.experimental.pallas import tpu as pltpu
from jax.sharding import PartitionSpec as P

BLOCK = 128
GROUP = 8
STEP = 8
CHUNK = 1024
META = 16


def query_kernel(q_ref, out_ref, rows_ref, turned_ref):
    count, tokens, _ = q_ref.shape
    rows_ref[...] = q_ref[...].reshape(rows_ref.shape).astype(jnp.float32)
    for t in range(tokens):
        turned_ref[t * count:(t + 1) * count, :] = rows_ref[pl.ds(t, count, stride=tokens), :]
    for j in range(count * tokens // 128):
        part = turned_ref[j * 128:(j + 1) * 128, :]
        out_ref[:, j * 128:(j + 1) * 128] = part.T.astype(out_ref.dtype)


def turn_queries(queries):
    count, tokens, width = queries.shape
    return pl.pallas_call(
        query_kernel,
        out_shape=jax.ShapeDtypeStruct((width, tokens * count), queries.dtype),
        in_specs=[pl.BlockSpec(memory_space=pltpu.VMEM)],
        out_specs=pl.BlockSpec(memory_space=pltpu.VMEM),
        scratch_shapes=[pltpu.VMEM((count * tokens, width), jnp.float32)] * 2,
        name="turn_queries",
    )(queries)


def document_kernel(order_ref, start_ref, docs_ref, length_ref, meta_ref, out_ref, rows_ref):
    ndoc, slots, _ = docs_ref.shape

    @pl.loop(0, ndoc // GROUP)
    def _(g):
        for i in range(GROUP):
            doc = order_ref[g * GROUP + i]
            rows_ref[i * slots:(i + 1) * slots, :] = docs_ref[doc].astype(jnp.float32)
        limit = length_ref[pl.ds(pl.multiple_of(g * GROUP, GROUP), GROUP), :]
        first = rows_ref[pl.ds(0, GROUP, stride=slots), :]
        base = start_ref[g] * (STEP * GROUP)
        for s in range(0, slots, 2):
            pair = []
            for k in (s, s + 1):
                tile = rows_ref[pl.ds(k, GROUP, stride=slots), :]
                pair.append(jnp.where(limit > k, tile, first))
            at = pl.multiple_of(base + s * GROUP, 2 * GROUP)
            out_ref[pl.ds(at, 2 * GROUP), :] = jnp.concatenate(pair, axis=0).astype(out_ref.dtype)

    out_ref[ndoc * slots:ndoc * slots + META, :] = meta_ref[...].astype(out_ref.dtype)


def pack_documents(documents, lengths):
    ndoc, slots, width = documents.shape
    groups = ndoc // GROUP
    ids = jnp.arange(ndoc, dtype=jnp.int32)
    mine, other = lengths[:, None], lengths[None, :]
    ahead = (other > mine) | ((other == mine) & (ids[None, :] < ids[:, None]))
    rank = jnp.sum(ahead.astype(jnp.int32), axis=1)
    place = (rank[None, :] == ids[:, None]).astype(jnp.int32)
    order = jnp.sum(place * ids[None, :], axis=1)
    by_length = jnp.sum(place * lengths[None, :], axis=1)
    steps = (by_length.reshape(groups, GROUP)[:, 0] + STEP - 1) // STEP
    gid = jnp.arange(groups, dtype=jnp.int32)
    starts = jnp.sum(jnp.where(gid[None, :] < gid[:, None], steps[None, :], 0), axis=1)
    per_chunk = CHUNK // (STEP * GROUP)
    chunks = (jnp.sum(steps) + per_chunk - 1) // per_chunk
    table = jnp.concatenate([steps, starts, chunks[None], jnp.zeros((128 - 2 * groups - 1,), jnp.int32)])
    meta = jnp.concatenate([rank[None], table[None], jnp.zeros((META - 2, 128), jnp.int32)])
    vmem = pl.BlockSpec(memory_space=pltpu.VMEM)
    smem = pl.BlockSpec(memory_space=pltpu.SMEM)
    return pl.pallas_call(
        document_kernel,
        out_shape=jax.ShapeDtypeStruct((ndoc * slots + META, width), documents.dtype),
        in_specs=[smem, smem, vmem, vmem, vmem],
        out_specs=vmem,
        scratch_shapes=[pltpu.VMEM((GROUP * slots, width), jnp.float32)],
        compiler_params=pltpu.CompilerParams(vmem_limit_bytes=16 << 20),
        name="pack_documents",
    )(order, starts, documents, by_length[:, None], meta.astype(jnp.float32))


def score_kernel(groups, info_ref, own_table, other_table, own_rank, other_rank, own_docs, other_docs,
                 near_ref, far_ref, own_out, other_out, q_ref, d_ref, max_ref, sum_ref, q_sem, d_sem, *, zmask):
    count = own_out.shape[1]
    width = q_ref.shape[2]
    core, chip = info_ref[0], info_ref[1]
    chunks_max = d_ref.shape[1] // CHUNK
    per_chunk = CHUNK // (STEP * GROUP)
    tile = min(256, width)
    tables = (own_table, other_table)
    docs = (own_docs, other_docs)

    def member(k, h):
        pos = jnp.where(core == 0, 2 * k + h, 2 * h + k)
        return pos, chip ^ (zmask * 4 + 2 * k + h)

    def flag(k, h, b):
        return info_ref[2 + 2 * member(k, h)[1] + b]

    wanted = [flag(0, 0, b) + flag(0, 1, b) + flag(1, 0, b) + flag(1, 1, b) for b in range(2)]

    def doc_copy(b, c):
        rows = pl.ds(pl.multiple_of(c * CHUNK, CHUNK), CHUNK)
        return pltpu.make_async_copy(docs[b].at[rows, :], d_ref.at[b, rows, :], d_sem.at[b, c])

    def query_copy(a, h):
        slot = jnp.where(core == 0, 2 * a + h, 2 * h + a)
        return pltpu.make_async_copy((near_ref, far_ref)[a].at[h], q_ref.at[slot], q_sem.at[a, h])

    needed = wanted[0] + wanted[1] > 0

    @pl.when(needed)
    def _():
        for a in range(2):
            for h in range(2):
                query_copy(a, h).start()

    for b in range(2):
        @pl.when(wanted[b] > 0)
        def _(b=b):
            @pl.loop(0, tables[b][2 * groups])
            def _(c):
                doc_copy(b, c).start()

    @pl.when(needed)
    def _():
        for a in range(2):
            for h in range(2):
                query_copy(a, h).wait()

    for b in range(2):
        table = tables[b]
        out = (own_out, other_out)[b]
        rank = (own_rank, other_rank)[b]

        @pl.when(wanted[b] > 0)
        def _(b=b, table=table):
            @pl.loop(0, table[2 * groups])
            def _(c):
                doc_copy(b, c).wait()

        @pl.loop(0, 2)
        def _(k, b=b, table=table, out=out, rank=rank):
            live = [flag(k, h, b) for h in range(2)]
            place = [member(k, h)[0] for h in range(2)]

            @pl.when(live[0] + live[1] > 0)
            def _():
                @pl.loop(0, table[2 * groups])
                def _(c):
                    rows = d_ref[b, pl.ds(pl.multiple_of(c * CHUNK, CHUNK), CHUNK), :]
                    for h in range(2):
                        for j in range(width // tile):
                            at = h * width + j * tile
                            similar = jnp.dot(rows, q_ref[2 * k + h, :, j * tile:(j + 1) * tile],
                                              preferred_element_type=jnp.float32)
                            similar = jnp.max(similar.reshape(per_chunk, STEP, GROUP, tile), axis=1)
                            max_ref[pl.ds(c * per_chunk, per_chunk), :, at:at + tile] = similar

                @pl.loop(0, groups)
                def _(g):
                    steps, start = table[g], table[groups + g]
                    index = [start + jnp.minimum(i, steps - 1) for i in range(max_ref.shape[0] // groups)]
                    for h in range(2):
                        total = None
                        for j in range(width // 128):
                            at = h * width + j * 128
                            best = max_ref[index[0], :, at:at + 128]
                            for i in index[1:]:
                                best = jnp.maximum(best, max_ref[i, :, at:at + 128])
                            total = best if total is None else total + best
                        sum_ref[h, pl.ds(pl.multiple_of(g * GROUP, GROUP), GROUP), :] = total

                ndoc = rank.shape[1]
                ids = lax.broadcasted_iota(jnp.int32, (ndoc, ndoc), 0).astype(jnp.float32)
                chosen = jnp.where(ids == rank[...], 1.0, 0.0)
                for h in range(2):
                    spread = jnp.dot(sum_ref[h].T, chosen, precision=lax.Precision.HIGHEST,
                                     preferred_element_type=jnp.float32)
                    score = spread[:count]
                    for j in range(1, 128 // count):
                        score = score + spread[j * count:(j + 1) * count]
                    out[place[h]] = jnp.where(live[h] > 0, score, 0.0)

            @pl.when(live[0] + live[1] == 0)
            def _():
                for h in range(2):
                    out[place[h]] = jnp.zeros(out.shape[1:], jnp.float32)


def score_plane(info, packs, near, far, zmask, count):
    width_dim, width = near.shape[1:]
    rows = packs[0][0].shape[0] - META
    ndoc = packs[0][2].shape[1]
    slots = rows // ndoc
    groups = ndoc // GROUP
    most = slots // STEP
    vmem = pl.BlockSpec(memory_space=pltpu.VMEM)
    smem = pl.BlockSpec(memory_space=pltpu.SMEM)
    anywhere = pl.BlockSpec(memory_space=pl.ANY)
    shape = jax.ShapeDtypeStruct((4, count, ndoc), jnp.float32)
    return pl.pallas_call(
        functools.partial(score_kernel, groups, zmask=zmask),
        out_shape=(shape, shape),
        in_specs=[smem, smem, smem, vmem, vmem, anywhere, anywhere, anywhere, anywhere],
        out_specs=(vmem, vmem),
        scratch_shapes=[
            pltpu.VMEM((4, width_dim, width), near.dtype),
            pltpu.VMEM((2, rows, width_dim), near.dtype),
            pltpu.VMEM((groups * most, GROUP, 2 * width), jnp.float32),
            pltpu.VMEM((2, ndoc, 128), jnp.float32),
            pltpu.SemaphoreType.DMA((2, 2)),
            pltpu.SemaphoreType.DMA((2, rows // CHUNK)),
        ],
        compiler_params=pltpu.CompilerParams(vmem_limit_bytes=24 << 20),
        cost_estimate=pl.CostEstimate(flops=4 << 30, bytes_accessed=4 << 20, transcendentals=0),
        name="score_plane",
    )(info, packs[0][1], packs[1][1], packs[0][2], packs[1][2], packs[0][0], packs[1][0], near, far)


def place_kernel(info_ref, *refs, zmasks):
    owns, got_ref, out_ref = refs[:-2], refs[-2], refs[-1]
    core, chip = info_ref[0], info_ref[1]
    for p, zmask in enumerate(zmasks):
        for i in range(4):
            swapped = 2 * (i % 2) + i // 2
            mine = chip ^ (zmask * 4 + jnp.where(core == 0, i, swapped))
            theirs = chip ^ (zmask * 4 + jnp.where(core == 0, swapped, i))
            out_ref[2 * mine + core] = owns[p][i]
            out_ref[2 * theirs + 1 - core] = got_ref[4 * p + i]


def place_scores(info, owns, got, zmasks):
    count, ndoc = got.shape[1:]
    vmem = pl.BlockSpec(memory_space=pltpu.VMEM)
    return pl.pallas_call(
        functools.partial(place_kernel, zmasks=zmasks),
        out_shape=jax.ShapeDtypeStruct((2 * got.shape[0], count, ndoc), jnp.float32),
        in_specs=[pl.BlockSpec(memory_space=pltpu.SMEM)] + [vmem] * (len(owns) + 1),
        out_specs=vmem,
        name="place_scores",
    )(info, *owns, got)


def routes(devices):
    def masks(even, odd):
        return [(i, ((i // 2) ^ (odd if i % 2 else even)) * 2 + i % 2) for i in range(devices)]
    return masks


def local(queries, documents, lengths, pattern):
    devices = lax.axis_size("docs")
    halves = lax.axis_size("pb")
    planes = devices // 8
    me = lax.axis_index("docs")
    core, chip = me % 2, me // 2
    shard_rows = queries.shape[0]
    masks = routes(devices)
    swap = [(i, i ^ 1) for i in range(devices)]

    if halves > 1:
        queries = lax.all_to_all(queries, "pb", split_axis=0, concat_axis=1, tiled=True)
    count = queries.shape[0]
    unit = turn_queries(queries)[None]

    def send(array, pairs):
        return lax.ppermute(array, "docs", pairs)

    def join(a, b):
        return jnp.concatenate([a, b], axis=0)

    first, second = masks(1, 2), masks(2, 1)
    near, far = {}, {}
    crossed = {e: send(unit, masks(4 * e, 4 * e)) for e in range(2, planes, 2)}
    near[0] = join(unit, send(unit, first))
    for e in range(2, planes, 2):
        near[e] = join(crossed[e], send(crossed[e], first))
    for e in range(0, planes, 2):
        if e + 1 < planes:
            near[e + 1] = send(near[e], masks(4, 4))
    for z in near:
        far[z] = send(near[z], second)

    packed = pack_documents(documents, lengths)
    rows = packed.shape[0] - META
    packs = []
    for pack in (packed, send(packed, swap)):
        meta = pack[rows:].astype(jnp.float32)
        packs.append((pack, meta[1].astype(jnp.int32), meta[:1]))

    chips = jnp.arange(devices // 2, dtype=jnp.int32)
    row_block = ((2 * chips + core) * shard_rows + lax.axis_index("pb") * count) // BLOCK
    own = jnp.take(pattern, jnp.stack([me, me ^ 1]), axis=1)
    hot = (row_block[:, None] == jnp.arange(pattern.shape[0], dtype=jnp.int32)[None]).astype(jnp.int32)
    flags = jnp.sum(hot[:, :, None] * own[None], axis=1)
    info = jnp.concatenate([jnp.stack([core, chip]), flags.reshape(-1)])

    order = [z for e in range(0, planes, 2) for z in (e, e + 1) if z < planes]
    owns, others = [], []
    for z in order:
        mine, theirs = score_plane(info, packs, near[z], far[z], z, count)
        owns.append(mine)
        others.append(theirs)
    got = send(jnp.concatenate(others, axis=0), swap)
    return place_scores(info, owns, got, tuple(order))


def solution(mesh):
    return jax.shard_map(
        local,
        mesh=mesh,
        in_specs=(P("docs", "pb", None), P("docs", None, None), P("docs"), P()),
        out_specs=P(None, "pb", "docs"),
        check_vma=False,
    )
```

```python
import functools

import jax
import jax.numpy as jnp
from jax import lax
from jax.experimental import pallas as pl
from jax.experimental.pallas import tpu as pltpu
from jax.sharding import PartitionSpec as P

BLOCK = 128
GROUP = 8
STEP = 8
SUB = GROUP * STEP
RING = 8
LAG = 7
META = 16
LOWEST = -3e38
VMEM = pl.BlockSpec(memory_space=pltpu.VMEM)
SMEM = pl.BlockSpec(memory_space=pltpu.SMEM)
ANY = pl.BlockSpec(memory_space=pl.ANY)


def query_kernel(q_ref, out_ref, rows_ref, turned_ref):
    count, tokens, _ = q_ref.shape
    rows_ref[...] = q_ref[...].reshape(rows_ref.shape).astype(jnp.float32)
    for t in range(tokens):
        turned_ref[t * count:(t + 1) * count, :] = rows_ref[pl.ds(t, count, stride=tokens), :]
    for j in range(count * tokens // 128):
        part = turned_ref[j * 128:(j + 1) * 128, :]
        out_ref[0, :, j * 128:(j + 1) * 128] = part.T.astype(out_ref.dtype)


def turn_queries(queries):
    count, tokens, width = queries.shape
    return pl.pallas_call(
        query_kernel,
        out_shape=jax.ShapeDtypeStruct((1, width, tokens * count), queries.dtype),
        in_specs=[VMEM],
        out_specs=VMEM,
        scratch_shapes=[pltpu.VMEM((count * tokens, width), jnp.float32)] * 2,
        name="turn_queries",
    )(queries)


def document_kernel(docs_ref, length_ref, out_ref, rows_ref, limit_ref, row_ref, table_ref, sem):
    ndoc, slots, _ = docs_ref.shape
    square = (ndoc, ndoc)
    down = lax.broadcasted_iota(jnp.int32, square, 0)
    across = lax.broadcasted_iota(jnp.int32, square, 1)
    down_f, across_f = down.astype(jnp.float32), across.astype(jnp.float32)
    len_across = jnp.broadcast_to(length_ref[...].astype(jnp.float32), square)
    len_down = len_across.T

    def count(hits, axis):
        return jnp.sum(jnp.where(hits, 1.0, 0.0), axis=axis, keepdims=True)

    ahead = (len_across > len_down) | ((len_across == len_down) & (across < down))
    behind = (len_down > len_across) | ((len_down == len_across) & (down < across))
    rank_down = count(ahead, 1)
    rank_across = count(behind, 0)
    limit_ref[...] = jnp.sum(jnp.where(rank_across == down_f, len_across, 0.0), axis=1, keepdims=True)
    taken = rank_down == across_f
    order = jnp.sum(jnp.where(taken, down_f, 0.0), axis=0, keepdims=True)
    limit_across = jnp.sum(jnp.where(taken, len_down, 0.0), axis=0, keepdims=True)

    def steps_of(limit):
        return ((limit.astype(jnp.int32) + (STEP - 1)) // STEP).astype(jnp.float32)

    steps_down = jnp.broadcast_to(steps_of(limit_ref[...]), square)
    steps_across = jnp.broadcast_to(steps_of(limit_across), square)
    head_down, head_across = down % GROUP == 0, across % GROUP == 0
    starts = jnp.sum(jnp.where(head_down & (down < across * GROUP), steps_down, 0.0), axis=0, keepdims=True)
    ends = jnp.sum(jnp.where(head_across & (across <= down), steps_across, 0.0), axis=1, keepdims=True)
    group = count(head_down & (ends <= across_f), 0)
    total = jnp.sum(jnp.where(head_down, steps_down, 0.0), axis=0, keepdims=True).astype(jnp.int32)
    rounds = ((total + (RING - 1)) // RING).astype(jnp.float32)

    row_ref[0:1, :] = order.astype(jnp.int32)
    row_ref[1:2, :] = starts.astype(jnp.int32)
    to_scalars = pltpu.make_async_copy(row_ref, table_ref, sem)
    to_scalars.start()
    meta = jnp.concatenate([rank_across, group, rounds, jnp.zeros((META - 3, ndoc), jnp.float32)], axis=0)
    out_ref[ndoc * slots:ndoc * slots + META, :] = meta.astype(out_ref.dtype)
    to_scalars.wait()

    @pl.loop(0, ndoc // GROUP)
    def _(g):
        for i in range(GROUP):
            doc = table_ref[0, g * GROUP + i]
            rows_ref[i * slots:(i + 1) * slots, :] = docs_ref[doc].astype(jnp.float32)
        limit = limit_ref[pl.ds(pl.multiple_of(g * GROUP, GROUP), GROUP), :].astype(jnp.int32)
        first = rows_ref[pl.ds(0, GROUP, stride=slots), :]
        base = table_ref[1, g] * SUB
        for s in range(0, slots, 2):
            pair = []
            for k in (s, s + 1):
                tile = rows_ref[pl.ds(k, GROUP, stride=slots), :]
                pair.append(jnp.where(limit > k, tile, first))
            at = pl.multiple_of(base + s * GROUP, 2 * GROUP)
            out_ref[pl.ds(at, 2 * GROUP), :] = jnp.concatenate(pair, axis=0).astype(out_ref.dtype)


def pack_documents(documents, lengths):
    ndoc, slots, width = documents.shape
    return pl.pallas_call(
        document_kernel,
        out_shape=jax.ShapeDtypeStruct((ndoc * slots + META, width), documents.dtype),
        in_specs=[VMEM, VMEM],
        out_specs=VMEM,
        scratch_shapes=[
            pltpu.VMEM((GROUP * slots, width), jnp.float32),
            pltpu.VMEM((ndoc, 1), jnp.float32),
            pltpu.VMEM((8, ndoc), jnp.int32),
            pltpu.SMEM((8, ndoc), jnp.int32),
            pltpu.SemaphoreType.DMA,
        ],
        compiler_params=pltpu.CompilerParams(vmem_limit_bytes=16 << 20),
        cost_estimate=pl.CostEstimate(flops=1 << 20, bytes_accessed=12 << 20, transcendentals=0),
        name="pack_documents",
    )(documents, lengths.reshape(1, ndoc))


def fold(max_ref, step_group, at, best):
    span = slice(at, at + best.shape[1])
    max_ref[step_group, :, span] = jnp.maximum(max_ref[step_group, :, span], best)


def streamed_maxima(rounds, table, d_ref, b, q_ref, u, max_ref, accs):
    width = q_ref.shape[2]
    none_q = jnp.zeros((q_ref.shape[1], 256), q_ref.dtype)
    none_d = jnp.zeros((SUB, q_ref.shape[1]), q_ref.dtype)

    def feed(step, slot, staged):
        rows = d_ref[b, pl.ds(pl.multiple_of(step * SUB, SUB), SUB), :]
        rows = jnp.concatenate([rows, none_d], axis=1)
        for unit in range(2):
            pltpu.matmul_acc_lhs(accs[unit][slot], rows, load_staged_rhs=staged)

    def retire(step, slot, pair):
        group = table[step]
        for unit in range(2):
            got = pltpu.matmul_pop(accs[unit][slot])
            best = jnp.max(got.reshape(STEP, GROUP, 256), axis=0)
            fold(max_ref, group, (2 * pair + unit) * 256, best)

    for pair in range(width // 512):
        for unit in range(2):
            at = (2 * pair + unit) * 256
            pltpu.matmul_push_rhs(jnp.concatenate([q_ref[u, :, at:at + 256], none_q], axis=0), pair % 2, unit)
        for slot in range(RING):
            feed(slot, slot, pair % 2 if slot == 0 else None)
            if slot >= LAG:
                retire(slot - LAG, slot - LAG, pair)

        @pl.loop(1, rounds)
        def _(r, pair=pair):
            for slot in range(RING):
                step = r * RING + slot
                feed(step, slot, None)
                retire(step - LAG, (slot - LAG) % RING, pair)

        for k in range(RING - LAG, RING):
            retire((rounds - 1) * RING + k, k, pair)


def plain_maxima(rounds, table, d_ref, b, q_ref, u, max_ref):
    @pl.loop(0, rounds * RING)
    def _(step):
        rows = d_ref[b, pl.ds(pl.multiple_of(step * SUB, SUB), SUB), :]
        similar = jnp.dot(rows, q_ref[u], preferred_element_type=jnp.float32)
        fold(max_ref, table[step], 0, jnp.max(similar.reshape(STEP, GROUP, similar.shape[1]), axis=0))


def score_kernel(info_ref, own_table, other_table, own_rank, other_rank, own_docs, other_docs, *refs, masks):
    arrays = len(masks) // 2
    units = len(masks)
    sent, (own_out, other_out, q_ref, d_ref, max_ref, sort_ref, mask_ref, q_sem, d_sem) = refs[:arrays], refs[arrays:]
    count, ndoc = own_out.shape[1:]
    width = q_ref.shape[2]
    groups = ndoc // GROUP
    core, chip = info_ref[0], info_ref[1]
    tables = (own_table, other_table)
    docs = (own_docs, other_docs)
    rows = RING * SUB

    for u, (even, odd) in enumerate(masks):
        mask_ref[u] = jnp.where(core == 0, even, odd)

    def flag(u, b):
        return info_ref[2 + 2 * (chip ^ mask_ref[u]) + b]

    wanted = [sum(flag(u, b) for u in range(units)) for b in range(2)]
    needed = wanted[0] + wanted[1] > 0

    def doc_copy(b, r):
        span = pl.ds(pl.multiple_of(r * rows, rows), rows)
        return pltpu.make_async_copy(docs[b].at[span, :], d_ref.at[b, span, :], d_sem.at[b, r])

    def query_copy(a):
        return pltpu.make_async_copy(sent[a], q_ref.at[pl.ds(2 * a, 2)], q_sem.at[a])

    @pl.when(needed)
    def _():
        for a in range(arrays):
            query_copy(a).start()

    for b in range(2):
        @pl.when(wanted[b] > 0)
        def _(b=b):
            @pl.loop(0, tables[b][ndoc])
            def _(r):
                doc_copy(b, r).start()

            ids = lax.broadcasted_iota(jnp.int32, (ndoc, ndoc), 0).astype(jnp.float32)
            place = jnp.where(ids == (own_rank, other_rank)[b][...], 1.0, 0.0).astype(sort_ref.dtype)
            sort_ref[b] = jnp.concatenate([jnp.concatenate([place, place], axis=0)] * 2, axis=1)

    @pl.when(needed)
    def _():
        for a in range(arrays):
            query_copy(a).wait()

    def scores(b, u, out, *flat):
        table = tables[b]
        rounds = table[ndoc]
        max_ref[...] = jnp.full(max_ref.shape, LOWEST, jnp.float32)
        if flat:
            streamed_maxima(rounds, table, d_ref, b, q_ref, u, max_ref, (flat[:RING], flat[RING:2 * RING]))
        else:
            plain_maxima(rounds, table, d_ref, b, q_ref, u, max_ref)
        sums = []
        for g in range(groups):
            total = max_ref[g, :, :128]
            for j in range(1, width // 128):
                total = total + max_ref[g, :, j * 128:(j + 1) * 128]
            sums.append(total)
        turned = jnp.concatenate(sums, axis=0).T
        high = turned.astype(sort_ref.dtype)
        low = (turned - high.astype(jnp.float32)).astype(sort_ref.dtype)
        halves = jnp.concatenate([high, low], axis=1)
        if flat:
            pltpu.matmul_push_rhs(sort_ref[b], 0, 0)
            pltpu.matmul_acc_lhs(flat[-1], halves, load_staged_rhs=0)
            spread = pltpu.matmul_pop(flat[-1])[:, :ndoc]
        else:
            spread = jnp.dot(halves, sort_ref[b], preferred_element_type=jnp.float32)[:, :ndoc]
        score = spread[:count]
        for j in range(1, 128 // count):
            score = score + spread[j * count:(j + 1) * count]
        out[u] = score

    for b in range(2):
        out = (own_out, other_out)[b]

        @pl.when(wanted[b] > 0)
        def _(b=b):
            @pl.loop(0, tables[b][ndoc])
            def _(r):
                doc_copy(b, r).wait()

        @pl.loop(0, units)
        def _(u, b=b, out=out):
            @pl.when(flag(u, b) > 0)
            def _():
                if width % 512 == 0:
                    pl.run_scoped(
                        functools.partial(scores, b, u, out),
                        *[pltpu.ACC(mxu_id=x)((SUB, 256), jnp.float32) for x in range(2) for _ in range(RING)],
                        pltpu.ACC(mxu_id=0)((128, 256), jnp.float32),
                    )
                else:
                    scores(b, u, out)

            @pl.when(flag(u, b) == 0)
            def _():
                out[u] = jnp.zeros(out.shape[1:], jnp.float32)


def score_units(info, packs, sent, masks, count):
    width_dim, width = sent[0].shape[1:]
    ndoc = packs[0][2].shape[1]
    rows = packs[0][0].shape[0] - META
    units = len(masks)
    shape = jax.ShapeDtypeStruct((units, count, ndoc), jnp.float32)
    return pl.pallas_call(
        functools.partial(score_kernel, masks=masks),
        out_shape=(shape, shape),
        in_specs=[SMEM, SMEM, SMEM, VMEM, VMEM, ANY, ANY] + [ANY] * len(sent),
        out_specs=(VMEM, VMEM),
        scratch_shapes=[
            pltpu.VMEM((units, width_dim, width), sent[0].dtype),
            pltpu.VMEM((2, rows, width_dim), sent[0].dtype),
            pltpu.VMEM((ndoc // GROUP + 1, GROUP, width), jnp.float32),
            pltpu.VMEM((2, 2 * ndoc, 2 * ndoc), sent[0].dtype),
            pltpu.SMEM((units,), jnp.int32),
            pltpu.SemaphoreType.DMA((len(sent),)),
            pltpu.SemaphoreType.DMA((2, rows // (RING * SUB))),
        ],
        compiler_params=pltpu.CompilerParams(vmem_limit_bytes=16 << 20),
        cost_estimate=pl.CostEstimate(flops=4 << 30, bytes_accessed=4 << 20, transcendentals=0),
        name="score_units",
    )(info, packs[0][1], packs[1][1], packs[0][2], packs[1][2], packs[0][0], packs[1][0], *sent)


def place_kernel(info_ref, *refs, masks):
    out_ref = refs[-1]
    core, chip = info_ref[0], info_ref[1]
    owns, gots = refs[:len(masks)], refs[len(masks):-1]
    for part, own_ref, got_ref in zip(masks, owns, gots):
        for u, (even, odd) in enumerate(part):
            mine = chip ^ jnp.where(core == 0, even, odd)
            theirs = chip ^ jnp.where(core == 0, odd, even)
            out_ref[2 * mine + core] = own_ref[u]
            out_ref[2 * theirs + 1 - core] = got_ref[u]


def place_scores(info, owns, gots, masks, devices):
    count, ndoc = gots[0].shape[1:]
    return pl.pallas_call(
        functools.partial(place_kernel, masks=masks),
        out_shape=jax.ShapeDtypeStruct((devices, count, ndoc), jnp.float32),
        in_specs=[SMEM] + [VMEM] * (len(owns) + len(gots)),
        out_specs=VMEM,
        name="place_scores",
    )(info, *owns, *gots)


def xor_pairs(devices, even, odd):
    return [(i, ((i // 2) ^ (odd if i % 2 else even)) * 2 + i % 2) for i in range(devices)]


def after(array, *others):
    return lax.optimization_barrier((array, *others))[0]


def local(queries, documents, lengths, pattern):
    devices = lax.axis_size("docs")
    halves = lax.axis_size("pb")
    planes = devices // 8
    me = lax.axis_index("docs")
    core, chip = me % 2, me // 2
    shard_rows = queries.shape[0]
    swap = [(i, i ^ 1) for i in range(devices)]

    if halves > 1:
        queries = lax.all_to_all(queries, "pb", split_axis=0, concat_axis=1, tiled=True)
    count = queries.shape[0]

    def send(array, even, odd=None):
        return lax.ppermute(array, "docs", xor_pairs(devices, even, even if odd is None else odd))

    def join(a, b):
        return jnp.concatenate([a, b], axis=0)

    unit = turn_queries(queries)
    beside = send(unit, 1, 2)
    crossed = {e: send(unit, 4 * e) for e in range(2, planes, 2)}

    packed = pack_documents(after(documents, unit), lengths)
    rows = packed.shape[0] - META
    packs = []
    for pack in (packed, lax.ppermute(packed, "docs", swap)):
        meta = pack[rows:].astype(jnp.float32)
        table = jnp.concatenate([meta[1], meta[2]]).astype(jnp.int32)
        packs.append((pack, table, meta[:1]))

    chips = jnp.arange(devices // 2, dtype=jnp.int32)
    row_block = ((2 * chips + core) * shard_rows + lax.axis_index("pb") * count) // BLOCK
    both = jnp.stack([me, me ^ 1])
    hot = (row_block[:, None] == jnp.arange(pattern.shape[0], dtype=jnp.int32)[None]).astype(jnp.int32)
    mine = (both[:, None] == jnp.arange(pattern.shape[1], dtype=jnp.int32)[None]).astype(jnp.int32)
    columns = jnp.sum(pattern[:, None, :] * mine[None], axis=2)
    flags = jnp.sum(hot[:, :, None] * columns[None], axis=1)
    info = jnp.concatenate([jnp.stack([core, chip]), flags.reshape(-1)])

    owns, others, placed = [], [], []

    def score(*parts):
        masks = []
        for _, z, past in parts:
            for i in range(2):
                masks.append((4 * z + 2 * past + i, 4 * z + past + 2 * i))
        own, other = score_units(info, packs, [p[0] for p in parts], tuple(masks), count)
        owns.append(own)
        others.append(other)
        placed.append(tuple(masks))
        return other

    near = join(unit, beside)
    done = None
    for e in range(0, planes, 2):
        if e:
            here = after(crossed[e], done)
            near = join(here, send(here, 1, 2))
            near = after(near, done)
        pair = send(near, 4) if e + 1 < planes else None
        far = send(near, 2, 1)
        done = score((near, e, 0))
        if pair is None:
            done = score((after(far, done), e, 1))
        else:
            pair = after(pair, done)
            pair_far = send(pair, 2, 1)
            done = score((after(far, done), e, 1), (pair, e + 1, 0))
            done = score((after(pair_far, done), e + 1, 1))

    gots = [lax.ppermute(o, "docs", swap) for o in others]
    return place_scores(info, owns, gots, tuple(placed), devices)


def solution(mesh):
    mapped = jax.shard_map(
        local,
        mesh=mesh,
        in_specs=(P("docs", "pb", None), P("docs", None, None), P("docs"), P()),
        out_specs=P(None, "pb", "docs"),
        check_vma=False,
    )

    def run(*arrays):
        with jax.sharding.use_abstract_mesh(mesh.abstract_mesh):
            return mapped(*arrays)

    return run
```

```python
import functools

import jax
import jax.numpy as jnp
from jax import lax
from jax.experimental import pallas as pl
from jax.experimental.pallas import tpu as pltpu
from jax.sharding import PartitionSpec as P

BLOCK = 128
GROUP = 8
STEP = 8
SUB = GROUP * STEP
RING = 8
LAG = 7
PAD = 8
SIDE = 4
LOWEST = -3e38
VMEM = pl.BlockSpec(memory_space=pltpu.VMEM)
SMEM = pl.BlockSpec(memory_space=pltpu.SMEM)
ANY = pl.BlockSpec(memory_space=pl.ANY)


def query_kernel(q_ref, out_ref, rows_ref):
    count, tokens, _ = q_ref.shape
    pitch = rows_ref.shape[0] // count
    for i in range(count):
        rows_ref[i * pitch:i * pitch + tokens, :] = q_ref[i].astype(jnp.float32)
    span = 128 // count
    for j in range(tokens // span):
        parts = [rows_ref[pl.ds(j * span + t, count, stride=pitch), :] for t in range(span)]
        out_ref[0, :, j * 128:(j + 1) * 128] = jnp.concatenate(parts, axis=0).T.astype(out_ref.dtype)


def turn_queries(queries):
    count, tokens, width = queries.shape
    return pl.pallas_call(
        query_kernel,
        out_shape=jax.ShapeDtypeStruct((1, width, tokens * count), queries.dtype),
        in_specs=[VMEM],
        out_specs=VMEM,
        scratch_shapes=[pltpu.VMEM((count * (tokens + PAD), width), jnp.float32)],
        name="turn_queries",
    )(queries)


def document_kernel(docs_ref, length_ref, out_ref, place_ref, steps_ref, rows_ref, limit_ref, row_ref, table_ref, sem):
    ndoc, slots, _ = docs_ref.shape
    pitch = rows_ref.shape[1] // GROUP
    square = (ndoc, ndoc)
    down = lax.broadcasted_iota(jnp.int32, square, 0)
    across = lax.broadcasted_iota(jnp.int32, square, 1)
    down_f, across_f = down.astype(jnp.float32), across.astype(jnp.float32)
    len_across = jnp.broadcast_to(length_ref[...].astype(jnp.float32), square)
    len_down = len_across.T

    def count(hits, axis):
        return jnp.sum(jnp.where(hits, 1.0, 0.0), axis=axis, keepdims=True)

    ahead = (len_across > len_down) | ((len_across == len_down) & (across < down))
    behind = (len_down > len_across) | ((len_down == len_across) & (down < across))
    rank_down = count(ahead, 1)
    rank_across = count(behind, 0)
    limit_ref[...] = jnp.sum(jnp.where(rank_across == down_f, len_across, 0.0), axis=1, keepdims=True)
    taken = rank_down == across_f
    order = jnp.sum(jnp.where(taken, down_f, 0.0), axis=0, keepdims=True)
    limit_across = jnp.sum(jnp.where(taken, len_down, 0.0), axis=0, keepdims=True)

    def steps_of(limit):
        return ((limit.astype(jnp.int32) + (STEP - 1)) // STEP).astype(jnp.float32)

    steps_down = jnp.broadcast_to(steps_of(limit_ref[...]), square)
    steps_across = jnp.broadcast_to(steps_of(limit_across), square)
    head_down, head_across = down % GROUP == 0, across % GROUP == 0
    starts = jnp.sum(jnp.where(head_down & (down < across * GROUP), steps_down, 0.0), axis=0, keepdims=True)
    ends = jnp.sum(jnp.where(head_across & (across <= down), steps_across, 0.0), axis=1, keepdims=True)
    group = count(head_down & (ends <= across_f), 0)
    total = jnp.sum(jnp.where(head_down, steps_down, 0.0), axis=0, keepdims=True).astype(jnp.int32)
    rounds = ((total + (RING - 1)) // RING).astype(jnp.float32)

    row_ref[0:1, :] = order.astype(jnp.int32)
    row_ref[1:2, :] = starts.astype(jnp.int32)
    to_scalars = pltpu.make_async_copy(row_ref, table_ref, sem)
    to_scalars.start()
    steps_ref[0:1, :] = group.astype(jnp.int32)
    steps_ref[1:2, :] = rounds.astype(jnp.int32)
    place = jnp.where(rank_across == down_f, 1.0, 0.0).astype(place_ref.dtype)
    place_ref[...] = jnp.concatenate([jnp.concatenate([place, place], axis=0)] * 2, axis=1)
    to_scalars.wait()

    @pl.loop(0, ndoc // GROUP // SIDE)
    def _(turn):
        for side in range(SIDE):
            g = turn * SIDE + side
            for i in range(GROUP):
                doc = table_ref[0, g * GROUP + i]
                rows_ref[side, i * pitch:i * pitch + slots, :] = docs_ref[doc].astype(jnp.float32)
        for side in range(SIDE):
            g = turn * SIDE + side
            limit = limit_ref[pl.ds(pl.multiple_of(g * GROUP, GROUP), GROUP), :].astype(jnp.int32)
            first = rows_ref[side, pl.ds(0, GROUP, stride=pitch), :]
            base = table_ref[1, g] * SUB
            for s in range(0, slots, 2):
                pair = []
                for k in (s, s + 1):
                    tile = rows_ref[side, pl.ds(k, GROUP, stride=pitch), :]
                    pair.append(jnp.where(limit > k, tile, first))
                at = pl.multiple_of(base + s * GROUP, 2 * GROUP)
                out_ref[pl.ds(at, 2 * GROUP), :] = jnp.concatenate(pair, axis=0).astype(out_ref.dtype)


def pack_documents(documents, lengths):
    ndoc, slots, width = documents.shape
    return pl.pallas_call(
        document_kernel,
        out_shape=(
            jax.ShapeDtypeStruct((ndoc * slots, width), documents.dtype),
            jax.ShapeDtypeStruct((2 * ndoc, 2 * ndoc), documents.dtype),
            jax.ShapeDtypeStruct((2, ndoc), jnp.int32),
        ),
        in_specs=[VMEM, VMEM],
        out_specs=(VMEM, VMEM, VMEM),
        scratch_shapes=[
            pltpu.VMEM((SIDE, GROUP * (slots + PAD), width), jnp.float32),
            pltpu.VMEM((ndoc, 1), jnp.float32),
            pltpu.VMEM((8, ndoc), jnp.int32),
            pltpu.SMEM((8, ndoc), jnp.int32),
            pltpu.SemaphoreType.DMA,
        ],
        compiler_params=pltpu.CompilerParams(vmem_limit_bytes=16 << 20),
        cost_estimate=pl.CostEstimate(flops=0, bytes_accessed=0, transcendentals=0),
        name="pack_documents",
    )(documents, lengths.reshape(1, ndoc))


def fold(max_ref, step_group, at, best):
    span = slice(at, at + best.shape[1])
    max_ref[step_group, :, span] = jnp.maximum(max_ref[step_group, :, span], best)


def streamed_maxima(rounds, table, b, docs_ref, q_ref, u, max_ref, accs):
    width = q_ref.shape[2]
    none_q = jnp.zeros((q_ref.shape[1], 256), q_ref.dtype)
    none_d = jnp.zeros((SUB, q_ref.shape[1]), q_ref.dtype)

    def feed(step, slot, staged):
        rows = docs_ref[pl.ds(pl.multiple_of(step * SUB, SUB), SUB), :]
        rows = jnp.concatenate([rows, none_d], axis=1)
        for unit in range(2):
            pltpu.matmul_acc_lhs(accs[unit][slot], rows, load_staged_rhs=staged)

    def retire(step, slot, pair):
        group = table[b, step]
        for unit in range(2):
            got = pltpu.matmul_pop(accs[unit][slot])
            best = jnp.max(got.reshape(STEP, GROUP, 256), axis=0)
            fold(max_ref, group, (2 * pair + unit) * 256, best)

    for pair in range(width // 512):
        for unit in range(2):
            at = (2 * pair + unit) * 256
            pltpu.matmul_push_rhs(jnp.concatenate([q_ref[u, :, at:at + 256], none_q], axis=0), pair % 2, unit)
        for slot in range(RING):
            feed(slot, slot, pair % 2 if slot == 0 else None)
            if slot >= LAG:
                retire(slot - LAG, slot - LAG, pair)

        @pl.loop(1, rounds)
        def _(r, pair=pair):
            for slot in range(RING):
                step = r * RING + slot
                feed(step, slot, None)
                retire(step - LAG, (slot - LAG) % RING, pair)

        for k in range(RING - LAG, RING):
            retire((rounds - 1) * RING + k, k, pair)


def plain_maxima(rounds, table, b, docs_ref, q_ref, u, max_ref):
    @pl.loop(0, rounds * RING)
    def _(step):
        rows = docs_ref[pl.ds(pl.multiple_of(step * SUB, SUB), SUB), :]
        similar = jnp.dot(rows, q_ref[u], preferred_element_type=jnp.float32)
        fold(max_ref, table[b, step], 0, jnp.max(similar.reshape(STEP, GROUP, similar.shape[1]), axis=0))


def score_kernel(info_ref, own_docs, other_docs, own_place, other_place, *refs, masks):
    arrays = len(masks) // 2
    sent, (own_out, other_out, max_ref) = refs[:arrays], refs[arrays:]
    count, ndoc = own_out.shape[1:]
    width = sent[0].shape[2]
    groups = ndoc // GROUP
    core, chip = info_ref[3, 0], info_ref[3, 1]

    def flag(a, i, b):
        (even0, odd0), (even1, odd1) = masks[2 * a:2 * a + 2]
        mask = jnp.where(core == 0, jnp.where(i == 0, even0, even1), jnp.where(i == 0, odd0, odd1))
        at = 2 + 2 * (chip ^ mask) + b
        return info_ref[3 + at // ndoc, at % ndoc]

    def scores(b, docs_ref, place_ref, q_ref, i, out_ref, u, *flat):
        rounds = info_ref[2, b]
        max_ref[...] = jnp.full(max_ref.shape, LOWEST, jnp.float32)
        if flat:
            streamed_maxima(rounds, info_ref, b, docs_ref, q_ref, i, max_ref, (flat[:RING], flat[RING:2 * RING]))
        else:
            plain_maxima(rounds, info_ref, b, docs_ref, q_ref, i, max_ref)
        sums = []
        for g in range(groups):
            total = max_ref[g, :, :128]
            for j in range(1, width // 128):
                total = total + max_ref[g, :, j * 128:(j + 1) * 128]
            sums.append(total)
        turned = jnp.concatenate(sums, axis=0).T
        high = turned.astype(place_ref.dtype)
        low = (turned - high.astype(jnp.float32)).astype(place_ref.dtype)
        halves = jnp.concatenate([high, low], axis=1)
        if flat:
            pltpu.matmul_push_rhs(place_ref[...], 0, 0)
            pltpu.matmul_acc_lhs(flat[-1], halves, load_staged_rhs=0)
            spread = pltpu.matmul_pop(flat[-1])[:, :ndoc]
        else:
            spread = jnp.dot(halves, place_ref[...], preferred_element_type=jnp.float32)[:, :ndoc]
        score = spread[:count]
        for j in range(1, 128 // count):
            score = score + spread[j * count:(j + 1) * count]
        out_ref[u] = score

    for b in range(2):
        docs_ref, place_ref = (own_docs, other_docs)[b], (own_place, other_place)[b]
        out_ref = (own_out, other_out)[b]

        for a in range(arrays):
            @pl.loop(0, 2)
            def _(i, a=a, b=b, docs_ref=docs_ref, place_ref=place_ref, out_ref=out_ref):
                @pl.when(flag(a, i, b) > 0)
                def _():
                    run = functools.partial(scores, b, docs_ref, place_ref, sent[a], i, out_ref, 2 * a + i)
                    if width % 512 == 0:
                        pl.run_scoped(
                            run,
                            *[pltpu.ACC(mxu_id=x)((SUB, 256), jnp.float32) for x in range(2) for _ in range(RING)],
                            pltpu.ACC(mxu_id=0)((128, 256), jnp.float32),
                        )
                    else:
                        run()

                @pl.when(flag(a, i, b) == 0)
                def _():
                    out_ref[2 * a + i] = jnp.zeros(out_ref.shape[1:], jnp.float32)


def score_units(info, packs, sent, masks, count):
    width = sent[0].shape[2]
    ndoc = packs[0][1].shape[0] // 2
    shape = jax.ShapeDtypeStruct((len(masks), count, ndoc), jnp.float32)
    return pl.pallas_call(
        functools.partial(score_kernel, masks=masks),
        out_shape=(shape, shape),
        in_specs=[SMEM] + [VMEM] * (4 + len(sent)),
        out_specs=(VMEM, VMEM),
        scratch_shapes=[pltpu.VMEM((ndoc // GROUP + 1, GROUP, width), jnp.float32)],
        compiler_params=pltpu.CompilerParams(vmem_limit_bytes=16 << 20),
        cost_estimate=pl.CostEstimate(flops=0, bytes_accessed=0, transcendentals=0),
        name="score_units",
    )(info, packs[0][0], packs[1][0], packs[0][1], packs[1][1], *sent)


def place_kernel(info_ref, *refs, masks):
    out_ref = refs[-1]
    core, chip = info_ref[3, 0], info_ref[3, 1]
    owns, (early_ref, last_ref) = refs[:len(masks)], refs[len(masks):-1]
    done = 0
    for part, own_ref in zip(masks, owns):
        for u, (even, odd) in enumerate(part):
            mine = chip ^ jnp.where(core == 0, even, odd)
            theirs = chip ^ jnp.where(core == 0, odd, even)
            got_ref, at = (early_ref, done) if done < early_ref.shape[0] else (last_ref, done - early_ref.shape[0])
            out_ref[2 * mine + core] = own_ref[u]
            out_ref[2 * theirs + 1 - core] = got_ref[at]
            done += 1


def place_scores(info, owns, gots, masks, devices):
    count, ndoc = gots[0].shape[1:]
    return pl.pallas_call(
        functools.partial(place_kernel, masks=masks),
        out_shape=jax.ShapeDtypeStruct((devices, count, ndoc), jnp.float32),
        in_specs=[SMEM] + [VMEM] * (len(owns) + len(gots)),
        out_specs=VMEM,
        name="place_scores",
    )(info, *owns, *gots)


def xor_pairs(devices, even, odd):
    return [(i, ((i // 2) ^ (odd if i % 2 else even)) * 2 + i % 2) for i in range(devices)]


def after(array, *others):
    return lax.optimization_barrier((array, *others))[0]


def local(queries, documents, lengths, pattern):
    devices = lax.axis_size("docs")
    halves = lax.axis_size("pb")
    planes = devices // 8
    me = lax.axis_index("docs")
    core, chip = me % 2, me // 2
    shard_rows = queries.shape[0]
    swap = [(i, i ^ 1) for i in range(devices)]

    if halves > 1:
        queries = lax.all_to_all(queries, "pb", split_axis=0, concat_axis=1, tiled=True)
    count = queries.shape[0]

    def send(array, even, odd=None):
        return lax.ppermute(array, "docs", xor_pairs(devices, even, even if odd is None else odd))

    def join(a, b):
        return jnp.concatenate([a, b], axis=0)

    unit = turn_queries(queries)
    crossed = {e: send(unit, 4 * e) for e in range(2, planes, 2)}

    packs = [pack_documents(documents, lengths),
             pack_documents(lax.ppermute(documents, "docs", swap), lax.ppermute(lengths, "docs", swap))]

    chips = jnp.arange(devices // 2, dtype=jnp.int32)
    row_block = ((2 * chips + core) * shard_rows + lax.axis_index("pb") * count) // BLOCK
    both = jnp.stack([me, me ^ 1])
    hot = (row_block[:, None] == jnp.arange(pattern.shape[0], dtype=jnp.int32)[None]).astype(jnp.int32)
    mine = (both[:, None] == jnp.arange(pattern.shape[1], dtype=jnp.int32)[None]).astype(jnp.int32)
    columns = jnp.sum(pattern[:, None, :] * mine[None], axis=2)
    flags = jnp.sum(hot[:, :, None] * columns[None], axis=1)
    ndoc = lengths.shape[0]
    seats = jnp.concatenate([jnp.stack([core, chip]), flags.reshape(-1)])
    seats = jnp.pad(seats, (0, -seats.shape[0] % ndoc)).reshape(-1, ndoc)
    steps = [p[2] for p in packs]
    rounds = jnp.pad(jnp.stack([steps[0][1, 0], steps[1][1, 0]]), (0, ndoc - 2))[None]
    info = jnp.concatenate([steps[0][:1], steps[1][:1], rounds, seats], axis=0)

    owns, others, placed = [], [], []

    def score(*parts):
        masks = []
        for _, z, past in parts:
            for i in range(2):
                masks.append((4 * z + 2 * past + i, 4 * z + past + 2 * i))
        own, other = score_units(info, packs, [p[0] for p in parts], tuple(masks), count)
        owns.append(own)
        others.append(other)
        placed.append(tuple(masks))
        return other

    def spread(z, here):
        return join(here, send(here, 1, 2))

    def onward(near, z):
        return send(near, 4) if z + 1 < planes else None, send(near, 2, 1)

    near = spread(0, unit)
    waiting = []
    for z in range(0, planes, 2):
        pair, far = onward(near, z)
        done = score((near, z, 0))
        if z + 2 < planes:
            near = spread(z + 2, after(crossed[z + 2], done))
        done = score((after(far, done), z, 1))
        if pair is not None:
            pair = after(pair, done)
            waiting.append((pair, send(pair, 2, 1), z + 1))
        near = after(near, done)
    for pair, far, z in waiting:
        done = score((after(pair, done), z, 0))
        done = score((after(far, done), z, 1))

    early = lax.ppermute(jnp.concatenate(others[:-1], axis=0), "docs", swap)
    gots = [early, lax.ppermute(others[-1], "docs", swap)]
    return place_scores(info, owns, gots, tuple(placed), devices)


def solution(mesh):
    mapped = jax.shard_map(
        local,
        mesh=mesh,
        in_specs=(P("docs", "pb", None), P("docs", None, None), P("docs"), P()),
        out_specs=P(None, "pb", "docs"),
        check_vma=False,
    )

    def run(*arrays):
        with jax.sharding.use_abstract_mesh(mesh.abstract_mesh):
            return mapped(*arrays)

    return run
```

```python
import functools

import jax
import jax.numpy as jnp
from jax import lax
from jax.experimental import pallas as pl
from jax.experimental.pallas import tpu as pltpu
from jax.sharding import PartitionSpec as P

BLOCK = 128
GROUP = 8
STEP = 8
SUB = GROUP * STEP
RING = 8
LAG = 7
PAD = 8
SIDE = 2
LOWEST = -3e38
VMEM = pl.BlockSpec(memory_space=pltpu.VMEM)
SMEM = pl.BlockSpec(memory_space=pltpu.SMEM)
ANY = pl.BlockSpec(memory_space=pl.ANY)
HBM = pl.BlockSpec(memory_space=pltpu.HBM)
FREE = pl.CostEstimate(flops=0, bytes_accessed=0, transcendentals=0)
BUSY = pl.CostEstimate(flops=16 << 30, bytes_accessed=0, transcendentals=0)


def query_kernel(q_ref, out_ref, rows_ref):
    count, tokens, _ = q_ref.shape
    pitch = rows_ref.shape[0] // count
    for i in range(count):
        rows_ref[i * pitch:i * pitch + tokens, :] = q_ref[i].astype(jnp.float32)
    span = 128 // count
    for j in range(tokens // span):
        parts = [rows_ref[pl.ds(j * span + t, count, stride=pitch), :] for t in range(span)]
        out_ref[0, :, j * 128:(j + 1) * 128] = jnp.concatenate(parts, axis=0).T.astype(out_ref.dtype)


def turn_queries(queries):
    count, tokens, width = queries.shape
    return pl.pallas_call(
        query_kernel,
        out_shape=jax.ShapeDtypeStruct((1, width, tokens * count), queries.dtype),
        in_specs=[VMEM],
        out_specs=VMEM,
        scratch_shapes=[pltpu.VMEM((count * (tokens + PAD), width), jnp.float32)],
        compiler_params=pltpu.CompilerParams(vmem_limit_bytes=4 << 20),
        cost_estimate=FREE,
        name="turn_queries",
    )(queries)


def sort_tables(length):
    ndoc = length.shape[1]
    square = (ndoc, ndoc)
    down = lax.broadcasted_iota(jnp.int32, square, 0)
    across = lax.broadcasted_iota(jnp.int32, square, 1)
    down_f, across_f = down.astype(jnp.float32), across.astype(jnp.float32)
    len_across = jnp.broadcast_to(length.astype(jnp.float32), square)
    len_down = len_across.T

    def count(hits, axis):
        return jnp.sum(jnp.where(hits, 1.0, 0.0), axis=axis, keepdims=True)

    ahead = (len_across > len_down) | ((len_across == len_down) & (across < down))
    behind = (len_down > len_across) | ((len_down == len_across) & (down < across))
    rank_down = count(ahead, 1)
    rank_across = count(behind, 0)
    placed = rank_across == down_f
    limit_down = jnp.sum(jnp.where(placed, len_across, 0.0), axis=1, keepdims=True)
    taken = rank_down == across_f
    order = jnp.sum(jnp.where(taken, down_f, 0.0), axis=0, keepdims=True)
    limit_across = jnp.sum(jnp.where(taken, len_down, 0.0), axis=0, keepdims=True)

    def steps_of(limit):
        return jnp.broadcast_to(((limit.astype(jnp.int32) + (STEP - 1)) // STEP).astype(jnp.float32), square)

    steps_down, steps_across = steps_of(limit_down), steps_of(limit_across)
    head_down, head_across = down % GROUP == 0, across % GROUP == 0
    starts = jnp.sum(jnp.where(head_down & (down < across * GROUP), steps_down, 0.0), axis=0, keepdims=True)
    ends = jnp.sum(jnp.where(head_across & (across <= down), steps_across, 0.0), axis=1, keepdims=True)
    group = count(head_down & (ends <= across_f), 0)
    total = jnp.sum(jnp.where(head_down, steps_down, 0.0), axis=0, keepdims=True).astype(jnp.int32)
    rounds = (total + (RING - 1)) // RING
    return order.astype(jnp.int32), starts.astype(jnp.int32), limit_down, group.astype(jnp.int32), rounds, placed


def document_kernel(docs_hbm, length_hbm, out_ref, place_ref, steps_ref,
                    docs_ref, rows_ref, limit_ref, length_ref, row_ref, table_ref, docs_sem, length_sem, sem):
    ndoc, slots, _ = docs_hbm.shape
    pitch = rows_ref.shape[1] // GROUP
    length_copy = pltpu.make_async_copy(length_hbm, length_ref, length_sem)
    docs_copy = pltpu.make_async_copy(docs_hbm, docs_ref, docs_sem)
    length_copy.start()
    docs_copy.start()
    length_copy.wait()
    order, starts, limit, group, rounds, placed = sort_tables(length_ref[...])
    row_ref[0:1, :] = order
    row_ref[1:2, :] = starts
    to_scalars = pltpu.make_async_copy(row_ref, table_ref, sem)
    to_scalars.start()
    limit_ref[...] = limit
    steps_ref[0:1, :] = group
    steps_ref[1:2, :] = rounds
    place = jnp.where(placed, 1.0, 0.0).astype(place_ref.dtype)
    place_ref[...] = jnp.concatenate([jnp.concatenate([place, place], axis=0)] * 2, axis=1)
    to_scalars.wait()
    docs_copy.wait()

    @pl.loop(0, ndoc // GROUP // SIDE)
    def _(turn):
        for side in range(SIDE):
            g = turn * SIDE + side
            for i in range(GROUP):
                doc = table_ref[0, g * GROUP + i]
                rows_ref[side, i * pitch:i * pitch + slots, :] = docs_ref[doc].astype(jnp.float32)
        for side in range(SIDE):
            g = turn * SIDE + side
            limit = limit_ref[pl.ds(pl.multiple_of(g * GROUP, GROUP), GROUP), :].astype(jnp.int32)
            first = rows_ref[side, pl.ds(0, GROUP, stride=pitch), :]
            base = table_ref[1, g] * SUB
            for s in range(0, slots, 2):
                pair = []
                for k in (s, s + 1):
                    tile = rows_ref[side, pl.ds(k, GROUP, stride=pitch), :]
                    pair.append(jnp.where(limit > k, tile, first))
                at = pl.multiple_of(base + s * GROUP, 2 * GROUP)
                out_ref[pl.ds(at, 2 * GROUP), :] = jnp.concatenate(pair, axis=0).astype(out_ref.dtype)


def pack_documents(documents, lengths, space, cost, limit):
    ndoc, slots, width = documents.shape
    return pl.pallas_call(
        document_kernel,
        out_shape=(
            jax.ShapeDtypeStruct((ndoc * slots, width), documents.dtype),
            jax.ShapeDtypeStruct((2 * ndoc, 2 * ndoc), documents.dtype),
            jax.ShapeDtypeStruct((2, ndoc), jnp.int32),
        ),
        in_specs=[space, space],
        out_specs=(VMEM, VMEM, VMEM),
        scratch_shapes=[
            pltpu.VMEM((ndoc, slots, width), documents.dtype),
            pltpu.VMEM((SIDE, GROUP * (slots + PAD), width), jnp.float32),
            pltpu.VMEM((ndoc, 1), jnp.float32),
            pltpu.VMEM((1, ndoc), jnp.int32),
            pltpu.VMEM((8, ndoc), jnp.int32),
            pltpu.SMEM((8, ndoc), jnp.int32),
            pltpu.SemaphoreType.DMA,
            pltpu.SemaphoreType.DMA,
            pltpu.SemaphoreType.DMA,
        ],
        compiler_params=pltpu.CompilerParams(vmem_limit_bytes=limit),
        cost_estimate=cost,
        name="pack_documents",
    )(documents, lengths.reshape(1, ndoc))


def fold(max_ref, step_group, at, best):
    span = slice(at, at + best.shape[1])
    max_ref[step_group, :, span] = jnp.maximum(max_ref[step_group, :, span], best)


def streamed_maxima(b, steps_ref, docs_ref, q_ref, u, max_ref, accs):
    width = q_ref.shape[2]
    rounds = steps_ref[2 * b + 1, 0]
    none_q = jnp.zeros((q_ref.shape[1], 256), q_ref.dtype)
    none_d = jnp.zeros((SUB, q_ref.shape[1]), q_ref.dtype)

    def feed(step, slot, staged):
        rows = docs_ref[pl.ds(pl.multiple_of(step * SUB, SUB), SUB), :]
        rows = jnp.concatenate([rows, none_d], axis=1)
        for unit in range(2):
            pltpu.matmul_acc_lhs(accs[unit][slot], rows, load_staged_rhs=staged)

    def retire(step, slot, pair):
        group = steps_ref[2 * b, step]
        for unit in range(2):
            got = pltpu.matmul_pop(accs[unit][slot])
            best = jnp.max(got.reshape(STEP, GROUP, 256), axis=0)
            fold(max_ref, group, (2 * pair + unit) * 256, best)

    for pair in range(width // 512):
        for unit in range(2):
            at = (2 * pair + unit) * 256
            pltpu.matmul_push_rhs(jnp.concatenate([q_ref[u, :, at:at + 256], none_q], axis=0), pair % 2, unit)
        for slot in range(RING):
            feed(slot, slot, pair % 2 if slot == 0 else None)
            if slot >= LAG:
                retire(slot - LAG, slot - LAG, pair)

        @pl.loop(1, rounds)
        def _(r, pair=pair):
            for slot in range(RING):
                step = r * RING + slot
                feed(step, slot, None)
                retire(step - LAG, (slot - LAG) % RING, pair)

        for k in range(RING - LAG, RING):
            retire((rounds - 1) * RING + k, k, pair)


def plain_maxima(b, steps_ref, docs_ref, q_ref, u, max_ref):
    @pl.loop(0, steps_ref[2 * b + 1, 0] * RING)
    def _(step):
        rows = docs_ref[pl.ds(pl.multiple_of(step * SUB, SUB), SUB), :]
        similar = jnp.dot(rows, q_ref[u], preferred_element_type=jnp.float32)
        fold(max_ref, steps_ref[2 * b, step], 0, jnp.max(similar.reshape(STEP, GROUP, similar.shape[1]), axis=0))


def seat():
    me = lax.axis_index("docs")
    return me % 2, me // 2


def score_kernel(pattern_ref, steps_ref, own_docs, other_docs, own_place, other_place, *refs,
                 masks, shard_rows):
    arrays = len(masks) // 2
    sent, (own_out, other_out, max_ref) = refs[:arrays], refs[arrays:]
    count, ndoc = own_out.shape[1:]
    width = sent[0].shape[2]
    groups = ndoc // GROUP
    core, chip = seat()

    def scores(b, docs_ref, place_ref, out_ref, q_ref, i, u, *flat):
        max_ref[...] = jnp.full(max_ref.shape, LOWEST, jnp.float32)
        if flat:
            streamed_maxima(b, steps_ref, docs_ref, q_ref, i, max_ref, (flat[:RING], flat[RING:2 * RING]))
        else:
            plain_maxima(b, steps_ref, docs_ref, q_ref, i, max_ref)
        sums = []
        for g in range(groups):
            total = max_ref[g, :, :128]
            for j in range(1, width // 128):
                total = total + max_ref[g, :, j * 128:(j + 1) * 128]
            sums.append(total)
        turned = jnp.concatenate(sums, axis=0).T
        high = turned.astype(place_ref.dtype)
        low = (turned - high.astype(jnp.float32)).astype(place_ref.dtype)
        halves = jnp.concatenate([high, low], axis=1)
        if flat:
            pltpu.matmul_push_rhs(place_ref[...], 0, 0)
            pltpu.matmul_acc_lhs(flat[-1], halves, load_staged_rhs=0)
            spread = pltpu.matmul_pop(flat[-1])[:, :ndoc]
        else:
            spread = jnp.dot(halves, place_ref[...], preferred_element_type=jnp.float32)[:, :ndoc]
        score = spread[:count]
        for j in range(1, 128 // count):
            score = score + spread[j * count:(j + 1) * count]
        out_ref[u] = score

    for b in range(2):
        block = (b, (own_docs, other_docs)[b], (own_place, other_place)[b], (own_out, other_out)[b])
        for a in range(arrays):
            (even0, odd0), (even1, odd1) = masks[2 * a:2 * a + 2]

            @pl.loop(0, 2)
            def _(i, a=a, b=b, block=block, even0=even0, odd0=odd0, even1=even1, odd1=odd1):
                mask = jnp.where(core == 0, jnp.where(i == 0, even0, even1), jnp.where(i == 0, odd0, odd1))
                first = (2 * (chip ^ mask) + core) * shard_rows + lax.axis_index("pb") * count
                flag = pattern_ref[first // BLOCK, 2 * chip + (core ^ b)]

                @pl.when(flag > 0)
                def _():
                    run = functools.partial(scores, *block, sent[a], i, 2 * a + i)
                    if width % 512 == 0:
                        pl.run_scoped(
                            run,
                            *[pltpu.ACC(mxu_id=x)((SUB, 256), jnp.float32) for x in range(2) for _ in range(RING)],
                            pltpu.ACC(mxu_id=0)((128, 256), jnp.float32),
                        )
                    else:
                        run()

                @pl.when(flag <= 0)
                def _():
                    block[3][2 * a + i] = jnp.zeros((count, ndoc), jnp.float32)


def score_units(pattern, steps, packs, sent, masks, count, shard_rows, cost):
    width = sent[0].shape[2]
    (own_docs, own_place, _), (other_docs, other_place, _) = packs
    ndoc = steps.shape[1]
    shape = jax.ShapeDtypeStruct((len(masks), count, ndoc), jnp.float32)
    return pl.pallas_call(
        functools.partial(score_kernel, masks=masks, shard_rows=shard_rows),
        out_shape=(shape, shape),
        in_specs=[SMEM] * 2 + [VMEM] * (4 + len(sent)),
        out_specs=(VMEM, VMEM),
        scratch_shapes=[pltpu.VMEM((ndoc // GROUP + 1, GROUP, width), jnp.float32)],
        compiler_params=pltpu.CompilerParams(vmem_limit_bytes=16 << 20),
        cost_estimate=cost,
        name="score_units",
    )(pattern, steps, own_docs, other_docs, own_place, other_place, *sent)


def place_kernel(*refs, masks):
    arrays = len(masks)
    owns, got_ref, out_ref, sem = refs[:arrays], refs[arrays], refs[-2], refs[-1]
    core, chip = seat()
    copies = []
    for part, own_ref in zip(masks, owns):
        for u, (even, odd) in enumerate(part):
            mine = chip ^ jnp.where(core == 0, even, odd)
            theirs = chip ^ jnp.where(core == 0, odd, even)
            at = len(copies)
            copies.append(pltpu.make_async_copy(own_ref.at[u], out_ref.at[2 * mine + core], sem.at[at]))
            copies.append(pltpu.make_async_copy(got_ref.at[at // 2], out_ref.at[2 * theirs + 1 - core], sem.at[at + 1]))
    for copy in copies:
        copy.start()
    for copy in copies:
        copy.wait()


def place_scores(before, owns, got, masks, devices):
    units, count, ndoc = got.shape
    held = [] if before is None else [before]
    return pl.pallas_call(
        functools.partial(place_kernel, masks=masks),
        out_shape=jax.ShapeDtypeStruct((devices, count, ndoc), jnp.float32),
        in_specs=[VMEM] * (len(owns) + 1) + [HBM] * len(held),
        out_specs=HBM,
        scratch_shapes=[pltpu.SemaphoreType.DMA((2 * units,))],
        input_output_aliases={len(owns) + 1: 0} if held else {},
        compiler_params=pltpu.CompilerParams(vmem_limit_bytes=4 << 20),
        cost_estimate=FREE,
        name="place_scores",
    )(*owns, got, *held)


def xor_pairs(devices, even, odd):
    return [(i, ((i // 2) ^ (odd if i % 2 else even)) * 2 + i % 2) for i in range(devices)]


def after(array, *others):
    return lax.optimization_barrier((array, *others))[0]


def local(queries, documents, lengths, pattern):
    devices = lax.axis_size("docs")
    halves = lax.axis_size("pb")
    planes = devices // 8
    shard_rows = queries.shape[0]
    swap = [(i, i ^ 1) for i in range(devices)]

    if halves > 1:
        queries = lax.all_to_all(queries, "pb", split_axis=0, concat_axis=1, tiled=True)
    count = queries.shape[0]

    def send(array, even, odd=None):
        return lax.ppermute(array, "docs", xor_pairs(devices, even, even if odd is None else odd))

    def join(a, b):
        return jnp.concatenate([a, b], axis=0)

    unit = turn_queries(queries)
    crossed = {e: send(unit, 4 * e) for e in range(2, planes, 2)}

    packs = (pack_documents(documents, lengths, HBM, FREE, 16 << 20),
             pack_documents(lax.ppermute(documents, "docs", swap), lax.ppermute(lengths, "docs", swap), ANY, FREE, 16 << 20))

    steps = jnp.concatenate([packs[0][2], packs[1][2]], axis=0)

    owns, others, placed = [], [], []

    def score(*parts):
        masks = []
        for _, z, past in parts:
            for i in range(2):
                masks.append((4 * z + 2 * past + i, 4 * z + past + 2 * i))
        own, other = score_units(pattern, steps, packs, [p[0] for p in parts], tuple(masks), count, shard_rows,
                                 BUSY if not owns else FREE)
        owns.append(own)
        others.append(other)
        placed.append(tuple(masks))
        return other

    def spread(z, here):
        return join(here, send(here, 1, 2))

    def onward(near, z):
        return send(near, 4) if z + 1 < planes else None, send(near, 2, 1)

    near = join(unit, after(send(unit, 1, 2), packs[0][2]))
    for z in range(0, planes, 2):
        pair, far = onward(near, z)
        more = z + 2 < planes
        arrived = after(crossed[z + 2], packs[1][2]) if more else near
        if z == 0:
            done = score((after(near, arrived), 0, 0))
        else:
            done = score((after(pair_before, done), z - 1, 0), (after(near, arrived), z, 0))
            done = score((after(far_before, done), z - 1, 1))
        if more:
            near = spread(z + 2, arrived if z == 0 else after(arrived, done))
            done = score((after(far, done), z, 1))
            near, pair = after(near, done), after(pair, done)
            pair_before, far_before = pair, send(pair, 2, 1)
    early = None
    if pair is None:
        done = score((after(far, done), z, 1))
    else:
        pair = after(pair, done)
        pair_far = send(pair, 2, 1)
        done = score((after(far, done), z, 1), (pair, z + 1, 0))
        got = lax.ppermute(jnp.concatenate(others, axis=0), "docs", swap)
        early = place_scores(None, owns, got, tuple(placed), devices)
        pair_far, early, _ = lax.optimization_barrier((pair_far, early, done))
        owns.clear(), others.clear(), placed.clear()
        score((pair_far, z + 1, 1))
    got = lax.ppermute(jnp.concatenate(others, axis=0), "docs", swap)
    return place_scores(early, owns, got, tuple(placed), devices)


def solution(mesh):
    mapped = jax.shard_map(
        local,
        mesh=mesh,
        in_specs=(P("docs", "pb", None), P("docs", None, None), P("docs"), P()),
        out_specs=P(None, "pb", "docs"),
        check_vma=False,
    )

    def run(*arrays):
        with jax.sharding.use_abstract_mesh(mesh.abstract_mesh):
            return mapped(*arrays)

    return run
```

```python
import functools

import jax
import jax.numpy as jnp
from jax import lax
from jax.experimental import pallas as pl
from jax.experimental.pallas import tpu as pltpu
from jax.sharding import PartitionSpec as P

BLOCK = 128
GROUP = 8
STEP = 8
SUB = GROUP * STEP
RING = 8
LAG = 7
PAD = 8
SIDE = 2
LOWEST = -3e38
VMEM = pl.BlockSpec(memory_space=pltpu.VMEM)
SMEM = pl.BlockSpec(memory_space=pltpu.SMEM)
ANY = pl.BlockSpec(memory_space=pl.ANY)
HBM = pl.BlockSpec(memory_space=pltpu.HBM)
FREE = pl.CostEstimate(flops=0, bytes_accessed=0, transcendentals=0)
BUSY = pl.CostEstimate(flops=16 << 30, bytes_accessed=0, transcendentals=0)


def query_kernel(q_ref, out_ref, rows_ref):
    count, tokens, _ = q_ref.shape
    pitch = rows_ref.shape[0] // count
    for i in range(count):
        rows_ref[i * pitch:i * pitch + tokens, :] = q_ref[i].astype(jnp.float32)
    span = 128 // count
    for j in range(tokens // span):
        parts = [rows_ref[pl.ds(j * span + t, count, stride=pitch), :] for t in range(span)]
        out_ref[0, :, j * 128:(j + 1) * 128] = jnp.concatenate(parts, axis=0).T.astype(out_ref.dtype)


def turn_queries(queries):
    count, tokens, width = queries.shape
    return pl.pallas_call(
        query_kernel,
        out_shape=jax.ShapeDtypeStruct((1, width, tokens * count), queries.dtype),
        in_specs=[VMEM],
        out_specs=VMEM,
        scratch_shapes=[pltpu.VMEM((count * (tokens + PAD), width), jnp.float32)],
        compiler_params=pltpu.CompilerParams(vmem_limit_bytes=4 << 20),
        cost_estimate=FREE,
        name="turn_queries",
    )(queries)


def sort_tables(length):
    ndoc = length.shape[1]
    square = (ndoc, ndoc)
    down = lax.broadcasted_iota(jnp.int32, square, 0)
    across = lax.broadcasted_iota(jnp.int32, square, 1)
    down_f, across_f = down.astype(jnp.float32), across.astype(jnp.float32)
    len_across = jnp.broadcast_to(length.astype(jnp.float32), square)
    len_down = len_across.T

    def count(hits, axis):
        return jnp.sum(jnp.where(hits, 1.0, 0.0), axis=axis, keepdims=True)

    ahead = (len_across > len_down) | ((len_across == len_down) & (across < down))
    behind = (len_down > len_across) | ((len_down == len_across) & (down < across))
    rank_down = count(ahead, 1)
    rank_across = count(behind, 0)
    placed = rank_across == down_f
    limit_down = jnp.sum(jnp.where(placed, len_across, 0.0), axis=1, keepdims=True)
    taken = rank_down == across_f
    order = jnp.sum(jnp.where(taken, down_f, 0.0), axis=0, keepdims=True)
    limit_across = jnp.sum(jnp.where(taken, len_down, 0.0), axis=0, keepdims=True)

    def steps_of(limit):
        return jnp.broadcast_to(((limit.astype(jnp.int32) + (STEP - 1)) // STEP).astype(jnp.float32), square)

    steps_down, steps_across = steps_of(limit_down), steps_of(limit_across)
    head_down, head_across = down % GROUP == 0, across % GROUP == 0
    starts = jnp.sum(jnp.where(head_down & (down < across * GROUP), steps_down, 0.0), axis=0, keepdims=True)
    ends = jnp.sum(jnp.where(head_across & (across <= down), steps_across, 0.0), axis=1, keepdims=True)
    group = count(head_down & (ends <= across_f), 0)
    total = jnp.sum(jnp.where(head_down, steps_down, 0.0), axis=0, keepdims=True).astype(jnp.int32)
    rounds = (total + (RING - 1)) // RING
    return order.astype(jnp.int32), starts.astype(jnp.int32), limit_down, group.astype(jnp.int32), rounds, placed


def document_kernel(docs_hbm, length_hbm, out_ref, place_ref, steps_ref,
                    docs_ref, rows_ref, limit_ref, length_ref, row_ref, table_ref, docs_sem, length_sem, sem):
    ndoc, slots, _ = docs_hbm.shape
    pitch = rows_ref.shape[1] // GROUP
    length_copy = pltpu.make_async_copy(length_hbm, length_ref, length_sem)
    docs_copy = pltpu.make_async_copy(docs_hbm, docs_ref, docs_sem)
    length_copy.start()
    docs_copy.start()
    length_copy.wait()
    order, starts, limit, group, rounds, placed = sort_tables(length_ref[...])
    row_ref[0:1, :] = order
    row_ref[1:2, :] = starts
    to_scalars = pltpu.make_async_copy(row_ref, table_ref, sem)
    to_scalars.start()
    limit_ref[...] = limit
    steps_ref[0:1, :] = group
    steps_ref[1:2, :] = rounds
    place = jnp.where(placed, 1.0, 0.0).astype(place_ref.dtype)
    place_ref[...] = jnp.concatenate([jnp.concatenate([place, place], axis=0)] * 2, axis=1)
    to_scalars.wait()
    docs_copy.wait()

    @pl.loop(0, ndoc // GROUP // SIDE)
    def _(turn):
        for side in range(SIDE):
            g = turn * SIDE + side
            for i in range(GROUP):
                doc = table_ref[0, g * GROUP + i]
                rows_ref[side, i * pitch:i * pitch + slots, :] = docs_ref[doc].astype(jnp.float32)
        for side in range(SIDE):
            g = turn * SIDE + side
            limit = limit_ref[pl.ds(pl.multiple_of(g * GROUP, GROUP), GROUP), :].astype(jnp.int32)
            first = rows_ref[side, pl.ds(0, GROUP, stride=pitch), :]
            base = table_ref[1, g] * SUB
            for s in range(0, slots, 2):
                pair = []
                for k in (s, s + 1):
                    tile = rows_ref[side, pl.ds(k, GROUP, stride=pitch), :]
                    pair.append(jnp.where(limit > k, tile, first))
                at = pl.multiple_of(base + s * GROUP, 2 * GROUP)
                out_ref[pl.ds(at, 2 * GROUP), :] = jnp.concatenate(pair, axis=0).astype(out_ref.dtype)


def pack_documents(documents, lengths, space, cost, limit):
    ndoc, slots, width = documents.shape
    return pl.pallas_call(
        document_kernel,
        out_shape=(
            jax.ShapeDtypeStruct((ndoc * slots, width), documents.dtype),
            jax.ShapeDtypeStruct((2 * ndoc, 2 * ndoc), documents.dtype),
            jax.ShapeDtypeStruct((2, ndoc), jnp.int32),
        ),
        in_specs=[space, space],
        out_specs=(VMEM, VMEM, VMEM),
        scratch_shapes=[
            pltpu.VMEM((ndoc, slots, width), documents.dtype),
            pltpu.VMEM((SIDE, GROUP * (slots + PAD), width), jnp.float32),
            pltpu.VMEM((ndoc, 1), jnp.float32),
            pltpu.VMEM((1, ndoc), jnp.int32),
            pltpu.VMEM((8, ndoc), jnp.int32),
            pltpu.SMEM((8, ndoc), jnp.int32),
            pltpu.SemaphoreType.DMA,
            pltpu.SemaphoreType.DMA,
            pltpu.SemaphoreType.DMA,
        ],
        compiler_params=pltpu.CompilerParams(vmem_limit_bytes=limit),
        cost_estimate=cost,
        name="pack_documents",
    )(documents, lengths.reshape(1, ndoc))


def fold(max_ref, step_group, at, best):
    span = slice(at, at + best.shape[1])
    max_ref[step_group, :, span] = jnp.maximum(max_ref[step_group, :, span], best)


def streamed_maxima(b, steps_ref, docs_ref, q_ref, u, max_ref, accs):
    width = q_ref.shape[2]
    rounds = steps_ref[2 * b + 1, 0]
    none_q = jnp.zeros((q_ref.shape[1], 256), q_ref.dtype)
    none_d = jnp.zeros((SUB, q_ref.shape[1]), q_ref.dtype)

    def feed(step, slot, staged):
        rows = docs_ref[pl.ds(pl.multiple_of(step * SUB, SUB), SUB), :]
        rows = jnp.concatenate([rows, none_d], axis=1)
        for unit in range(2):
            pltpu.matmul_acc_lhs(accs[unit][slot], rows, load_staged_rhs=staged)

    def retire(step, slot, pair):
        group = steps_ref[2 * b, step]
        for unit in range(2):
            got = pltpu.matmul_pop(accs[unit][slot])
            best = jnp.max(got.reshape(STEP, GROUP, 256), axis=0)
            fold(max_ref, group, (2 * pair + unit) * 256, best)

    for pair in range(width // 512):
        for unit in range(2):
            at = (2 * pair + unit) * 256
            pltpu.matmul_push_rhs(jnp.concatenate([q_ref[u, :, at:at + 256], none_q], axis=0), pair % 2, unit)
        for slot in range(RING):
            feed(slot, slot, pair % 2 if slot == 0 else None)
            if slot >= LAG:
                retire(slot - LAG, slot - LAG, pair)

        @pl.loop(1, rounds)
        def _(r, pair=pair):
            for slot in range(RING):
                step = r * RING + slot
                feed(step, slot, None)
                retire(step - LAG, (slot - LAG) % RING, pair)

        for k in range(RING - LAG, RING):
            retire((rounds - 1) * RING + k, k, pair)


def plain_maxima(b, steps_ref, docs_ref, q_ref, u, max_ref):
    @pl.loop(0, steps_ref[2 * b + 1, 0] * RING)
    def _(step):
        rows = docs_ref[pl.ds(pl.multiple_of(step * SUB, SUB), SUB), :]
        similar = jnp.dot(rows, q_ref[u], preferred_element_type=jnp.float32)
        fold(max_ref, steps_ref[2 * b, step], 0, jnp.max(similar.reshape(STEP, GROUP, similar.shape[1]), axis=0))


def seat():
    me = lax.axis_index("docs")
    return me % 2, me // 2


def score_kernel(pattern_ref, steps_ref, own_docs, other_docs, own_place, other_place, *refs,
                 masks, shard_rows):
    arrays = len(masks) // 2
    sent, (own_out, other_out, max_ref) = refs[:arrays], refs[arrays:]
    count, ndoc = own_out.shape[1:]
    width = sent[0].shape[2]
    groups = ndoc // GROUP
    core, chip = seat()

    def scores(b, docs_ref, place_ref, out_ref, q_ref, i, u, *flat):
        max_ref[...] = jnp.full(max_ref.shape, LOWEST, jnp.float32)
        if flat:
            streamed_maxima(b, steps_ref, docs_ref, q_ref, i, max_ref, (flat[:RING], flat[RING:2 * RING]))
        else:
            plain_maxima(b, steps_ref, docs_ref, q_ref, i, max_ref)
        sums = []
        for g in range(groups):
            total = max_ref[g, :, :128]
            for j in range(1, width // 128):
                total = total + max_ref[g, :, j * 128:(j + 1) * 128]
            sums.append(total)
        turned = jnp.concatenate(sums, axis=0).T
        high = turned.astype(place_ref.dtype)
        low = (turned - high.astype(jnp.float32)).astype(place_ref.dtype)
        halves = jnp.concatenate([high, low], axis=1)
        if flat:
            pltpu.matmul_push_rhs(place_ref[...], 0, 0)
            pltpu.matmul_acc_lhs(flat[-1], halves, load_staged_rhs=0)
            spread = pltpu.matmul_pop(flat[-1])[:, :ndoc]
        else:
            spread = jnp.dot(halves, place_ref[...], preferred_element_type=jnp.float32)[:, :ndoc]
        score = spread[:count]
        for j in range(1, 128 // count):
            score = score + spread[j * count:(j + 1) * count]
        out_ref[u] = score

    for b in range(2):
        block = (b, (own_docs, other_docs)[b], (own_place, other_place)[b], (own_out, other_out)[b])
        for a in range(arrays):
            (even0, odd0), (even1, odd1) = masks[2 * a:2 * a + 2]

            @pl.loop(0, 2)
            def _(i, a=a, b=b, block=block, even0=even0, odd0=odd0, even1=even1, odd1=odd1):
                mask = jnp.where(core == 0, jnp.where(i == 0, even0, even1), jnp.where(i == 0, odd0, odd1))
                first = (2 * (chip ^ mask) + core) * shard_rows + lax.axis_index("pb") * count
                flag = pattern_ref[first // BLOCK, 2 * chip + (core ^ b)]

                @pl.when(flag > 0)
                def _():
                    run = functools.partial(scores, *block, sent[a], i, 2 * a + i)
                    if width % 512 == 0:
                        pl.run_scoped(
                            run,
                            *[pltpu.ACC(mxu_id=x)((SUB, 256), jnp.float32) for x in range(2) for _ in range(RING)],
                            pltpu.ACC(mxu_id=0)((128, 256), jnp.float32),
                        )
                    else:
                        run()

                @pl.when(flag <= 0)
                def _():
                    block[3][2 * a + i] = jnp.zeros((count, ndoc), jnp.float32)


def score_units(pattern, steps, packs, sent, masks, count, shard_rows, cost):
    width = sent[0].shape[2]
    (own_docs, own_place, _), (other_docs, other_place, _) = packs
    ndoc = steps.shape[1]
    shape = jax.ShapeDtypeStruct((len(masks), count, ndoc), jnp.float32)
    return pl.pallas_call(
        functools.partial(score_kernel, masks=masks, shard_rows=shard_rows),
        out_shape=(shape, shape),
        in_specs=[SMEM] * 2 + [VMEM] * (4 + len(sent)),
        out_specs=(VMEM, VMEM),
        scratch_shapes=[pltpu.VMEM((ndoc // GROUP + 1, GROUP, width), jnp.float32)],
        compiler_params=pltpu.CompilerParams(vmem_limit_bytes=16 << 20),
        cost_estimate=cost,
        name="score_units",
    )(pattern, steps, own_docs, other_docs, own_place, other_place, *sent)


def place_kernel(*refs, masks):
    arrays = len(masks)
    owns, got_ref, out_ref, sem = refs[:arrays], refs[arrays], refs[-2], refs[-1]
    core, chip = seat()
    copies = []
    for part, own_ref in zip(masks, owns):
        for u, (even, odd) in enumerate(part):
            mine = chip ^ jnp.where(core == 0, even, odd)
            theirs = chip ^ jnp.where(core == 0, odd, even)
            at = len(copies)
            copies.append(pltpu.make_async_copy(own_ref.at[u], out_ref.at[2 * mine + core], sem.at[at]))
            copies.append(pltpu.make_async_copy(got_ref.at[at // 2], out_ref.at[2 * theirs + 1 - core], sem.at[at + 1]))
    for copy in copies:
        copy.start()
    for copy in copies:
        copy.wait()


def place_scores(owns, got, masks, devices):
    units, count, ndoc = got.shape
    return pl.pallas_call(
        functools.partial(place_kernel, masks=masks),
        out_shape=jax.ShapeDtypeStruct((devices, count, ndoc), jnp.float32),
        in_specs=[VMEM] * (len(owns) + 1),
        out_specs=HBM,
        scratch_shapes=[pltpu.SemaphoreType.DMA((2 * units,))],
        compiler_params=pltpu.CompilerParams(vmem_limit_bytes=4 << 20),
        cost_estimate=FREE,
        name="place_scores",
    )(*owns, got)


def xor_pairs(devices, even, odd):
    return [(i, ((i // 2) ^ (odd if i % 2 else even)) * 2 + i % 2) for i in range(devices)]


def after(array, *others):
    return lax.optimization_barrier((array, *others))[0]


def local(queries, documents, lengths, pattern):
    devices = lax.axis_size("docs")
    halves = lax.axis_size("pb")
    planes = devices // 8
    shard_rows = queries.shape[0]
    swap = [(i, i ^ 1) for i in range(devices)]

    if halves > 1:
        queries = lax.all_to_all(queries, "pb", split_axis=0, concat_axis=1, tiled=True)
    count = queries.shape[0]

    def send(array, even, odd=None):
        return lax.ppermute(array, "docs", xor_pairs(devices, even, even if odd is None else odd))

    def join(a, b):
        return jnp.concatenate([a, b], axis=0)

    unit = turn_queries(queries)
    crossed = {e: send(unit, 4 * e) for e in range(2, planes, 2)}

    packs = (pack_documents(documents, lengths, HBM, FREE, 16 << 20),
             pack_documents(lax.ppermute(documents, "docs", swap), lax.ppermute(lengths, "docs", swap), ANY, FREE, 16 << 20))

    steps = jnp.concatenate([packs[0][2], packs[1][2]], axis=0)

    owns, others, placed = [], [], []

    def score(*parts):
        masks = []
        for _, z, past in parts:
            for i in range(2):
                masks.append((4 * z + 2 * past + i, 4 * z + past + 2 * i))
        own, other = score_units(pattern, steps, packs, [p[0] for p in parts], tuple(masks), count, shard_rows,
                                 BUSY if not owns else FREE)
        owns.append(own)
        others.append(other)
        placed.append(tuple(masks))
        return other

    def spread(z, here):
        return join(here, send(here, 1, 2))

    def onward(near, z):
        return send(near, 4) if z + 1 < planes else None, send(near, 2, 1)

    near = join(unit, after(send(unit, 1, 2), packs[0][2]))
    pair, far = onward(near, 0)
    upcoming = None
    if planes > 2:
        arrived = after(crossed[2], packs[1][2])
        upcoming = spread(2, arrived)
        near = after(near, arrived)
    done = score((near, 0, 0))
    done = score((after(far, done), 0, 1))
    pending = []
    for z in range(2, planes, 2):
        near = after(upcoming, done)
        before, (pair, far) = pair, onward(near, z)
        before = after(before, done, near)
        before_far = send(before, 2, 1)
        done = score((before, z - 1, 0), (near, z, 0))
        pending = [(before_far, z - 1, 1), (far, z, 1)]
        if z + 2 < planes:
            upcoming = spread(z + 2, after(crossed[z + 2], done))
            done = score((after(before_far, done), z - 1, 1), (far, z, 1))
            pending = []
    if pair is not None:
        pair = after(pair, done)
        pair_far = send(pair, 2, 1)
        done = score(*[(after(array, done), z, past) for array, z, past in pending + [(pair, planes - 1, 0)]])
        score((after(pair_far, done), planes - 1, 1))

    got = lax.ppermute(jnp.concatenate(others, axis=0), "docs", swap)
    return place_scores(owns, got, tuple(placed), devices)


def solution(mesh):
    mapped = jax.shard_map(
        local,
        mesh=mesh,
        in_specs=(P("docs", "pb", None), P("docs", None, None), P("docs"), P()),
        out_specs=P(None, "pb", "docs"),
        check_vma=False,
    )

    def run(*arrays):
        with jax.sharding.use_abstract_mesh(mesh.abstract_mesh):
            return mapped(*arrays)

    return run
```

```python
import functools

import jax
import jax.numpy as jnp
from jax import lax
from jax.experimental import pallas as pl
from jax.experimental.pallas import tpu as pltpu
from jax.sharding import PartitionSpec as P

BLOCK = 128
GROUP = 8
STEP = 8
SUB = GROUP * STEP
RING = 8
LAG = 7
PAD = 8
SIDE = 2
LOWEST = -3e38
VMEM = pl.BlockSpec(memory_space=pltpu.VMEM)
SMEM = pl.BlockSpec(memory_space=pltpu.SMEM)
ANY = pl.BlockSpec(memory_space=pl.ANY)
HBM = pl.BlockSpec(memory_space=pltpu.HBM)
FREE = pl.CostEstimate(flops=0, bytes_accessed=0, transcendentals=0)
BUSY = pl.CostEstimate(flops=16 << 30, bytes_accessed=0, transcendentals=0)


def query_kernel(q_ref, out_ref, rows_ref):
    count, tokens, _ = q_ref.shape
    pitch = rows_ref.shape[0] // count
    for i in range(count):
        rows_ref[i * pitch:i * pitch + tokens, :] = q_ref[i].astype(jnp.float32)
    span = 128 // count
    for j in range(tokens // span):
        parts = [rows_ref[pl.ds(j * span + t, count, stride=pitch), :] for t in range(span)]
        out_ref[0, :, j * 128:(j + 1) * 128] = jnp.concatenate(parts, axis=0).T.astype(out_ref.dtype)


def turn_queries(queries):
    count, tokens, width = queries.shape
    return pl.pallas_call(
        query_kernel,
        out_shape=jax.ShapeDtypeStruct((1, width, tokens * count), queries.dtype),
        in_specs=[VMEM],
        out_specs=VMEM,
        scratch_shapes=[pltpu.VMEM((count * (tokens + PAD), width), jnp.float32)],
        compiler_params=pltpu.CompilerParams(vmem_limit_bytes=4 << 20),
        cost_estimate=FREE,
        name="turn_queries",
    )(queries)


def sort_tables(length):
    ndoc = length.shape[1]
    square = (ndoc, ndoc)
    down = lax.broadcasted_iota(jnp.int32, square, 0)
    across = lax.broadcasted_iota(jnp.int32, square, 1)
    down_f, across_f = down.astype(jnp.float32), across.astype(jnp.float32)
    len_across = jnp.broadcast_to(length.astype(jnp.float32), square)
    len_down = len_across.T

    def count(hits, axis):
        return jnp.sum(jnp.where(hits, 1.0, 0.0), axis=axis, keepdims=True)

    ahead = (len_across > len_down) | ((len_across == len_down) & (across < down))
    behind = (len_down > len_across) | ((len_down == len_across) & (down < across))
    rank_down = count(ahead, 1)
    rank_across = count(behind, 0)
    placed = rank_across == down_f
    limit_down = jnp.sum(jnp.where(placed, len_across, 0.0), axis=1, keepdims=True)
    taken = rank_down == across_f
    order = jnp.sum(jnp.where(taken, down_f, 0.0), axis=0, keepdims=True)
    limit_across = jnp.sum(jnp.where(taken, len_down, 0.0), axis=0, keepdims=True)

    def steps_of(limit):
        return jnp.broadcast_to(((limit.astype(jnp.int32) + (STEP - 1)) // STEP).astype(jnp.float32), square)

    steps_down, steps_across = steps_of(limit_down), steps_of(limit_across)
    head_down, head_across = down % GROUP == 0, across % GROUP == 0
    starts = jnp.sum(jnp.where(head_down & (down < across * GROUP), steps_down, 0.0), axis=0, keepdims=True)
    ends = jnp.sum(jnp.where(head_across & (across <= down), steps_across, 0.0), axis=1, keepdims=True)
    group = count(head_down & (ends <= across_f), 0)
    total = jnp.sum(jnp.where(head_down, steps_down, 0.0), axis=0, keepdims=True).astype(jnp.int32)
    rounds = (total + (RING - 1)) // RING
    return order.astype(jnp.int32), starts.astype(jnp.int32), limit_down, group.astype(jnp.int32), rounds, placed


def document_kernel(docs_hbm, length_hbm, out_ref, place_ref, steps_ref,
                    docs_ref, rows_ref, limit_ref, length_ref, row_ref, table_ref, docs_sem, length_sem, sem):
    ndoc, slots, _ = docs_hbm.shape
    pitch = rows_ref.shape[1] // GROUP
    length_copy = pltpu.make_async_copy(length_hbm, length_ref, length_sem)
    docs_copy = pltpu.make_async_copy(docs_hbm, docs_ref, docs_sem)
    length_copy.start()
    docs_copy.start()
    length_copy.wait()
    order, starts, limit, group, rounds, placed = sort_tables(length_ref[...])
    row_ref[0:1, :] = order
    row_ref[1:2, :] = starts
    to_scalars = pltpu.make_async_copy(row_ref, table_ref, sem)
    to_scalars.start()
    limit_ref[...] = limit
    steps_ref[0:1, :] = group
    steps_ref[1:2, :] = rounds
    place = jnp.where(placed, 1.0, 0.0).astype(place_ref.dtype)
    place_ref[...] = jnp.concatenate([jnp.concatenate([place, place], axis=0)] * 2, axis=1)
    to_scalars.wait()
    docs_copy.wait()

    @pl.loop(0, ndoc // GROUP // SIDE)
    def _(turn):
        for side in range(SIDE):
            g = turn * SIDE + side
            for i in range(GROUP):
                doc = table_ref[0, g * GROUP + i]
                rows_ref[side, i * pitch:i * pitch + slots, :] = docs_ref[doc].astype(jnp.float32)
        for side in range(SIDE):
            g = turn * SIDE + side
            limit = limit_ref[pl.ds(pl.multiple_of(g * GROUP, GROUP), GROUP), :].astype(jnp.int32)
            first = rows_ref[side, pl.ds(0, GROUP, stride=pitch), :]
            base = table_ref[1, g] * SUB
            for s in range(0, slots, 2):
                pair = []
                for k in (s, s + 1):
                    tile = rows_ref[side, pl.ds(k, GROUP, stride=pitch), :]
                    pair.append(jnp.where(limit > k, tile, first))
                at = pl.multiple_of(base + s * GROUP, 2 * GROUP)
                out_ref[pl.ds(at, 2 * GROUP), :] = jnp.concatenate(pair, axis=0).astype(out_ref.dtype)


def pack_documents(documents, lengths, space):
    ndoc, slots, width = documents.shape
    return pl.pallas_call(
        document_kernel,
        out_shape=(
            jax.ShapeDtypeStruct((ndoc * slots, width), documents.dtype),
            jax.ShapeDtypeStruct((2 * ndoc, 2 * ndoc), documents.dtype),
            jax.ShapeDtypeStruct((2, ndoc), jnp.int32),
        ),
        in_specs=[space, space],
        out_specs=(VMEM, VMEM, VMEM),
        scratch_shapes=[
            pltpu.VMEM((ndoc, slots, width), documents.dtype),
            pltpu.VMEM((SIDE, GROUP * (slots + PAD), width), jnp.float32),
            pltpu.VMEM((ndoc, 1), jnp.float32),
            pltpu.VMEM((1, ndoc), jnp.int32),
            pltpu.VMEM((8, ndoc), jnp.int32),
            pltpu.SMEM((8, ndoc), jnp.int32),
            pltpu.SemaphoreType.DMA,
            pltpu.SemaphoreType.DMA,
            pltpu.SemaphoreType.DMA,
        ],
        compiler_params=pltpu.CompilerParams(vmem_limit_bytes=16 << 20),
        cost_estimate=FREE,
        name="pack_documents",
    )(documents, lengths)


def fold(max_ref, step_group, at, best):
    span = slice(at, at + best.shape[1])
    max_ref[step_group, :, span] = jnp.maximum(max_ref[step_group, :, span], best)


def streamed_maxima(b, steps_ref, docs_ref, q_ref, u, max_ref, accs):
    width = q_ref.shape[2]
    rounds = steps_ref[2 * b + 1, 0]
    none_q = jnp.zeros((q_ref.shape[1], 256), q_ref.dtype)
    none_d = jnp.zeros((SUB, q_ref.shape[1]), q_ref.dtype)

    def feed(step, slot, staged):
        rows = docs_ref[pl.ds(pl.multiple_of(step * SUB, SUB), SUB), :]
        rows = jnp.concatenate([rows, none_d], axis=1)
        for unit in range(2):
            pltpu.matmul_acc_lhs(accs[unit][slot], rows, load_staged_rhs=staged)

    def retire(step, slot, pair):
        group = steps_ref[2 * b, step]
        for unit in range(2):
            got = pltpu.matmul_pop(accs[unit][slot])
            best = jnp.max(got.reshape(STEP, GROUP, 256), axis=0)
            fold(max_ref, group, (2 * pair + unit) * 256, best)

    for pair in range(width // 512):
        for unit in range(2):
            at = (2 * pair + unit) * 256
            pltpu.matmul_push_rhs(jnp.concatenate([q_ref[u, :, at:at + 256], none_q], axis=0), pair % 2, unit)
        for slot in range(RING):
            feed(slot, slot, pair % 2 if slot == 0 else None)
            if slot >= LAG:
                retire(slot - LAG, slot - LAG, pair)

        @pl.loop(1, rounds)
        def _(r, pair=pair):
            for slot in range(RING):
                step = r * RING + slot
                feed(step, slot, None)
                retire(step - LAG, (slot - LAG) % RING, pair)

        for k in range(RING - LAG, RING):
            retire((rounds - 1) * RING + k, k, pair)


def plain_maxima(b, steps_ref, docs_ref, q_ref, u, max_ref):
    @pl.loop(0, steps_ref[2 * b + 1, 0] * RING)
    def _(step):
        rows = docs_ref[pl.ds(pl.multiple_of(step * SUB, SUB), SUB), :]
        similar = jnp.dot(rows, q_ref[u], preferred_element_type=jnp.float32)
        fold(max_ref, steps_ref[2 * b, step], 0, jnp.max(similar.reshape(STEP, GROUP, similar.shape[1]), axis=0))


def seat():
    me = lax.axis_index("docs")
    return me % 2, me // 2


def score_kernel(pattern_ref, steps_ref, own_docs, other_docs, own_place, other_place, *refs,
                 masks, shard_rows):
    arrays = len(masks) // 2
    sent, (own_out, other_out, max_ref) = refs[:arrays], refs[arrays:]
    count, ndoc = own_out.shape[1:]
    width = sent[0].shape[2]
    groups = ndoc // GROUP
    core, chip = seat()

    def scores(b, docs_ref, place_ref, out_ref, q_ref, i, u, *flat):
        max_ref[...] = jnp.full(max_ref.shape, LOWEST, jnp.float32)
        if flat:
            streamed_maxima(b, steps_ref, docs_ref, q_ref, i, max_ref, (flat[:RING], flat[RING:2 * RING]))
        else:
            plain_maxima(b, steps_ref, docs_ref, q_ref, i, max_ref)
        sums = []
        for g in range(groups):
            total = max_ref[g, :, :128]
            for j in range(1, width // 128):
                total = total + max_ref[g, :, j * 128:(j + 1) * 128]
            sums.append(total)
        turned = jnp.concatenate(sums, axis=0).T
        high = turned.astype(place_ref.dtype)
        low = (turned - high.astype(jnp.float32)).astype(place_ref.dtype)
        halves = jnp.concatenate([high, low], axis=1)
        if flat:
            pltpu.matmul_push_rhs(place_ref[...], 0, 0)
            pltpu.matmul_acc_lhs(flat[-1], halves, load_staged_rhs=0)
            spread = pltpu.matmul_pop(flat[-1])[:, :ndoc]
        else:
            spread = jnp.dot(halves, place_ref[...], preferred_element_type=jnp.float32)[:, :ndoc]
        score = spread[:count]
        for j in range(1, 128 // count):
            score = score + spread[j * count:(j + 1) * count]
        out_ref[u] = score

    for b in range(2):
        block = (b, (own_docs, other_docs)[b], (own_place, other_place)[b], (own_out, other_out)[b])
        for a in range(arrays):
            (even0, odd0), (even1, odd1) = masks[2 * a:2 * a + 2]

            @pl.loop(0, 2)
            def _(i, a=a, b=b, block=block, even0=even0, odd0=odd0, even1=even1, odd1=odd1):
                mask = jnp.where(core == 0, jnp.where(i == 0, even0, even1), jnp.where(i == 0, odd0, odd1))
                first = (2 * (chip ^ mask) + core) * shard_rows + lax.axis_index("pb") * count
                flag = pattern_ref[first // BLOCK, 2 * chip + (core ^ b)]

                @pl.when(flag > 0)
                def _():
                    run = functools.partial(scores, *block, sent[a], i, 2 * a + i)
                    if width % 512 == 0:
                        pl.run_scoped(
                            run,
                            *[pltpu.ACC(mxu_id=x)((SUB, 256), jnp.float32) for x in range(2) for _ in range(RING)],
                            pltpu.ACC(mxu_id=0)((128, 256), jnp.float32),
                        )
                    else:
                        run()

                @pl.when(flag <= 0)
                def _():
                    block[3][2 * a + i] = jnp.zeros((count, ndoc), jnp.float32)


def score_units(pattern, steps, packs, sent, masks, count, shard_rows, cost):
    width = sent[0].shape[2]
    (own_docs, own_place, _), (other_docs, other_place, _) = packs
    ndoc = steps.shape[1]
    shape = jax.ShapeDtypeStruct((len(masks), count, ndoc), jnp.float32)
    return pl.pallas_call(
        functools.partial(score_kernel, masks=masks, shard_rows=shard_rows),
        out_shape=(shape, shape),
        in_specs=[SMEM] * 2 + [VMEM] * (4 + len(sent)),
        out_specs=(VMEM, VMEM),
        scratch_shapes=[pltpu.VMEM((ndoc // GROUP + 1, GROUP, width), jnp.float32)],
        compiler_params=pltpu.CompilerParams(vmem_limit_bytes=16 << 20),
        cost_estimate=cost,
        name="score_units",
    )(pattern, steps, own_docs, other_docs, own_place, other_place, *sent)


def place_kernel(*refs, masks):
    arrays = len(masks)
    owns, got_ref, out_ref, sem = refs[:arrays], refs[arrays], refs[-2], refs[-1]
    core, chip = seat()
    copies = []
    for part, own_ref in zip(masks, owns):
        for u, (even, odd) in enumerate(part):
            mine = chip ^ jnp.where(core == 0, even, odd)
            theirs = chip ^ jnp.where(core == 0, odd, even)
            at = len(copies)
            copies.append(pltpu.make_async_copy(own_ref.at[u], out_ref.at[2 * mine + core], sem.at[at]))
            copies.append(pltpu.make_async_copy(got_ref.at[at // 2], out_ref.at[2 * theirs + 1 - core], sem.at[at + 1]))
    for copy in copies:
        copy.start()
    for copy in copies:
        copy.wait()


def place_scores(owns, got, masks, devices):
    units, count, ndoc = got.shape
    return pl.pallas_call(
        functools.partial(place_kernel, masks=masks),
        out_shape=jax.ShapeDtypeStruct((devices, count, ndoc), jnp.float32),
        in_specs=[VMEM] * (len(owns) + 1),
        out_specs=HBM,
        scratch_shapes=[pltpu.SemaphoreType.DMA((2 * units,))],
        compiler_params=pltpu.CompilerParams(vmem_limit_bytes=4 << 20),
        cost_estimate=FREE,
        name="place_scores",
    )(*owns, got)


def xor_pairs(devices, even, odd):
    return [(i, ((i // 2) ^ (odd if i % 2 else even)) * 2 + i % 2) for i in range(devices)]


def after(array, *others):
    return lax.optimization_barrier((array, *others))[0]


def local(queries, documents, lengths, pattern):
    devices = lax.axis_size("docs")
    halves = lax.axis_size("pb")
    planes = devices // 8
    shard_rows = queries.shape[0]
    swap = [(i, i ^ 1) for i in range(devices)]

    if halves > 1:
        queries = lax.all_to_all(queries, "pb", split_axis=0, concat_axis=1, tiled=True)
    count = queries.shape[0]

    def send(array, even, odd=None):
        return lax.ppermute(array, "docs", xor_pairs(devices, even, even if odd is None else odd))

    def join(a, b):
        return jnp.concatenate([a, b], axis=0)

    unit = turn_queries(queries)
    crossed = {e: send(unit, 4 * e) for e in range(2, planes, 2)}

    def held(array):
        return pltpu.with_memory_space_constraint(array, pltpu.HBM)

    lengths = lengths.reshape(1, -1)
    packs = (pack_documents(held(documents), held(lengths), HBM),
             pack_documents(lax.ppermute(documents, "docs", swap), lax.ppermute(lengths, "docs", swap), ANY))
    steps = jnp.concatenate([packs[0][2], packs[1][2]], axis=0)

    owns, others, placed = [], [], []

    def score(*parts, busy=False):
        masks = []
        for _, z, past in parts:
            for i in range(2):
                masks.append((4 * z + 2 * past + i, 4 * z + past + 2 * i))
        own, other = score_units(pattern, steps, packs, [p[0] for p in parts], tuple(masks), count, shard_rows,
                                 BUSY if busy else FREE)
        owns.append(own)
        others.append(other)
        placed.append(tuple(masks))
        return other

    def spread(z, here):
        return join(here, send(here, 1, 2))

    def onward(near, z):
        return send(near, 4) if z + 1 < planes else None, send(near, 2, 1)

    near = join(unit, after(send(unit, 1, 2), packs[0][2]))
    pair, far = onward(near, 0)
    upcoming = None
    if planes > 2:
        arrived = after(crossed[2], packs[1][2])
        upcoming = spread(2, arrived)
        near = after(near, arrived)
    done = score((near, 0, 0), busy=True)
    done = score((after(far, done), 0, 1))
    pending = []
    for z in range(2, planes, 2):
        near = after(upcoming, done)
        before, (pair, far) = pair, onward(near, z)
        before = after(before, done, near)
        before_far = send(before, 2, 1)
        done = score((before, z - 1, 0), (near, z, 0))
        pending = [(before_far, z - 1, 1)]
        done = score((after(far, done), z, 1))
        if z + 2 < planes:
            upcoming = spread(z + 2, after(crossed[z + 2], done))
            done = score((after(before_far, done), z - 1, 1))
            pending = []
    if pair is not None:
        pair = after(pair, done)
        pair_far = send(pair, 2, 1)
        done = score(*[(after(array, done), z, past) for array, z, past in pending + [(pair, planes - 1, 0)]])
        score((after(pair_far, done), planes - 1, 1))

    got = lax.ppermute(jnp.concatenate(others, axis=0), "docs", swap)
    return place_scores(owns, got, tuple(placed), devices)


def solution(mesh):
    mapped = jax.shard_map(
        local,
        mesh=mesh,
        in_specs=(P("docs", "pb", None), P("docs", None, None), P("docs"), P()),
        out_specs=P(None, "pb", "docs"),
        check_vma=False,
    )

    def run(*arrays):
        with jax.sharding.use_abstract_mesh(mesh.abstract_mesh):
            return mapped(*arrays)

    return run
```

```python
import functools

import jax
import jax.numpy as jnp
from jax import lax
from jax.experimental import pallas as pl
from jax.experimental.pallas import tpu as pltpu
from jax.sharding import PartitionSpec as P

BLOCK = 128
GROUP = 8
STEP = 8
SUB = GROUP * STEP
RING = 8
LAG = 7
PAD = 8
SIDE = 2
LOWEST = -3e38
JOBS = 256
VMEM = pl.BlockSpec(memory_space=pltpu.VMEM)
SMEM = pl.BlockSpec(memory_space=pltpu.SMEM)
ANY = pl.BlockSpec(memory_space=pl.ANY)
HBM = pl.BlockSpec(memory_space=pltpu.HBM)
FREE = pl.CostEstimate(flops=0, bytes_accessed=0, transcendentals=0)
BUSY = pl.CostEstimate(flops=16 << 30, bytes_accessed=0, transcendentals=0)


def query_kernel(q_ref, out_ref, rows_ref):
    count, tokens, _ = q_ref.shape
    pitch = rows_ref.shape[0] // count
    for i in range(count):
        rows_ref[i * pitch:i * pitch + tokens, :] = q_ref[i].astype(jnp.float32)
    span = 128 // count
    for j in range(tokens // span):
        parts = [rows_ref[pl.ds(j * span + t, count, stride=pitch), :] for t in range(span)]
        out_ref[0, :, j * 128:(j + 1) * 128] = jnp.concatenate(parts, axis=0).T.astype(out_ref.dtype)


def turn_queries(queries):
    count, tokens, width = queries.shape
    return pl.pallas_call(
        query_kernel,
        out_shape=jax.ShapeDtypeStruct((1, width, tokens * count), queries.dtype),
        in_specs=[VMEM],
        out_specs=VMEM,
        scratch_shapes=[pltpu.VMEM((count * (tokens + PAD), width), jnp.float32)],
        compiler_params=pltpu.CompilerParams(vmem_limit_bytes=4 << 20),
        cost_estimate=FREE,
        name="turn_queries",
    )(queries)


def sort_tables(length):
    ndoc = length.shape[1]
    square = (ndoc, ndoc)
    down = lax.broadcasted_iota(jnp.int32, square, 0)
    across = lax.broadcasted_iota(jnp.int32, square, 1)
    down_f, across_f = down.astype(jnp.float32), across.astype(jnp.float32)
    len_across = jnp.broadcast_to(length.astype(jnp.float32), square)
    len_down = len_across.T

    def count(hits, axis):
        return jnp.sum(jnp.where(hits, 1.0, 0.0), axis=axis, keepdims=True)

    ahead = (len_across > len_down) | ((len_across == len_down) & (across < down))
    behind = (len_down > len_across) | ((len_down == len_across) & (down < across))
    rank_down = count(ahead, 1)
    rank_across = count(behind, 0)
    placed = rank_across == down_f
    limit_down = jnp.sum(jnp.where(placed, len_across, 0.0), axis=1, keepdims=True)
    taken = rank_down == across_f
    order = jnp.sum(jnp.where(taken, down_f, 0.0), axis=0, keepdims=True)
    limit_across = jnp.sum(jnp.where(taken, len_down, 0.0), axis=0, keepdims=True)

    def steps_of(limit):
        return jnp.broadcast_to(((limit.astype(jnp.int32) + (STEP - 1)) // STEP).astype(jnp.float32), square)

    steps_down, steps_across = steps_of(limit_down), steps_of(limit_across)
    head_down, head_across = down % GROUP == 0, across % GROUP == 0
    starts = jnp.sum(jnp.where(head_down & (down < across * GROUP), steps_down, 0.0), axis=0, keepdims=True)
    ends = jnp.sum(jnp.where(head_across & (across <= down), steps_across, 0.0), axis=1, keepdims=True)
    group = count(head_down & (ends <= across_f), 0)
    total = jnp.sum(jnp.where(head_down, steps_down, 0.0), axis=0, keepdims=True).astype(jnp.int32)
    rounds = (total + (RING - 1)) // RING
    return order.astype(jnp.int32), starts.astype(jnp.int32), limit_down, group.astype(jnp.int32), rounds, placed


def seat():
    me = lax.axis_index("docs")
    return me % 2, me // 2


def plan_jobs(pattern_ref, plan_ref, order, shard_rows, count):
    core, chip = seat()
    found = jnp.int32(0)
    for at, (z, past) in enumerate(order):
        plan_ref[1, at] = found
        for i in range(2):
            there = chip ^ (4 * z + jnp.where(core == 0, 2 * past + i, past + 2 * i))
            first = (2 * there + core) * shard_rows + lax.axis_index("pb") * count
            for b in range(2):
                plan_ref[0, found] = there * JOBS + 4 * at + 2 * i + b
                found = found + jnp.where(pattern_ref[first // BLOCK, 2 * chip + (core ^ b)] > 0, 1, 0)
    plan_ref[1, len(order)] = found


def document_kernel(docs_hbm, length_hbm, *refs, order, shard_rows, count):
    if order:
        pattern_ref, out_ref, place_ref, steps_ref, plan_ref, *scratch = refs
    else:
        out_ref, place_ref, steps_ref, *scratch = refs
    pack_block(docs_hbm, length_hbm, out_ref, place_ref, steps_ref, *scratch)
    if order:
        plan_jobs(pattern_ref, plan_ref, order, shard_rows, count)


def pack_block(docs_hbm, length_hbm, out_ref, place_ref, steps_ref,
                    docs_ref, rows_ref, limit_ref, length_ref, row_ref, table_ref, docs_sem, length_sem, sem):
    ndoc, slots, _ = docs_hbm.shape
    pitch = rows_ref.shape[1] // GROUP
    length_copy = pltpu.make_async_copy(length_hbm, length_ref, length_sem)
    docs_copy = pltpu.make_async_copy(docs_hbm, docs_ref, docs_sem)
    length_copy.start()
    docs_copy.start()
    length_copy.wait()
    sequence, starts, limit, group, rounds, placed = sort_tables(length_ref[...])
    row_ref[0:1, :] = sequence
    row_ref[1:2, :] = starts
    to_scalars = pltpu.make_async_copy(row_ref, table_ref, sem)
    to_scalars.start()
    limit_ref[...] = limit
    steps_ref[0:1, :] = group
    steps_ref[1:2, :] = rounds
    place = jnp.where(placed, 1.0, 0.0).astype(place_ref.dtype)
    place_ref[...] = jnp.concatenate([jnp.concatenate([place, place], axis=0)] * 2, axis=1)
    to_scalars.wait()
    docs_copy.wait()

    @pl.loop(0, ndoc // GROUP // SIDE)
    def _(turn):
        for side in range(SIDE):
            g = turn * SIDE + side
            for i in range(GROUP):
                doc = table_ref[0, g * GROUP + i]
                rows_ref[side, i * pitch:i * pitch + slots, :] = docs_ref[doc].astype(jnp.float32)
        for side in range(SIDE):
            g = turn * SIDE + side
            limit = limit_ref[pl.ds(pl.multiple_of(g * GROUP, GROUP), GROUP), :].astype(jnp.int32)
            first = rows_ref[side, pl.ds(0, GROUP, stride=pitch), :]
            base = table_ref[1, g] * SUB
            for s in range(0, slots, 2):
                pair = []
                for k in (s, s + 1):
                    tile = rows_ref[side, pl.ds(k, GROUP, stride=pitch), :]
                    pair.append(jnp.where(limit > k, tile, first))
                at = pl.multiple_of(base + s * GROUP, 2 * GROUP)
                out_ref[pl.ds(at, 2 * GROUP), :] = jnp.concatenate(pair, axis=0).astype(out_ref.dtype)


def pack_documents(documents, lengths, space, pattern=None, order=(), shard_rows=0, count=0):
    ndoc, slots, width = documents.shape
    out_shape = [
        jax.ShapeDtypeStruct((ndoc * slots, width), documents.dtype),
        jax.ShapeDtypeStruct((2 * ndoc, 2 * ndoc), documents.dtype),
        jax.ShapeDtypeStruct((2, ndoc), jnp.int32),
    ]
    planned = pattern is not None
    if planned:
        out_shape.append(jax.ShapeDtypeStruct((2, JOBS), jnp.int32))
    return pl.pallas_call(
        functools.partial(document_kernel, order=order, shard_rows=shard_rows, count=count),
        out_shape=out_shape,
        in_specs=[space, space] + [SMEM] * planned,
        out_specs=[VMEM, VMEM, VMEM] + [SMEM] * planned,
        scratch_shapes=[
            pltpu.VMEM((ndoc, slots, width), documents.dtype),
            pltpu.VMEM((SIDE, GROUP * (slots + PAD), width), jnp.float32),
            pltpu.VMEM((ndoc, 1), jnp.float32),
            pltpu.VMEM((1, ndoc), jnp.int32),
            pltpu.VMEM((8, ndoc), jnp.int32),
            pltpu.SMEM((8, ndoc), jnp.int32),
            pltpu.SemaphoreType.DMA,
            pltpu.SemaphoreType.DMA,
            pltpu.SemaphoreType.DMA,
        ],
        compiler_params=pltpu.CompilerParams(vmem_limit_bytes=16 << 20),
        cost_estimate=FREE,
        name="pack_documents",
    )(documents, lengths, *([pattern] if planned else []))


def fold(max_ref, step_group, at, best):
    span = slice(at, at + best.shape[1])
    max_ref[step_group, :, span] = jnp.maximum(max_ref[step_group, :, span], best)


def streamed_maxima(b, steps_ref, docs_ref, q_ref, u, max_ref, accs):
    width = q_ref.shape[2]
    rounds = steps_ref[2 * b + 1, 0]
    none_q = jnp.zeros((q_ref.shape[1], 256), q_ref.dtype)
    none_d = jnp.zeros((SUB, q_ref.shape[1]), q_ref.dtype)

    def feed(step, slot, staged):
        rows = docs_ref[pl.ds(pl.multiple_of(step * SUB, SUB), SUB), :]
        rows = jnp.concatenate([rows, none_d], axis=1)
        for unit in range(2):
            pltpu.matmul_acc_lhs(accs[unit][slot], rows, load_staged_rhs=staged)

    def retire(step, slot, pair):
        group = steps_ref[2 * b, step]
        for unit in range(2):
            got = pltpu.matmul_pop(accs[unit][slot])
            best = jnp.max(got.reshape(STEP, GROUP, 256), axis=0)
            fold(max_ref, group, (2 * pair + unit) * 256, best)

    for pair in range(width // 512):
        for unit in range(2):
            at = (2 * pair + unit) * 256
            pltpu.matmul_push_rhs(jnp.concatenate([q_ref[u, :, at:at + 256], none_q], axis=0), pair % 2, unit)
        for slot in range(RING):
            feed(slot, slot, pair % 2 if slot == 0 else None)
            if slot >= LAG:
                retire(slot - LAG, slot - LAG, pair)

        @pl.loop(1, rounds)
        def _(r, pair=pair):
            for slot in range(RING):
                step = r * RING + slot
                feed(step, slot, None)
                retire(step - LAG, (slot - LAG) % RING, pair)

        for k in range(RING - LAG, RING):
            retire((rounds - 1) * RING + k, k, pair)


def plain_maxima(b, steps_ref, docs_ref, q_ref, u, max_ref):
    @pl.loop(0, steps_ref[2 * b + 1, 0] * RING)
    def _(step):
        rows = docs_ref[pl.ds(pl.multiple_of(step * SUB, SUB), SUB), :]
        similar = jnp.dot(rows, q_ref[u], preferred_element_type=jnp.float32)
        fold(max_ref, steps_ref[2 * b, step], 0, jnp.max(similar.reshape(STEP, GROUP, similar.shape[1]), axis=0))


def score_kernel(plan_ref, steps_ref, own_docs, other_docs, own_place, other_place, *refs, calls):
    arrays = calls[-1][0]
    sent, refs = refs[:arrays], refs[arrays + 2:]
    own_out, other_out, max_ref, q_ref, score_ref, q_sem, score_sem = refs
    count, ndoc = score_ref.shape[1:]
    width = q_ref.shape[2]
    groups = ndoc // GROUP
    core, _ = seat()
    begin = end = jnp.int32(0)
    for arrived, budget in calls:
        begin, end = end, plan_ref[1, arrived]
        if budget is not None:
            end = jnp.minimum(begin + budget, end)

    def fetch(n):
        job = plan_ref[0, n] % JOBS
        for a in range(arrays):
            @pl.when(job // 4 == a)
            def _(a=a):
                pltpu.make_async_copy(sent[a].at[(job // 2) % 2], q_ref.at[n % 2], q_sem.at[n % 2]).start()

    def written(slot):
        pltpu.make_async_copy(score_ref.at[slot], other_out.at[0], score_sem.at[slot]).wait()

    def scores(b, docs_ref, place_ref, slot, *flat):
        max_ref[...] = jnp.full(max_ref.shape, LOWEST, jnp.float32)
        if flat:
            streamed_maxima(b, steps_ref, docs_ref, q_ref, slot, max_ref, (flat[:RING], flat[RING:2 * RING]))
        else:
            plain_maxima(b, steps_ref, docs_ref, q_ref, slot, max_ref)
        sums = []
        for g in range(groups):
            total = max_ref[g, :, :128]
            for j in range(1, width // 128):
                total = total + max_ref[g, :, j * 128:(j + 1) * 128]
            sums.append(total)
        turned = jnp.concatenate(sums, axis=0).T
        high = turned.astype(place_ref.dtype)
        low = (turned - high.astype(jnp.float32)).astype(place_ref.dtype)
        halves = jnp.concatenate([high, low], axis=1)
        if flat:
            pltpu.matmul_push_rhs(place_ref[...], 0, 0)
            pltpu.matmul_acc_lhs(flat[-1], halves, load_staged_rhs=0)
            spread = pltpu.matmul_pop(flat[-1])[:, :ndoc]
        else:
            spread = jnp.dot(halves, place_ref[...], preferred_element_type=jnp.float32)[:, :ndoc]
        score = spread[:count]
        for j in range(1, 128 // count):
            score = score + spread[j * count:(j + 1) * count]
        score_ref[slot] = score

    @pl.when(begin < end)
    def _():
        fetch(begin)

    @pl.loop(begin, end)
    def _(n):
        slot = n % 2
        job, there = plan_ref[0, n] % JOBS, plan_ref[0, n] // JOBS

        @pl.when(n + 1 < end)
        def _():
            fetch(n + 1)

        pltpu.make_async_copy(sent[0].at[0], q_ref.at[slot], q_sem.at[slot]).wait()

        @pl.when(n >= begin + 2)
        def _():
            written(slot)

        for b in range(2):
            @pl.when(job % 2 == b)
            def _(b=b):
                run = functools.partial(scores, b, (own_docs, other_docs)[b], (own_place, other_place)[b], slot)
                if width % 512 == 0:
                    pl.run_scoped(
                        run,
                        *[pltpu.ACC(mxu_id=x)((SUB, 256), jnp.float32) for x in range(2) for _ in range(RING)],
                        pltpu.ACC(mxu_id=0)((128, 256), jnp.float32),
                    )
                else:
                    run()
                row = own_out.at[2 * there + core] if b == 0 else other_out.at[there]
                pltpu.make_async_copy(score_ref.at[slot], row, score_sem.at[slot]).start()

    for k in (2, 1):
        @pl.when(end >= begin + k)
        def _(k=k):
            written((end - k) % 2)


def score_jobs(plan, steps, packs, sent, outs, calls, cost):
    width_dim, width = sent[0].shape[1:]
    _, count, ndoc = outs[0].shape
    (own_docs, own_place), (other_docs, other_place) = packs
    fixed = 6 + len(sent)
    return pl.pallas_call(
        functools.partial(score_kernel, calls=calls),
        out_shape=[jax.ShapeDtypeStruct(o.shape, o.dtype) for o in outs],
        in_specs=[SMEM] * 2 + [VMEM] * 4 + [ANY] * len(sent) + [HBM] * 2,
        out_specs=[HBM] * 2,
        scratch_shapes=[
            pltpu.VMEM((ndoc // GROUP + 1, GROUP, width), jnp.float32),
            pltpu.VMEM((2, width_dim, width), sent[0].dtype),
            pltpu.VMEM((2, count, ndoc), jnp.float32),
            pltpu.SemaphoreType.DMA((2,)),
            pltpu.SemaphoreType.DMA((2,)),
        ],
        input_output_aliases={fixed: 0, fixed + 1: 1},
        compiler_params=pltpu.CompilerParams(vmem_limit_bytes=16 << 20),
        cost_estimate=cost,
        name="score_jobs",
    )(plan, steps, own_docs, other_docs, own_place, other_place, *sent, *outs)


def place_kernel(got_ref, _, out_ref, sem):
    core, _ = seat()
    copies = [pltpu.make_async_copy(got_ref.at[c], out_ref.at[2 * c + 1 - core], sem.at[c]) for c in range(got_ref.shape[0])]
    for copy in copies:
        copy.start()
    for copy in copies:
        copy.wait()


def place_scores(got, out):
    return pl.pallas_call(
        place_kernel,
        out_shape=jax.ShapeDtypeStruct(out.shape, out.dtype),
        in_specs=[ANY, HBM],
        out_specs=HBM,
        scratch_shapes=[pltpu.SemaphoreType.DMA((got.shape[0],))],
        input_output_aliases={1: 0},
        compiler_params=pltpu.CompilerParams(vmem_limit_bytes=4 << 20),
        cost_estimate=FREE,
        name="place_scores",
    )(got, out)


def xor_pairs(devices, even, odd):
    return [(i, ((i // 2) ^ (odd if i % 2 else even)) * 2 + i % 2) for i in range(devices)]


def after(array, *others):
    return lax.optimization_barrier((array, *others))[0]


def local(queries, documents, lengths, pattern):
    devices = lax.axis_size("docs")
    halves = lax.axis_size("pb")
    planes = devices // 8
    shard_rows = queries.shape[0]
    swap = [(i, i ^ 1) for i in range(devices)]

    if halves > 1:
        queries = lax.all_to_all(queries, "pb", split_axis=0, concat_axis=1, tiled=True)
    count = queries.shape[0]

    def send(array, even, odd=None):
        return lax.ppermute(array, "docs", xor_pairs(devices, even, even if odd is None else odd))

    def join(a, b):
        return jnp.concatenate([a, b], axis=0)

    unit = turn_queries(queries)
    crossed = {e: send(unit, 4 * e) for e in range(2, planes, 2)}

    def held(array):
        return pltpu.with_memory_space_constraint(array, pltpu.HBM)

    order = [(0, 0), (0, 1)]
    for z in range(2, planes, 2):
        order += [(z, 0), (z - 1, 0), (z, 1), (z - 1, 1)]
    if planes > 1:
        order += [(planes - 1, 0), (planes - 1, 1)]

    lengths = lengths.reshape(1, -1)
    *own_pack, own_steps, plan = pack_documents(held(documents), held(lengths), HBM, pattern, tuple(order), shard_rows, count)
    *other_pack, other_steps = pack_documents(
        lax.ppermute(documents, "docs", swap), lax.ppermute(lengths, "docs", swap), ANY)
    packs = (own_pack, other_pack)
    steps = jnp.concatenate([own_steps, other_steps], axis=0)

    sent, calls = [], []
    outs = [jnp.zeros((n, count, lengths.shape[1]), jnp.float32) for n in (devices, devices // 2)]

    def score(arrays, budget, busy=False):
        sent.extend(arrays)
        calls.append((len(sent), budget))
        outs[:] = score_jobs(plan, steps, packs, sent, outs, tuple(calls), BUSY if busy else FREE)

    def later(*arrays):
        *arrays, outs[1] = lax.optimization_barrier((*arrays, outs[1]))
        return arrays if len(arrays) > 1 else arrays[0]

    def spread(here):
        return join(here, send(here, 1, 2))

    def onward(near, z):
        return send(near, 4) if z + 1 < planes else None, send(near, 2, 1)

    near = join(unit, after(send(unit, 1, 2), own_steps))
    pair, far = onward(near, 0)
    if planes > 2:
        arrived = after(crossed[2], other_steps)
        upcoming = spread(arrived)
        near = after(near, arrived)
    score([near], 1, busy=True)
    score([later(far)], 1 if planes > 1 else None)
    waiting = None
    for z in range(2, planes, 2):
        near = later(upcoming)
        before, (pair, far) = pair, onward(near, z)
        before = after(later(before), near)
        before_far = send(before, 2, 1)
        score([near, before], 4)
        waiting = [far, before_far]
        if z + 2 < planes:
            upcoming = spread(later(crossed[z + 2]))
            score(later(*waiting), 2)
            waiting = []
    if pair is not None:
        pair = later(pair)
        pair_far = send(pair, 2, 1)
        score((later(*waiting) if waiting else []) + [pair], 3)
        score([later(pair_far)], None)
    own, other = outs
    return place_scores(lax.ppermute(other, "docs", swap), own)


def solution(mesh):
    mapped = jax.shard_map(
        local,
        mesh=mesh,
        in_specs=(P("docs", "pb", None), P("docs", None, None), P("docs"), P()),
        out_specs=P(None, "pb", "docs"),
        check_vma=False,
    )

    def run(*arrays):
        with jax.sharding.use_abstract_mesh(mesh.abstract_mesh):
            return mapped(*arrays)

    return run
```

```python
import functools

import jax
import jax.numpy as jnp
from jax import lax
from jax.experimental import pallas as pl
from jax.experimental.pallas import tpu as pltpu
from jax.sharding import PartitionSpec as P

BLOCK = 128
GROUP = 8
STEP = 8
SUB = GROUP * STEP
RING = 8
LAG = 7
PAD = 8
SIDE = 2
LOWEST = -3e38
JOBS = 256
VMEM = pl.BlockSpec(memory_space=pltpu.VMEM)
SMEM = pl.BlockSpec(memory_space=pltpu.SMEM)
ANY = pl.BlockSpec(memory_space=pl.ANY)
HBM = pl.BlockSpec(memory_space=pltpu.HBM)
FREE = pl.CostEstimate(flops=0, bytes_accessed=0, transcendentals=0)
BUSY = pl.CostEstimate(flops=16 << 30, bytes_accessed=0, transcendentals=0)


def query_kernel(q_ref, out_ref, rows_ref):
    count, tokens, _ = q_ref.shape
    pitch = rows_ref.shape[0] // count
    for i in range(count):
        rows_ref[i * pitch:i * pitch + tokens, :] = q_ref[i].astype(jnp.float32)
    span = 128 // count
    for j in range(tokens // span):
        parts = [rows_ref[pl.ds(j * span + t, count, stride=pitch), :] for t in range(span)]
        out_ref[0, :, j * 128:(j + 1) * 128] = jnp.concatenate(parts, axis=0).T.astype(out_ref.dtype)


def turn_queries(queries):
    count, tokens, width = queries.shape
    return pl.pallas_call(
        query_kernel,
        out_shape=jax.ShapeDtypeStruct((1, width, tokens * count), queries.dtype),
        in_specs=[VMEM],
        out_specs=VMEM,
        scratch_shapes=[pltpu.VMEM((count * (tokens + PAD), width), jnp.float32)],
        compiler_params=pltpu.CompilerParams(vmem_limit_bytes=4 << 20),
        cost_estimate=FREE,
        name="turn_queries",
    )(queries)


def sort_tables(length):
    ndoc = length.shape[1]
    square = (ndoc, ndoc)
    down = lax.broadcasted_iota(jnp.int32, square, 0)
    across = lax.broadcasted_iota(jnp.int32, square, 1)
    down_f, across_f = down.astype(jnp.float32), across.astype(jnp.float32)
    len_across = jnp.broadcast_to(length.astype(jnp.float32), square)
    len_down = len_across.T

    def count(hits, axis):
        return jnp.sum(jnp.where(hits, 1.0, 0.0), axis=axis, keepdims=True)

    ahead = (len_across > len_down) | ((len_across == len_down) & (across < down))
    behind = (len_down > len_across) | ((len_down == len_across) & (down < across))
    rank_down = count(ahead, 1)
    rank_across = count(behind, 0)
    placed = rank_across == down_f
    limit_down = jnp.sum(jnp.where(placed, len_across, 0.0), axis=1, keepdims=True)
    taken = rank_down == across_f
    order = jnp.sum(jnp.where(taken, down_f, 0.0), axis=0, keepdims=True)
    limit_across = jnp.sum(jnp.where(taken, len_down, 0.0), axis=0, keepdims=True)

    def steps_of(limit):
        return jnp.broadcast_to(((limit.astype(jnp.int32) + (STEP - 1)) // STEP).astype(jnp.float32), square)

    steps_down, steps_across = steps_of(limit_down), steps_of(limit_across)
    head_down, head_across = down % GROUP == 0, across % GROUP == 0
    starts = jnp.sum(jnp.where(head_down & (down < across * GROUP), steps_down, 0.0), axis=0, keepdims=True)
    ends = jnp.sum(jnp.where(head_across & (across <= down), steps_across, 0.0), axis=1, keepdims=True)
    group = count(head_down & (ends <= across_f), 0)
    total = jnp.sum(jnp.where(head_down, steps_down, 0.0), axis=0, keepdims=True).astype(jnp.int32)
    rounds = (total + (RING - 1)) // RING
    return order.astype(jnp.int32), starts.astype(jnp.int32), limit_down, group.astype(jnp.int32), rounds, placed


def seat():
    me = lax.axis_index("docs")
    return me % 2, me // 2


def plan_jobs(pattern_ref, plan_ref, order, shard_rows, count):
    core, chip = seat()
    shift = BLOCK.bit_length() - 1
    found = jnp.int32(0)
    for at, (z, past) in enumerate(order):
        plan_ref[1, at] = found
        for i in range(2):
            there = chip ^ (4 * z + jnp.where(core == 0, 2 * past + i, past + 2 * i))
            block = jnp.right_shift((2 * there + core) * shard_rows + lax.axis_index("pb") * count, shift)
            for b in range(2):
                plan_ref[0, found] = there * JOBS + 4 * at + 2 * i + b
                found = found + pattern_ref[block, 2 * chip + (core ^ b)]
    plan_ref[1, len(order)] = found


def document_kernel(docs_hbm, length_hbm, *refs, order, shard_rows, count):
    if order:
        pattern_ref, out_ref, place_ref, steps_ref, plan_ref, *scratch = refs
    else:
        out_ref, place_ref, steps_ref, *scratch = refs
    pack_block(docs_hbm, length_hbm, out_ref, place_ref, steps_ref, *scratch)
    if order:
        plan_jobs(pattern_ref, plan_ref, order, shard_rows, count)


def pack_block(docs_hbm, length_hbm, out_ref, place_ref, steps_ref,
                    docs_ref, rows_ref, limit_ref, length_ref, row_ref, table_ref, docs_sem, length_sem, sem):
    ndoc, slots, _ = docs_hbm.shape
    pitch = rows_ref.shape[1] // GROUP
    length_copy = pltpu.make_async_copy(length_hbm, length_ref, length_sem)
    docs_copy = pltpu.make_async_copy(docs_hbm, docs_ref, docs_sem)
    length_copy.start()
    docs_copy.start()
    length_copy.wait()
    sequence, starts, limit, group, rounds, placed = sort_tables(length_ref[...])
    row_ref[0:1, :] = sequence
    row_ref[1:2, :] = starts
    to_scalars = pltpu.make_async_copy(row_ref, table_ref, sem)
    to_scalars.start()
    limit_ref[...] = limit
    steps_ref[0:1, :] = group
    steps_ref[1:2, :] = rounds
    place = jnp.where(placed, 1.0, 0.0).astype(place_ref.dtype)
    place_ref[...] = jnp.concatenate([jnp.concatenate([place, place], axis=0)] * 2, axis=1)
    to_scalars.wait()
    docs_copy.wait()

    @pl.loop(0, ndoc // GROUP // SIDE)
    def _(turn):
        for side in range(SIDE):
            g = turn * SIDE + side
            for i in range(GROUP):
                doc = table_ref[0, g * GROUP + i]
                rows_ref[side, i * pitch:i * pitch + slots, :] = docs_ref[doc].astype(jnp.float32)
        for side in range(SIDE):
            g = turn * SIDE + side
            limit = limit_ref[pl.ds(pl.multiple_of(g * GROUP, GROUP), GROUP), :].astype(jnp.int32)
            first = rows_ref[side, pl.ds(0, GROUP, stride=pitch), :]
            base = table_ref[1, g] * SUB
            for s in range(0, slots, 2):
                pair = []
                for k in (s, s + 1):
                    tile = rows_ref[side, pl.ds(k, GROUP, stride=pitch), :]
                    pair.append(jnp.where(limit > k, tile, first))
                at = pl.multiple_of(base + s * GROUP, 2 * GROUP)
                out_ref[pl.ds(at, 2 * GROUP), :] = jnp.concatenate(pair, axis=0).astype(out_ref.dtype)


def pack_documents(documents, lengths, space, pattern=None, order=(), shard_rows=0, count=0):
    ndoc, slots, width = documents.shape
    out_shape = [
        jax.ShapeDtypeStruct((ndoc * slots, width), documents.dtype),
        jax.ShapeDtypeStruct((2 * ndoc, 2 * ndoc), documents.dtype),
        jax.ShapeDtypeStruct((2, ndoc), jnp.int32),
    ]
    planned = pattern is not None
    if planned:
        out_shape.append(jax.ShapeDtypeStruct((2, JOBS), jnp.int32))
    return pl.pallas_call(
        functools.partial(document_kernel, order=order, shard_rows=shard_rows, count=count),
        out_shape=out_shape,
        in_specs=[space, space] + [SMEM] * planned,
        out_specs=[VMEM, VMEM, VMEM] + [SMEM] * planned,
        scratch_shapes=[
            pltpu.VMEM((ndoc, slots, width), documents.dtype),
            pltpu.VMEM((SIDE, GROUP * (slots + PAD), width), jnp.float32),
            pltpu.VMEM((ndoc, 1), jnp.float32),
            pltpu.VMEM((1, ndoc), jnp.int32),
            pltpu.VMEM((8, ndoc), jnp.int32),
            pltpu.SMEM((8, ndoc), jnp.int32),
            pltpu.SemaphoreType.DMA,
            pltpu.SemaphoreType.DMA,
            pltpu.SemaphoreType.DMA,
        ],
        compiler_params=pltpu.CompilerParams(vmem_limit_bytes=16 << 20),
        cost_estimate=FREE,
        name="pack_documents",
    )(documents, lengths, *([pattern] if planned else []))


def fold(max_ref, step_group, at, best):
    span = slice(at, at + best.shape[1])
    max_ref[step_group, :, span] = jnp.maximum(max_ref[step_group, :, span], best)


def streamed_maxima(b, steps_ref, docs_ref, q_ref, u, max_ref, accs):
    width = q_ref.shape[2]
    rounds = steps_ref[2 * b + 1, 0]
    none_q = jnp.zeros((q_ref.shape[1], 256), q_ref.dtype)
    none_d = jnp.zeros((SUB, q_ref.shape[1]), q_ref.dtype)

    def feed(step, slot, staged):
        rows = docs_ref[pl.ds(pl.multiple_of(step * SUB, SUB), SUB), :]
        rows = jnp.concatenate([rows, none_d], axis=1)
        for unit in range(2):
            pltpu.matmul_acc_lhs(accs[unit][slot], rows, load_staged_rhs=staged)

    def retire(step, slot, pair):
        group = steps_ref[2 * b, step]
        for unit in range(2):
            got = pltpu.matmul_pop(accs[unit][slot])
            best = jnp.max(got.reshape(STEP, GROUP, 256), axis=0)
            fold(max_ref, group, (2 * pair + unit) * 256, best)

    for pair in range(width // 512):
        for unit in range(2):
            at = (2 * pair + unit) * 256
            pltpu.matmul_push_rhs(jnp.concatenate([q_ref[u, :, at:at + 256], none_q], axis=0), pair % 2, unit)
        for slot in range(RING):
            feed(slot, slot, pair % 2 if slot == 0 else None)
            if slot >= LAG:
                retire(slot - LAG, slot - LAG, pair)

        @pl.loop(1, rounds)
        def _(r, pair=pair):
            for slot in range(RING):
                step = r * RING + slot
                feed(step, slot, None)
                retire(step - LAG, (slot - LAG) % RING, pair)

        for k in range(RING - LAG, RING):
            retire((rounds - 1) * RING + k, k, pair)


def plain_maxima(b, steps_ref, docs_ref, q_ref, u, max_ref):
    @pl.loop(0, steps_ref[2 * b + 1, 0] * RING)
    def _(step):
        rows = docs_ref[pl.ds(pl.multiple_of(step * SUB, SUB), SUB), :]
        similar = jnp.dot(rows, q_ref[u], preferred_element_type=jnp.float32)
        fold(max_ref, steps_ref[2 * b, step], 0, jnp.max(similar.reshape(STEP, GROUP, similar.shape[1]), axis=0))


def score_kernel(plan_ref, steps_ref, own_docs, other_docs, own_place, other_place, *refs, calls):
    arrays = calls[-1][0]
    sent, refs = refs[:arrays], refs[arrays + 2:]
    own_out, other_out, max_ref, q_ref, score_ref, q_sem, score_sem = refs
    count, ndoc = score_ref.shape[1:]
    width = q_ref.shape[2]
    groups = ndoc // GROUP
    core, _ = seat()
    begin = end = jnp.int32(0)
    for arrived, budget in calls:
        begin, end = end, plan_ref[1, arrived]
        if budget is not None:
            end = jnp.minimum(begin + budget, end)

    def fetch(n):
        job = plan_ref[0, n] % JOBS
        for a in range(arrays):
            @pl.when(job // 4 == a)
            def _(a=a):
                pltpu.make_async_copy(sent[a].at[(job // 2) % 2], q_ref.at[n % 2], q_sem.at[n % 2]).start()

    def written(slot):
        pltpu.make_async_copy(score_ref.at[slot], other_out.at[0], score_sem.at[slot]).wait()

    def scores(b, docs_ref, place_ref, slot, *flat):
        max_ref[...] = jnp.full(max_ref.shape, LOWEST, jnp.float32)
        if flat:
            streamed_maxima(b, steps_ref, docs_ref, q_ref, slot, max_ref, (flat[:RING], flat[RING:2 * RING]))
        else:
            plain_maxima(b, steps_ref, docs_ref, q_ref, slot, max_ref)
        sums = []
        for g in range(groups):
            total = max_ref[g, :, :128]
            for j in range(1, width // 128):
                total = total + max_ref[g, :, j * 128:(j + 1) * 128]
            sums.append(total)
        turned = jnp.concatenate(sums, axis=0).T
        high = turned.astype(place_ref.dtype)
        low = (turned - high.astype(jnp.float32)).astype(place_ref.dtype)
        halves = jnp.concatenate([high, low], axis=1)
        if flat:
            pltpu.matmul_push_rhs(place_ref[...], 0, 0)
            pltpu.matmul_acc_lhs(flat[-1], halves, load_staged_rhs=0)
            spread = pltpu.matmul_pop(flat[-1])[:, :ndoc]
        else:
            spread = jnp.dot(halves, place_ref[...], preferred_element_type=jnp.float32)[:, :ndoc]
        score = spread[:count]
        for j in range(1, 128 // count):
            score = score + spread[j * count:(j + 1) * count]
        score_ref[slot] = score

    @pl.when(begin < end)
    def _():
        fetch(begin)

    @pl.loop(begin, end)
    def _(n):
        slot = n % 2
        job, there = plan_ref[0, n] % JOBS, plan_ref[0, n] // JOBS

        @pl.when(n + 1 < end)
        def _():
            fetch(n + 1)

        pltpu.make_async_copy(sent[0].at[0], q_ref.at[slot], q_sem.at[slot]).wait()

        @pl.when(n >= begin + 2)
        def _():
            written(slot)

        for b in range(2):
            @pl.when(job % 2 == b)
            def _(b=b):
                run = functools.partial(scores, b, (own_docs, other_docs)[b], (own_place, other_place)[b], slot)
                if width % 512 == 0:
                    pl.run_scoped(
                        run,
                        *[pltpu.ACC(mxu_id=x)((SUB, 256), jnp.float32) for x in range(2) for _ in range(RING)],
                        pltpu.ACC(mxu_id=0)((128, 256), jnp.float32),
                    )
                else:
                    run()
                row = own_out.at[2 * there + core] if b == 0 else other_out.at[there]
                pltpu.make_async_copy(score_ref.at[slot], row, score_sem.at[slot]).start()

    for k in (2, 1):
        @pl.when(end >= begin + k)
        def _(k=k):
            written((end - k) % 2)


def score_jobs(plan, steps, packs, sent, outs, calls, cost):
    width_dim, width = sent[0].shape[1:]
    _, count, ndoc = outs[0].shape
    (own_docs, own_place), (other_docs, other_place) = packs
    fixed = 6 + len(sent)
    return pl.pallas_call(
        functools.partial(score_kernel, calls=calls),
        out_shape=[jax.ShapeDtypeStruct(o.shape, o.dtype) for o in outs],
        in_specs=[SMEM] * 2 + [VMEM] * 4 + [ANY] * len(sent) + [HBM] * 2,
        out_specs=[HBM] * 2,
        scratch_shapes=[
            pltpu.VMEM((ndoc // GROUP + 1, GROUP, width), jnp.float32),
            pltpu.VMEM((2, width_dim, width), sent[0].dtype),
            pltpu.VMEM((2, count, ndoc), jnp.float32),
            pltpu.SemaphoreType.DMA((2,)),
            pltpu.SemaphoreType.DMA((2,)),
        ],
        input_output_aliases={fixed: 0, fixed + 1: 1},
        compiler_params=pltpu.CompilerParams(vmem_limit_bytes=16 << 20),
        cost_estimate=cost,
        name="score_jobs",
    )(plan, steps, own_docs, other_docs, own_place, other_place, *sent, *outs)


def place_kernel(got_ref, _, out_ref, sem):
    core, _ = seat()
    copies = [pltpu.make_async_copy(got_ref.at[c], out_ref.at[2 * c + 1 - core], sem.at[c]) for c in range(got_ref.shape[0])]
    for copy in copies:
        copy.start()
    for copy in copies:
        copy.wait()


def place_scores(got, out):
    return pl.pallas_call(
        place_kernel,
        out_shape=jax.ShapeDtypeStruct(out.shape, out.dtype),
        in_specs=[ANY, HBM],
        out_specs=HBM,
        scratch_shapes=[pltpu.SemaphoreType.DMA((got.shape[0],))],
        input_output_aliases={1: 0},
        compiler_params=pltpu.CompilerParams(vmem_limit_bytes=4 << 20),
        cost_estimate=FREE,
        name="place_scores",
    )(got, out)


def xor_pairs(devices, even, odd):
    return [(i, ((i // 2) ^ (odd if i % 2 else even)) * 2 + i % 2) for i in range(devices)]


def after(array, *others):
    return lax.optimization_barrier((array, *others))[0]


def local(queries, documents, lengths, pattern):
    devices = lax.axis_size("docs")
    halves = lax.axis_size("pb")
    planes = devices // 8
    shard_rows = queries.shape[0]
    swap = [(i, i ^ 1) for i in range(devices)]

    if halves > 1:
        queries = lax.all_to_all(queries, "pb", split_axis=0, concat_axis=1, tiled=True)
    count = queries.shape[0]

    def send(array, even, odd=None):
        return lax.ppermute(array, "docs", xor_pairs(devices, even, even if odd is None else odd))

    def join(a, b):
        return jnp.concatenate([a, b], axis=0)

    unit = turn_queries(queries)
    crossed = {z: send(unit, 4 * z) for z in range(1, planes) if z == 1 or z % 2 == 0}

    def held(array):
        return pltpu.with_memory_space_constraint(array, pltpu.HBM)

    order = [(0, 0), (0, 1)]
    for z in range(2, planes, 2):
        order += [(z - 1, 0), (z - 1, 1), (z, 0), (z, 1)]
    if planes > 1:
        order += [(planes - 1, 0), (planes - 1, 1)]

    lengths = lengths.reshape(1, -1)
    *own_pack, own_steps = pack_documents(held(documents), held(lengths), HBM)
    *other_pack, other_steps, plan = pack_documents(
        lax.ppermute(documents, "docs", swap), lax.ppermute(lengths, "docs", swap), ANY,
        pattern, tuple(order), shard_rows, count)
    packs = (own_pack, other_pack)
    steps = jnp.concatenate([own_steps, other_steps], axis=0)

    sent, calls = [], []
    outs = [jnp.zeros((n, count, lengths.shape[1]), jnp.float32) for n in (devices, devices // 2)]

    def score(arrays, budget, busy=False):
        sent.extend(arrays)
        calls.append((len(sent), budget))
        outs[:] = score_jobs(plan, steps, packs, sent, outs, tuple(calls), BUSY if busy else FREE)

    def later(*arrays):
        *arrays, outs[1] = lax.optimization_barrier((*arrays, outs[1]))
        return arrays if len(arrays) > 1 else arrays[0]

    def along(array):
        return send(array, 1, 2)

    def across(pair):
        return send(pair, 2, 1)

    beside = along(unit)
    beside, outs[0], outs[1], _ = lax.optimization_barrier((beside, *outs, own_steps))
    near = join(unit, beside)
    far = across(near)
    if planes == 1:
        score([near], 1)
        score([far], None)
    else:
        column = after(crossed[1], other_steps)
        beside = along(column)
        if planes > 2:
            ahead = after(crossed[2], column)
            beside_ahead, column_ahead = along(ahead), send(ahead, 4)
            near = after(near, ahead)
        score([near], 1, busy=True)
        fars = [later(far)]
        for z in range(2, planes, 2):
            near = join(column, later(beside))
            far = across(near)
            score(fars + [near], 2)
            near_ahead = join(ahead, later(beside_ahead))
            far_ahead = across(near_ahead)
            column, far, fars = later(column_ahead), later(far), [far_ahead]
            beside = along(column)
            score([far, near_ahead], 2)
            if z + 2 < planes:
                ahead = later(crossed[z + 2])
                beside_ahead, column_ahead = along(ahead), send(ahead, 4)
        near = join(column, later(beside))
        far = across(near)
        score(fars + [near], 3)
        score([later(far)], None)
    own, other = outs
    return place_scores(lax.ppermute(other, "docs", swap), own)


def solution(mesh):
    mapped = jax.shard_map(
        local,
        mesh=mesh,
        in_specs=(P("docs", "pb", None), P("docs", None, None), P("docs"), P()),
        out_specs=P(None, "pb", "docs"),
        check_vma=False,
    )

    def run(*arrays):
        with jax.sharding.use_abstract_mesh(mesh.abstract_mesh):
            return mapped(*arrays)

    return run
```

```python
import functools

import jax
import jax.numpy as jnp
from jax import lax
from jax.experimental import pallas as pl
from jax.experimental.pallas import tpu as pltpu
from jax.sharding import PartitionSpec as P

BLOCK = 128
GROUP = 8
STEP = 8
SUB = GROUP * STEP
RING = 8
LAG = 7
PAD = 8
SIDE = 2
LOWEST = -3e38
JOBS = 256
VMEM = pl.BlockSpec(memory_space=pltpu.VMEM)
SMEM = pl.BlockSpec(memory_space=pltpu.SMEM)
ANY = pl.BlockSpec(memory_space=pl.ANY)
HBM = pl.BlockSpec(memory_space=pltpu.HBM)
FREE = pl.CostEstimate(flops=0, bytes_accessed=0, transcendentals=0)
BUSY = pl.CostEstimate(flops=16 << 30, bytes_accessed=0, transcendentals=0)


def query_kernel(q_ref, out_ref, rows_ref):
    count, tokens, _ = q_ref.shape
    pitch = rows_ref.shape[0] // count
    for i in range(count):
        rows_ref[i * pitch:i * pitch + tokens, :] = q_ref[i].astype(jnp.float32)
    span = 128 // count
    for j in range(tokens // span):
        parts = [rows_ref[pl.ds(j * span + t, count, stride=pitch), :] for t in range(span)]
        out_ref[0, :, j * 128:(j + 1) * 128] = jnp.concatenate(parts, axis=0).T.astype(out_ref.dtype)


def turn_queries(queries):
    count, tokens, width = queries.shape
    return pl.pallas_call(
        query_kernel,
        out_shape=jax.ShapeDtypeStruct((1, width, tokens * count), queries.dtype),
        in_specs=[VMEM],
        out_specs=VMEM,
        scratch_shapes=[pltpu.VMEM((count * (tokens + PAD), width), jnp.float32)],
        compiler_params=pltpu.CompilerParams(vmem_limit_bytes=4 << 20),
        cost_estimate=FREE,
        name="turn_queries",
    )(queries)


def sort_tables(length, parts):
    ndoc = length.shape[1]
    square = (ndoc, ndoc)
    down = lax.broadcasted_iota(jnp.int32, square, 0)
    across = lax.broadcasted_iota(jnp.int32, square, 1)
    down_f, across_f = down.astype(jnp.float32), across.astype(jnp.float32)
    len_across = jnp.broadcast_to(length.astype(jnp.float32), square)
    len_down = len_across.T

    def count(hits, axis):
        return jnp.sum(jnp.where(hits, 1.0, 0.0), axis=axis, keepdims=True)

    ahead = (len_across > len_down) | ((len_across == len_down) & (across < down))
    behind = (len_down > len_across) | ((len_down == len_across) & (down < across))
    rank_down = count(ahead, 1)
    rank_across = count(behind, 0)
    placed = rank_across == down_f
    limit_down = jnp.sum(jnp.where(placed, len_across, 0.0), axis=1, keepdims=True)
    taken = rank_down == across_f
    order = jnp.sum(jnp.where(taken, down_f, 0.0), axis=0, keepdims=True)
    limit_across = jnp.sum(jnp.where(taken, len_down, 0.0), axis=0, keepdims=True)

    def steps_of(limit):
        return jnp.broadcast_to(((limit.astype(jnp.int32) + (STEP - 1)) // STEP).astype(jnp.float32), square)

    steps_down, steps_across = steps_of(limit_down), steps_of(limit_across)
    head_down, head_across = down % GROUP == 0, across % GROUP == 0
    starts = jnp.sum(jnp.where(head_down & (down < across * GROUP), steps_down, 0.0), axis=0, keepdims=True)
    ends = jnp.sum(jnp.where(head_across & (across <= down), steps_across, 0.0), axis=1, keepdims=True)
    group = jnp.concatenate([count(head_down & (ends <= across_f + part * ndoc), 0) for part in range(parts)], axis=1)
    total = jnp.sum(jnp.where(head_down, steps_down, 0.0), axis=0, keepdims=True).astype(jnp.int32)
    rounds = (total + (RING - 1)) // RING
    return order.astype(jnp.int32), starts.astype(jnp.int32), limit_down, group.astype(jnp.int32), rounds, rank_across.astype(jnp.int32)


def seat():
    me = lax.axis_index("docs")
    return me % 2, me // 2


def plan_jobs(pattern_ref, plan_ref, order, shard_rows, count):
    core, chip = seat()
    shift = BLOCK.bit_length() - 1
    found = jnp.int32(0)
    for at, (z, past) in enumerate(order):
        plan_ref[1, at] = found
        for i in range(2):
            there = chip ^ (4 * z + jnp.where(core == 0, 2 * past + i, past + 2 * i))
            block = jnp.right_shift((2 * there + core) * shard_rows + lax.axis_index("pb") * count, shift)
            for b in range(2):
                plan_ref[0, found] = there * JOBS + 4 * at + 2 * i + b
                found = found + pattern_ref[block, 2 * chip + (core ^ b)]
    plan_ref[1, len(order)] = found


def document_kernel(docs_hbm, length_hbm, *refs, order, shard_rows, count):
    if order:
        pattern_ref, out_ref, rank_ref, steps_ref, plan_ref, *scratch = refs
    else:
        out_ref, rank_ref, steps_ref, *scratch = refs
    pack_block(docs_hbm, length_hbm, out_ref, rank_ref, steps_ref, *scratch)
    if order:
        plan_jobs(pattern_ref, plan_ref, order, shard_rows, count)


def pack_block(docs_hbm, length_hbm, out_ref, rank_ref, steps_ref,
                    docs_ref, rows_ref, limit_ref, length_ref, row_ref, table_ref, docs_sem, length_sem, sem):
    ndoc, slots, _ = docs_hbm.shape
    pitch = rows_ref.shape[1] // GROUP
    length_copy = pltpu.make_async_copy(length_hbm, length_ref, length_sem)
    docs_copy = pltpu.make_async_copy(docs_hbm, docs_ref, docs_sem)
    length_copy.start()
    docs_copy.start()
    length_copy.wait()
    sequence, starts, limit, group, rounds, rank = sort_tables(length_ref[...], steps_ref.shape[1] // ndoc)
    row_ref[0:1, :] = sequence
    row_ref[1:2, :] = starts
    to_scalars = pltpu.make_async_copy(row_ref, table_ref, sem)
    to_scalars.start()
    limit_ref[...] = limit
    steps_ref[0:1, :] = group
    steps_ref[1:2, :] = jnp.concatenate([rounds] * (steps_ref.shape[1] // ndoc), axis=1)
    rank_ref[...] = rank
    to_scalars.wait()
    docs_copy.wait()

    @pl.loop(0, ndoc // GROUP // SIDE)
    def _(turn):
        for side in range(SIDE):
            g = turn * SIDE + side
            for i in range(GROUP):
                doc = table_ref[0, g * GROUP + i]
                rows_ref[side, i * pitch:i * pitch + slots, :] = docs_ref[doc].astype(jnp.float32)
        for side in range(SIDE):
            g = turn * SIDE + side
            limit = limit_ref[pl.ds(pl.multiple_of(g * GROUP, GROUP), GROUP), :].astype(jnp.int32)
            first = rows_ref[side, pl.ds(0, GROUP, stride=pitch), :]
            base = table_ref[1, g] * SUB
            for s in range(0, slots, 2):
                pair = []
                for k in (s, s + 1):
                    tile = rows_ref[side, pl.ds(k, GROUP, stride=pitch), :]
                    pair.append(jnp.where(limit > k, tile, first))
                at = pl.multiple_of(base + s * GROUP, 2 * GROUP)
                out_ref[pl.ds(at, 2 * GROUP), :] = jnp.concatenate(pair, axis=0).astype(out_ref.dtype)


def pack_documents(documents, lengths, space, pattern=None, order=(), shard_rows=0, count=0):
    ndoc, slots, width = documents.shape
    out_shape = [
        jax.ShapeDtypeStruct((ndoc * slots, width), documents.dtype),
        jax.ShapeDtypeStruct((1, ndoc), jnp.int32),
        jax.ShapeDtypeStruct((2, ndoc // GROUP * slots // STEP), jnp.int32),
    ]
    planned = pattern is not None
    if planned:
        out_shape.append(jax.ShapeDtypeStruct((2, JOBS), jnp.int32))
    return pl.pallas_call(
        functools.partial(document_kernel, order=order, shard_rows=shard_rows, count=count),
        out_shape=out_shape,
        in_specs=[space, space] + [SMEM] * planned,
        out_specs=[VMEM, VMEM, VMEM] + [SMEM] * planned,
        scratch_shapes=[
            pltpu.VMEM((ndoc, slots, width), documents.dtype),
            pltpu.VMEM((SIDE, GROUP * (slots + PAD), width), jnp.float32),
            pltpu.VMEM((ndoc, 1), jnp.float32),
            pltpu.VMEM((1, ndoc), jnp.int32),
            pltpu.VMEM((8, ndoc), jnp.int32),
            pltpu.SMEM((8, ndoc), jnp.int32),
            pltpu.SemaphoreType.DMA,
            pltpu.SemaphoreType.DMA,
            pltpu.SemaphoreType.DMA,
        ],
        compiler_params=pltpu.CompilerParams(vmem_limit_bytes=16 << 20),
        cost_estimate=FREE,
        name="pack_documents",
    )(documents, lengths, *([pattern] if planned else []))


def fold(max_ref, step_group, at, best):
    span = slice(at, at + best.shape[1])
    max_ref[step_group, :, span] = jnp.maximum(max_ref[step_group, :, span], best)


def streamed_maxima(b, steps_ref, docs_ref, q_ref, u, max_ref, accs):
    width = q_ref.shape[2]
    rounds = steps_ref[2 * b + 1, 0]
    none_q = jnp.zeros((q_ref.shape[1], 256), q_ref.dtype)
    none_d = jnp.zeros((SUB, q_ref.shape[1]), q_ref.dtype)

    def feed(step, slot, staged):
        rows = docs_ref[pl.ds(pl.multiple_of(step * SUB, SUB), SUB), :]
        rows = jnp.concatenate([rows, none_d], axis=1)
        for unit in range(2):
            pltpu.matmul_acc_lhs(accs[unit][slot], rows, load_staged_rhs=staged)

    def retire(step, slot, pair):
        group = steps_ref[2 * b, step]
        for unit in range(2):
            got = pltpu.matmul_pop(accs[unit][slot])
            best = jnp.max(got.reshape(STEP, GROUP, 256), axis=0)
            fold(max_ref, group, (2 * pair + unit) * 256, best)

    for pair in range(width // 512):
        for unit in range(2):
            at = (2 * pair + unit) * 256
            pltpu.matmul_push_rhs(jnp.concatenate([q_ref[u, :, at:at + 256], none_q], axis=0), pair % 2, unit)
        for slot in range(RING):
            feed(slot, slot, pair % 2 if slot == 0 else None)
            if slot >= LAG:
                retire(slot - LAG, slot - LAG, pair)

        @pl.loop(1, rounds)
        def _(r, pair=pair):
            for slot in range(RING):
                step = r * RING + slot
                feed(step, slot, None)
                retire(step - LAG, (slot - LAG) % RING, pair)

        for k in range(RING - LAG, RING):
            retire((rounds - 1) * RING + k, k, pair)


def plain_maxima(b, steps_ref, docs_ref, q_ref, u, max_ref):
    @pl.loop(0, steps_ref[2 * b + 1, 0] * RING)
    def _(step):
        rows = docs_ref[pl.ds(pl.multiple_of(step * SUB, SUB), SUB), :]
        similar = jnp.dot(rows, q_ref[u], preferred_element_type=jnp.float32)
        fold(max_ref, steps_ref[2 * b, step], 0, jnp.max(similar.reshape(STEP, GROUP, similar.shape[1]), axis=0))


def score_kernel(plan_ref, steps_ref, own_docs, other_docs, own_rank, other_rank, *refs, calls):
    arrays = calls[-1][0]
    sent, refs = refs[:arrays], refs[arrays + 2:]
    own_out, other_out, max_ref, q_ref, score_ref, q_sem, score_sem = refs
    count, ndoc = score_ref.shape[1:]
    width = q_ref.shape[2]
    groups = ndoc // GROUP
    core, _ = seat()
    begin = end = jnp.int32(0)
    for arrived, budget in calls:
        begin, end = end, plan_ref[1, arrived]
        if budget is not None:
            end = jnp.minimum(begin + budget, end)

    def fetch(n):
        job = plan_ref[0, n] % JOBS
        for a in range(arrays):
            @pl.when(job // 4 == a)
            def _(a=a):
                pltpu.make_async_copy(sent[a].at[(job // 2) % 2], q_ref.at[n % 2], q_sem.at[n % 2]).start()

    def written(slot):
        pltpu.make_async_copy(score_ref.at[slot], other_out.at[0], score_sem.at[slot]).wait()

    def scores(b, docs_ref, rank_ref, slot, *flat):
        max_ref[...] = jnp.full(max_ref.shape, LOWEST, jnp.float32)
        if flat:
            streamed_maxima(b, steps_ref, docs_ref, q_ref, slot, max_ref, (flat[:RING], flat[RING:2 * RING]))
        else:
            plain_maxima(b, steps_ref, docs_ref, q_ref, slot, max_ref)
        sums = []
        for g in range(groups):
            total = max_ref[g, :, :128]
            for j in range(1, width // 128):
                total = total + max_ref[g, :, j * 128:(j + 1) * 128]
            sums.append(total)
        turned = jnp.concatenate(sums, axis=0).T
        score = turned[:count]
        for j in range(1, 128 // count):
            score = score + turned[j * count:(j + 1) * count]
        score = jnp.take_along_axis(score, jnp.broadcast_to(rank_ref[...], score.shape), axis=1)
        score_ref[slot] = score

    @pl.when(begin < end)
    def _():
        fetch(begin)

    @pl.loop(begin, end)
    def _(n):
        slot = n % 2
        job, there = plan_ref[0, n] % JOBS, plan_ref[0, n] // JOBS

        @pl.when(n + 1 < end)
        def _():
            fetch(n + 1)

        pltpu.make_async_copy(sent[0].at[0], q_ref.at[slot], q_sem.at[slot]).wait()

        @pl.when(n >= begin + 2)
        def _():
            written(slot)

        for b in range(2):
            @pl.when(job % 2 == b)
            def _(b=b):
                run = functools.partial(scores, b, (own_docs, other_docs)[b], (own_rank, other_rank)[b], slot)
                if width % 512 == 0:
                    pl.run_scoped(
                        run,
                        *[pltpu.ACC(mxu_id=x)((SUB, 256), jnp.float32) for x in range(2) for _ in range(RING)],
                    )
                else:
                    run()
                row = own_out.at[2 * there + core] if b == 0 else other_out.at[there]
                pltpu.make_async_copy(score_ref.at[slot], row, score_sem.at[slot]).start()

    for k in (2, 1):
        @pl.when(end >= begin + k)
        def _(k=k):
            written((end - k) % 2)


def score_jobs(plan, steps, packs, sent, outs, calls, cost):
    width_dim, width = sent[0].shape[1:]
    _, count, ndoc = outs[0].shape
    (own_docs, own_rank), (other_docs, other_rank) = packs
    fixed = 6 + len(sent)
    return pl.pallas_call(
        functools.partial(score_kernel, calls=calls),
        out_shape=[jax.ShapeDtypeStruct(o.shape, o.dtype) for o in outs],
        in_specs=[SMEM] * 2 + [VMEM] * 4 + [ANY] * len(sent) + [HBM] * 2,
        out_specs=[HBM] * 2,
        scratch_shapes=[
            pltpu.VMEM((ndoc // GROUP + 1, GROUP, width), jnp.float32),
            pltpu.VMEM((2, width_dim, width), sent[0].dtype),
            pltpu.VMEM((2, count, ndoc), jnp.float32),
            pltpu.SemaphoreType.DMA((2,)),
            pltpu.SemaphoreType.DMA((2,)),
        ],
        input_output_aliases={fixed: 0, fixed + 1: 1},
        compiler_params=pltpu.CompilerParams(vmem_limit_bytes=16 << 20),
        cost_estimate=cost,
        name="score_jobs",
    )(plan, steps, own_docs, other_docs, own_rank, other_rank, *sent, *outs)


def place_kernel(got_ref, _, out_ref, sem):
    core, _ = seat()
    copies = [pltpu.make_async_copy(got_ref.at[c], out_ref.at[2 * c + 1 - core], sem.at[c]) for c in range(got_ref.shape[0])]
    for copy in copies:
        copy.start()
    for copy in copies:
        copy.wait()


def place_scores(got, out):
    return pl.pallas_call(
        place_kernel,
        out_shape=jax.ShapeDtypeStruct(out.shape, out.dtype),
        in_specs=[ANY, HBM],
        out_specs=HBM,
        scratch_shapes=[pltpu.SemaphoreType.DMA((got.shape[0],))],
        input_output_aliases={1: 0},
        compiler_params=pltpu.CompilerParams(vmem_limit_bytes=4 << 20),
        cost_estimate=FREE,
        name="place_scores",
    )(got, out)


def xor_pairs(devices, even, odd):
    return [(i, ((i // 2) ^ (odd if i % 2 else even)) * 2 + i % 2) for i in range(devices)]


def after(array, *others):
    return lax.optimization_barrier((array, *others))[0]


def local(queries, documents, lengths, pattern):
    devices = lax.axis_size("docs")
    halves = lax.axis_size("pb")
    planes = devices // 8
    shard_rows = queries.shape[0]
    swap = [(i, i ^ 1) for i in range(devices)]

    if halves > 1:
        queries = lax.all_to_all(queries, "pb", split_axis=0, concat_axis=1, tiled=True)
    count = queries.shape[0]

    def send(array, even, odd=None):
        return lax.ppermute(array, "docs", xor_pairs(devices, even, even if odd is None else odd))

    def join(a, b):
        return jnp.concatenate([a, b], axis=0)

    unit = turn_queries(queries)
    crossed = {e: send(unit, 4 * e) for e in range(2, planes, 2)}

    def held(array):
        return pltpu.with_memory_space_constraint(array, pltpu.HBM)

    order = [(0, 0), (0, 1)]
    for z in range(2, planes, 2):
        order += [(z, 0), (z - 1, 0), (z, 1), (z - 1, 1)]
    if planes > 1:
        order += [(planes - 1, 0), (planes - 1, 1)]

    lengths = lengths.reshape(1, -1)
    *own_pack, own_steps = pack_documents(held(documents), held(lengths), HBM)
    *other_pack, other_steps, plan = pack_documents(
        lax.ppermute(documents, "docs", swap), lax.ppermute(lengths, "docs", swap), ANY,
        pattern, tuple(order), shard_rows, count)
    packs = (own_pack, other_pack)
    steps = jnp.concatenate([own_steps, other_steps], axis=0)

    sent, calls = [], []
    outs = [jnp.zeros((n, count, lengths.shape[1]), jnp.float32) for n in (devices, devices // 2)]

    def score(arrays, budget, busy=False):
        sent.extend(arrays)
        calls.append((len(sent), budget))
        outs[:] = score_jobs(plan, steps, packs, sent, outs, tuple(calls), BUSY if busy else FREE)

    def later(*arrays):
        *arrays, outs[1] = lax.optimization_barrier((*arrays, outs[1]))
        return arrays if len(arrays) > 1 else arrays[0]

    def spread(here):
        return join(here, send(here, 1, 2))

    def onward(near, z):
        return send(near, 4) if z + 1 < planes else None, send(near, 2, 1)

    beside = send(unit, 1, 2)
    beside, outs[0], outs[1], _ = lax.optimization_barrier((beside, *outs, own_steps))
    near = join(unit, beside)
    pair, far = onward(near, 0)
    if planes > 2:
        score([near], 1)
        upcoming = spread(later(crossed[2]))
        score([], 1, busy=True)
        ready = [later(far)]
    else:
        score([near], 1)
        score([later(far)], 1 if planes > 1 else None)
        ready = []
    waiting = None
    for z in range(2, planes, 2):
        near = later(upcoming)
        before, (pair, far) = pair, onward(near, z)
        before = after(later(before), near)
        before_far = send(before, 2, 1)
        score(ready + [near, before], 4)
        ready = []
        waiting = [far, before_far]
        if z + 2 < planes:
            upcoming = spread(later(crossed[z + 2]))
            score(later(*waiting), 2)
            waiting = []
    if pair is not None:
        pair = later(pair)
        pair_far = send(pair, 2, 1)
        score((later(*waiting) if waiting else []) + [pair], 4)
        score([later(pair_far)], None)
    own, other = outs
    return place_scores(lax.ppermute(other, "docs", swap), own)


def solution(mesh):
    mapped = jax.shard_map(
        local,
        mesh=mesh,
        in_specs=(P("docs", "pb", None), P("docs", None, None), P("docs"), P()),
        out_specs=P(None, "pb", "docs"),
        check_vma=False,
    )

    def run(*arrays):
        with jax.sharding.use_abstract_mesh(mesh.abstract_mesh):
            return mapped(*arrays)

    return run
```

```python
import functools

import jax
import jax.numpy as jnp
from jax import lax
from jax.experimental import pallas as pl
from jax.experimental.pallas import tpu as pltpu
from jax.sharding import PartitionSpec as P

BLOCK = 128
GROUP = 8
STEP = 8
SUB = GROUP * STEP
RING = 8
LAG = 7
PAD = 8
SIDE = 2
LOWEST = -3e38
JOBS = 256
VMEM = pl.BlockSpec(memory_space=pltpu.VMEM)
SMEM = pl.BlockSpec(memory_space=pltpu.SMEM)
ANY = pl.BlockSpec(memory_space=pl.ANY)
HBM = pl.BlockSpec(memory_space=pltpu.HBM)
FREE = pl.CostEstimate(flops=0, bytes_accessed=0, transcendentals=0)
BUSY = pl.CostEstimate(flops=16 << 30, bytes_accessed=0, transcendentals=0)


def query_kernel(q_ref, out_ref, rows_ref):
    count, tokens, _ = q_ref.shape
    pitch = rows_ref.shape[0] // count
    for i in range(count):
        rows_ref[i * pitch:i * pitch + tokens, :] = q_ref[i].astype(jnp.float32)
    span = 128 // count
    for j in range(tokens // span):
        parts = [rows_ref[pl.ds(j * span + t, count, stride=pitch), :] for t in range(span)]
        out_ref[0, :, j * 128:(j + 1) * 128] = jnp.concatenate(parts, axis=0).T.astype(out_ref.dtype)


def turn_queries(queries):
    count, tokens, width = queries.shape
    return pl.pallas_call(
        query_kernel,
        out_shape=jax.ShapeDtypeStruct((1, width, tokens * count), queries.dtype),
        in_specs=[VMEM],
        out_specs=VMEM,
        scratch_shapes=[pltpu.VMEM((count * (tokens + PAD), width), jnp.float32)],
        compiler_params=pltpu.CompilerParams(vmem_limit_bytes=4 << 20),
        cost_estimate=FREE,
        name="turn_queries",
    )(queries)


def sort_tables(length, parts):
    ndoc = length.shape[1]
    square = (ndoc, ndoc)
    down = lax.broadcasted_iota(jnp.int32, square, 0)
    across = lax.broadcasted_iota(jnp.int32, square, 1)
    down_f, across_f = down.astype(jnp.float32), across.astype(jnp.float32)
    len_across = jnp.broadcast_to(length.astype(jnp.float32), square)
    len_down = len_across.T

    def count(hits, axis):
        return jnp.sum(jnp.where(hits, 1.0, 0.0), axis=axis, keepdims=True)

    ahead = (len_across > len_down) | ((len_across == len_down) & (across < down))
    behind = (len_down > len_across) | ((len_down == len_across) & (down < across))
    rank_down = count(ahead, 1)
    rank_across = count(behind, 0)
    placed = rank_across == down_f
    limit_down = jnp.sum(jnp.where(placed, len_across, 0.0), axis=1, keepdims=True)
    taken = rank_down == across_f
    order = jnp.sum(jnp.where(taken, down_f, 0.0), axis=0, keepdims=True)
    limit_across = jnp.sum(jnp.where(taken, len_down, 0.0), axis=0, keepdims=True)

    def steps_of(limit):
        return jnp.broadcast_to(((limit.astype(jnp.int32) + (STEP - 1)) // STEP).astype(jnp.float32), square)

    steps_down, steps_across = steps_of(limit_down), steps_of(limit_across)
    head_down, head_across = down % GROUP == 0, across % GROUP == 0
    starts = jnp.sum(jnp.where(head_down & (down < across * GROUP), steps_down, 0.0), axis=0, keepdims=True)
    ends = jnp.sum(jnp.where(head_across & (across <= down), steps_across, 0.0), axis=1, keepdims=True)
    group = jnp.concatenate([count(head_down & (ends <= across_f + part * ndoc), 0) for part in range(parts)], axis=1)
    total = jnp.sum(jnp.where(head_down, steps_down, 0.0), axis=0, keepdims=True).astype(jnp.int32)
    rounds = (total + (RING - 1)) // RING
    return order.astype(jnp.int32), starts.astype(jnp.int32), limit_down, group.astype(jnp.int32), rounds, rank_across.astype(jnp.int32)


def seat():
    me = lax.axis_index("docs")
    return me % 2, me // 2


def plan_jobs(pattern_ref, plan_ref, order, shard_rows, count):
    core, chip = seat()
    blocks, columns = pattern_ref.shape
    wide = plan_ref.shape[1]
    job = lax.broadcasted_iota(jnp.int32, (1, wide), 1)
    at, i, b = job >> 2, (job >> 1) & 1, job & 1
    plane = sum(jnp.where(at == k, z, 0) for k, (z, _) in enumerate(order))
    past = sum(jnp.where(at == k, p, 0) for k, (_, p) in enumerate(order))
    there = chip ^ (4 * plane + jnp.where(core == 0, 2 * past + i, past + 2 * i))
    first = (2 * there + core) * shard_rows + lax.axis_index("pb") * count
    block = jnp.right_shift(first, BLOCK.bit_length() - 1)

    column = lax.broadcasted_iota(jnp.int32, (blocks, columns), 1)
    wanted = jnp.where(pattern_ref[...] > 0, 1.0, 0.0)
    own, other = [jnp.sum(jnp.where(column == 2 * chip + (core ^ k), wanted, 0.0), axis=1, keepdims=True) for k in range(2)]
    hit = lax.broadcasted_iota(jnp.int32, (blocks, wide), 0) == block
    active = jnp.sum(jnp.where(hit, jnp.where(b == 0, own, other), 0.0), axis=0, keepdims=True)
    active = jnp.where(job < 4 * len(order), active, 0.0)

    square = (wide, wide)
    down = lax.broadcasted_iota(jnp.int32, square, 0)
    across = lax.broadcasted_iota(jnp.int32, square, 1)
    active_across = jnp.broadcast_to(active, square)
    active_down = active_across.T
    name_down = jnp.broadcast_to((there * JOBS + job).astype(jnp.float32), square).T
    before_down = jnp.sum(jnp.where(across < down, active_across, 0.0), axis=1, keepdims=True)
    chosen = (active_down > 0) & (before_down == across.astype(jnp.float32))
    names = jnp.sum(jnp.where(chosen, name_down, 0.0), axis=0, keepdims=True)
    counts = jnp.sum(jnp.where(down < 4 * across, active_down, 0.0), axis=0, keepdims=True)
    plan_ref[...] = jnp.concatenate([names, counts], axis=0).astype(jnp.int32)


def document_kernel(docs_hbm, length_hbm, *refs, order, shard_rows, count):
    if order:
        pattern_ref, out_ref, rank_ref, steps_ref, plan_ref, *scratch = refs
    else:
        out_ref, rank_ref, steps_ref, *scratch = refs
    pack_block(docs_hbm, length_hbm, out_ref, rank_ref, steps_ref, *scratch)
    if order:
        plan_jobs(pattern_ref, plan_ref, order, shard_rows, count)


def pack_block(docs_hbm, length_hbm, out_ref, rank_ref, steps_ref,
                    docs_ref, rows_ref, limit_ref, length_ref, row_ref, table_ref, docs_sem, length_sem, sem):
    ndoc, slots, _ = docs_hbm.shape
    pitch = rows_ref.shape[1] // GROUP
    length_copy = pltpu.make_async_copy(length_hbm, length_ref, length_sem)
    docs_copy = pltpu.make_async_copy(docs_hbm, docs_ref, docs_sem)
    length_copy.start()
    docs_copy.start()
    length_copy.wait()
    sequence, starts, limit, group, rounds, rank = sort_tables(length_ref[...], steps_ref.shape[1] // ndoc)
    row_ref[0:1, :] = sequence
    row_ref[1:2, :] = starts
    to_scalars = pltpu.make_async_copy(row_ref, table_ref, sem)
    to_scalars.start()
    limit_ref[...] = limit
    steps_ref[0:1, :] = group
    steps_ref[1:2, :] = jnp.concatenate([rounds] * (steps_ref.shape[1] // ndoc), axis=1)
    rank_ref[...] = rank
    to_scalars.wait()
    docs_copy.wait()

    @pl.loop(0, ndoc // GROUP // SIDE)
    def _(turn):
        for side in range(SIDE):
            g = turn * SIDE + side
            for i in range(GROUP):
                doc = table_ref[0, g * GROUP + i]
                rows_ref[side, i * pitch:i * pitch + slots, :] = docs_ref[doc].astype(jnp.float32)
        for side in range(SIDE):
            g = turn * SIDE + side
            limit = limit_ref[pl.ds(pl.multiple_of(g * GROUP, GROUP), GROUP), :].astype(jnp.int32)
            first = rows_ref[side, pl.ds(0, GROUP, stride=pitch), :]
            base = table_ref[1, g] * SUB
            for s in range(0, slots, 2):
                pair = []
                for k in (s, s + 1):
                    tile = rows_ref[side, pl.ds(k, GROUP, stride=pitch), :]
                    pair.append(jnp.where(limit > k, tile, first))
                at = pl.multiple_of(base + s * GROUP, 2 * GROUP)
                out_ref[pl.ds(at, 2 * GROUP), :] = jnp.concatenate(pair, axis=0).astype(out_ref.dtype)


def pack_documents(documents, lengths, space, pattern=None, order=(), shard_rows=0, count=0):
    ndoc, slots, width = documents.shape
    out_shape = [
        jax.ShapeDtypeStruct((ndoc * slots, width), documents.dtype),
        jax.ShapeDtypeStruct((1, ndoc), jnp.int32),
        jax.ShapeDtypeStruct((2, ndoc // GROUP * slots // STEP), jnp.int32),
    ]
    planned = pattern is not None
    if planned:
        out_shape.append(jax.ShapeDtypeStruct((2, ndoc), jnp.int32))
    return pl.pallas_call(
        functools.partial(document_kernel, order=order, shard_rows=shard_rows, count=count),
        out_shape=out_shape,
        in_specs=[space, space] + [VMEM] * planned,
        out_specs=[VMEM, VMEM, VMEM] + [VMEM] * planned,
        scratch_shapes=[
            pltpu.VMEM((ndoc, slots, width), documents.dtype),
            pltpu.VMEM((SIDE, GROUP * (slots + PAD), width), jnp.float32),
            pltpu.VMEM((ndoc, 1), jnp.float32),
            pltpu.VMEM((1, ndoc), jnp.int32),
            pltpu.VMEM((8, ndoc), jnp.int32),
            pltpu.SMEM((8, ndoc), jnp.int32),
            pltpu.SemaphoreType.DMA,
            pltpu.SemaphoreType.DMA,
            pltpu.SemaphoreType.DMA,
        ],
        compiler_params=pltpu.CompilerParams(vmem_limit_bytes=16 << 20),
        cost_estimate=FREE,
        name="pack_documents",
    )(documents, lengths, *([pattern] if planned else []))


def fold(max_ref, step_group, at, best):
    span = slice(at, at + best.shape[1])
    max_ref[step_group, :, span] = jnp.maximum(max_ref[step_group, :, span], best)


def streamed_maxima(b, steps_ref, docs_ref, q_ref, u, max_ref, accs):
    width = q_ref.shape[2]
    rounds = steps_ref[2 * b + 1, 0]
    none_q = jnp.zeros((q_ref.shape[1], 256), q_ref.dtype)
    none_d = jnp.zeros((SUB, q_ref.shape[1]), q_ref.dtype)

    def feed(step, slot, staged):
        rows = docs_ref[pl.ds(pl.multiple_of(step * SUB, SUB), SUB), :]
        rows = jnp.concatenate([rows, none_d], axis=1)
        for unit in range(2):
            pltpu.matmul_acc_lhs(accs[unit][slot], rows, load_staged_rhs=staged)

    def retire(step, slot, pair):
        group = steps_ref[2 * b, step]
        for unit in range(2):
            got = pltpu.matmul_pop(accs[unit][slot])
            best = jnp.max(got.reshape(STEP, GROUP, 256), axis=0)
            fold(max_ref, group, (2 * pair + unit) * 256, best)

    for pair in range(width // 512):
        for unit in range(2):
            at = (2 * pair + unit) * 256
            pltpu.matmul_push_rhs(jnp.concatenate([q_ref[u, :, at:at + 256], none_q], axis=0), pair % 2, unit)
        for slot in range(RING):
            feed(slot, slot, pair % 2 if slot == 0 else None)
            if slot >= LAG:
                retire(slot - LAG, slot - LAG, pair)

        @pl.loop(1, rounds)
        def _(r, pair=pair):
            for slot in range(RING):
                step = r * RING + slot
                feed(step, slot, None)
                retire(step - LAG, (slot - LAG) % RING, pair)

        for k in range(RING - LAG, RING):
            retire((rounds - 1) * RING + k, k, pair)


def plain_maxima(b, steps_ref, docs_ref, q_ref, u, max_ref):
    @pl.loop(0, steps_ref[2 * b + 1, 0] * RING)
    def _(step):
        rows = docs_ref[pl.ds(pl.multiple_of(step * SUB, SUB), SUB), :]
        similar = jnp.dot(rows, q_ref[u], preferred_element_type=jnp.float32)
        fold(max_ref, steps_ref[2 * b, step], 0, jnp.max(similar.reshape(STEP, GROUP, similar.shape[1]), axis=0))


def score_kernel(plan_ref, steps_ref, own_docs, other_docs, own_rank, other_rank, *refs, calls):
    arrays = calls[-1][0]
    sent, refs = refs[:arrays], refs[arrays + 2:]
    own_out, other_out, max_ref, q_ref, score_ref, q_sem, score_sem = refs
    count, ndoc = score_ref.shape[1:]
    width = q_ref.shape[2]
    groups = ndoc // GROUP
    core, _ = seat()
    begin = end = jnp.int32(0)
    for arrived, budget in calls:
        begin, end = end, plan_ref[1, arrived]
        if budget is not None:
            end = jnp.minimum(begin + budget, end)

    def fetch(n):
        job = plan_ref[0, n] % JOBS
        for a in range(arrays):
            @pl.when(job // 4 == a)
            def _(a=a):
                pltpu.make_async_copy(sent[a].at[(job // 2) % 2], q_ref.at[n % 2], q_sem.at[n % 2]).start()

    def written(slot):
        pltpu.make_async_copy(score_ref.at[slot], other_out.at[0], score_sem.at[slot]).wait()

    def scores(b, docs_ref, rank_ref, slot, *flat):
        max_ref[...] = jnp.full(max_ref.shape, LOWEST, jnp.float32)
        if flat:
            streamed_maxima(b, steps_ref, docs_ref, q_ref, slot, max_ref, (flat[:RING], flat[RING:2 * RING]))
        else:
            plain_maxima(b, steps_ref, docs_ref, q_ref, slot, max_ref)
        sums = []
        for g in range(groups):
            total = max_ref[g, :, :128]
            for j in range(1, width // 128):
                total = total + max_ref[g, :, j * 128:(j + 1) * 128]
            sums.append(total)
        turned = jnp.concatenate(sums, axis=0).T
        score = turned[:count]
        for j in range(1, 128 // count):
            score = score + turned[j * count:(j + 1) * count]
        score = jnp.take_along_axis(score, jnp.broadcast_to(rank_ref[...], score.shape), axis=1)
        score_ref[slot] = score

    @pl.when(begin < end)
    def _():
        fetch(begin)

    @pl.loop(begin, end)
    def _(n):
        slot = n % 2
        job, there = plan_ref[0, n] % JOBS, plan_ref[0, n] // JOBS

        @pl.when(n + 1 < end)
        def _():
            fetch(n + 1)

        pltpu.make_async_copy(sent[0].at[0], q_ref.at[slot], q_sem.at[slot]).wait()

        @pl.when(n >= begin + 2)
        def _():
            written(slot)

        for b in range(2):
            @pl.when(job % 2 == b)
            def _(b=b):
                run = functools.partial(scores, b, (own_docs, other_docs)[b], (own_rank, other_rank)[b], slot)
                if width % 512 == 0:
                    pl.run_scoped(
                        run,
                        *[pltpu.ACC(mxu_id=x)((SUB, 256), jnp.float32) for x in range(2) for _ in range(RING)],
                    )
                else:
                    run()
                row = own_out.at[2 * there + core] if b == 0 else other_out.at[there]
                pltpu.make_async_copy(score_ref.at[slot], row, score_sem.at[slot]).start()

    for k in (2, 1):
        @pl.when(end >= begin + k)
        def _(k=k):
            written((end - k) % 2)


def score_jobs(plan, steps, packs, sent, outs, calls, cost):
    width_dim, width = sent[0].shape[1:]
    _, count, ndoc = outs[0].shape
    (own_docs, own_rank), (other_docs, other_rank) = packs
    fixed = 6 + len(sent)
    return pl.pallas_call(
        functools.partial(score_kernel, calls=calls),
        out_shape=[jax.ShapeDtypeStruct(o.shape, o.dtype) for o in outs],
        in_specs=[SMEM] * 2 + [VMEM] * 4 + [ANY] * len(sent) + [HBM] * 2,
        out_specs=[HBM] * 2,
        scratch_shapes=[
            pltpu.VMEM((ndoc // GROUP + 1, GROUP, width), jnp.float32),
            pltpu.VMEM((2, width_dim, width), sent[0].dtype),
            pltpu.VMEM((2, count, ndoc), jnp.float32),
            pltpu.SemaphoreType.DMA((2,)),
            pltpu.SemaphoreType.DMA((2,)),
        ],
        input_output_aliases={fixed: 0, fixed + 1: 1},
        compiler_params=pltpu.CompilerParams(vmem_limit_bytes=16 << 20),
        cost_estimate=cost,
        name="score_jobs",
    )(plan, steps, own_docs, other_docs, own_rank, other_rank, *sent, *outs)


def place_kernel(got_ref, _, out_ref, sem):
    core, _ = seat()
    copies = [pltpu.make_async_copy(got_ref.at[c], out_ref.at[2 * c + 1 - core], sem.at[c]) for c in range(got_ref.shape[0])]
    for copy in copies:
        copy.start()
    for copy in copies:
        copy.wait()


def place_scores(got, out):
    return pl.pallas_call(
        place_kernel,
        out_shape=jax.ShapeDtypeStruct(out.shape, out.dtype),
        in_specs=[ANY, HBM],
        out_specs=HBM,
        scratch_shapes=[pltpu.SemaphoreType.DMA((got.shape[0],))],
        input_output_aliases={1: 0},
        compiler_params=pltpu.CompilerParams(vmem_limit_bytes=4 << 20),
        cost_estimate=FREE,
        name="place_scores",
    )(got, out)


def xor_pairs(devices, even, odd):
    return [(i, ((i // 2) ^ (odd if i % 2 else even)) * 2 + i % 2) for i in range(devices)]


def after(array, *others):
    return lax.optimization_barrier((array, *others))[0]


def local(queries, documents, lengths, pattern):
    devices = lax.axis_size("docs")
    halves = lax.axis_size("pb")
    planes = devices // 8
    shard_rows = queries.shape[0]
    swap = [(i, i ^ 1) for i in range(devices)]

    if halves > 1:
        queries = lax.all_to_all(queries, "pb", split_axis=0, concat_axis=1, tiled=True)
    count = queries.shape[0]

    def send(array, even, odd=None):
        return lax.ppermute(array, "docs", xor_pairs(devices, even, even if odd is None else odd))

    def join(a, b):
        return jnp.concatenate([a, b], axis=0)

    unit = turn_queries(queries)
    crossed = {e: send(unit, 4 * e) for e in range(2, planes, 2)}

    def held(array):
        return pltpu.with_memory_space_constraint(array, pltpu.HBM)

    order = [(0, 0), (0, 1)]
    for z in range(2, planes, 2):
        order += [(z, 0), (z - 1, 0), (z, 1), (z - 1, 1)]
    if planes > 1:
        order += [(planes - 1, 0), (planes - 1, 1)]

    lengths = lengths.reshape(1, -1)
    *own_pack, own_steps = pack_documents(held(documents), held(lengths), HBM)
    *other_pack, other_steps, plan = pack_documents(
        lax.ppermute(documents, "docs", swap), lax.ppermute(lengths, "docs", swap), ANY,
        pattern, tuple(order), shard_rows, count)
    packs = (own_pack, other_pack)
    steps = jnp.concatenate([own_steps, other_steps], axis=0)

    sent, calls = [], []
    outs = [jnp.zeros((n, count, lengths.shape[1]), jnp.float32) for n in (devices, devices // 2)]

    def score(arrays, budget, busy=False):
        sent.extend(arrays)
        calls.append((len(sent), budget))
        outs[:] = score_jobs(plan, steps, packs, sent, outs, tuple(calls), BUSY if busy else FREE)

    def later(*arrays):
        *arrays, outs[1] = lax.optimization_barrier((*arrays, outs[1]))
        return arrays if len(arrays) > 1 else arrays[0]

    def spread(here):
        return join(here, send(here, 1, 2))

    def onward(near, z):
        return send(near, 4) if z + 1 < planes else None, send(near, 2, 1)

    beside = send(unit, 1, 2)
    beside, outs[0], outs[1], _ = lax.optimization_barrier((beside, *outs, own_steps))
    near = join(unit, beside)
    pair, far = onward(near, 0)
    if planes > 2:
        score([near], 1)
        upcoming = spread(later(crossed[2]))
        score([], 1, busy=True)
        ready = [later(far)]
    else:
        score([near], 1)
        score([later(far)], 1 if planes > 1 else None)
        ready = []
    waiting = None
    for z in range(2, planes, 2):
        near = later(upcoming)
        before, (pair, far) = pair, onward(near, z)
        before = after(later(before), near)
        before_far = send(before, 2, 1)
        score(ready + [near, before], 4)
        ready = []
        waiting = [far, before_far]
        if z + 2 < planes:
            upcoming = spread(later(crossed[z + 2]))
            score(later(*waiting), 2)
            waiting = []
    if pair is not None:
        pair = later(pair)
        pair_far = send(pair, 2, 1)
        score((later(*waiting) if waiting else []) + [pair], 4)
        score([later(pair_far)], None)
    own, other = outs
    return place_scores(lax.ppermute(other, "docs", swap), own)


def solution(mesh):
    mapped = jax.shard_map(
        local,
        mesh=mesh,
        in_specs=(P("docs", "pb", None), P("docs", None, None), P("docs"), P()),
        out_specs=P(None, "pb", "docs"),
        check_vma=False,
    )

    def run(*arrays):
        with jax.sharding.use_abstract_mesh(mesh.abstract_mesh):
            return mapped(*arrays)

    return run
```

```python
import functools

import jax
import jax.numpy as jnp
from jax import lax
from jax.experimental import pallas as pl
from jax.experimental.pallas import tpu as pltpu
from jax.sharding import PartitionSpec as P

BLOCK = 128
GROUP = 8
STEP = 8
SUB = GROUP * STEP
RING = 8
LAG = 7
PAD = 8
SIDE = 2
LOWEST = -3e38
JOBS = 256
VMEM = pl.BlockSpec(memory_space=pltpu.VMEM)
SMEM = pl.BlockSpec(memory_space=pltpu.SMEM)
ANY = pl.BlockSpec(memory_space=pl.ANY)
HBM = pl.BlockSpec(memory_space=pltpu.HBM)
FREE = pl.CostEstimate(flops=0, bytes_accessed=0, transcendentals=0)
BUSY = pl.CostEstimate(flops=16 << 30, bytes_accessed=0, transcendentals=0)


def query_kernel(q_ref, out_ref, rows_ref):
    count, tokens, _ = q_ref.shape
    pitch = rows_ref.shape[0] // count
    for i in range(count):
        rows_ref[i * pitch:i * pitch + tokens, :] = q_ref[i].astype(jnp.float32)
    span = 128 // count
    for j in range(tokens // span):
        parts = [rows_ref[pl.ds(j * span + t, count, stride=pitch), :] for t in range(span)]
        out_ref[0, :, j * 128:(j + 1) * 128] = jnp.concatenate(parts, axis=0).T.astype(out_ref.dtype)


def turn_queries(queries):
    count, tokens, width = queries.shape
    return pl.pallas_call(
        query_kernel,
        out_shape=jax.ShapeDtypeStruct((1, width, tokens * count), queries.dtype),
        in_specs=[VMEM],
        out_specs=VMEM,
        scratch_shapes=[pltpu.VMEM((count * (tokens + PAD), width), jnp.float32)],
        compiler_params=pltpu.CompilerParams(vmem_limit_bytes=4 << 20),
        cost_estimate=FREE,
        name="turn_queries",
    )(queries)


def sort_tables(length, parts):
    ndoc = length.shape[1]
    square = (ndoc, ndoc)
    down = lax.broadcasted_iota(jnp.int32, square, 0)
    across = lax.broadcasted_iota(jnp.int32, square, 1)
    down_f, across_f = down.astype(jnp.float32), across.astype(jnp.float32)
    len_across = jnp.broadcast_to(length.astype(jnp.float32), square)
    len_down = len_across.T

    def count(hits, axis):
        return jnp.sum(jnp.where(hits, 1.0, 0.0), axis=axis, keepdims=True)

    ahead = (len_across > len_down) | ((len_across == len_down) & (across < down))
    behind = (len_down > len_across) | ((len_down == len_across) & (down < across))
    rank_down = count(ahead, 1)
    rank_across = count(behind, 0)
    placed = rank_across == down_f
    limit_down = jnp.sum(jnp.where(placed, len_across, 0.0), axis=1, keepdims=True)
    taken = rank_down == across_f
    order = jnp.sum(jnp.where(taken, down_f, 0.0), axis=0, keepdims=True)
    limit_across = jnp.sum(jnp.where(taken, len_down, 0.0), axis=0, keepdims=True)

    def steps_of(limit):
        return jnp.broadcast_to(((limit.astype(jnp.int32) + (STEP - 1)) // STEP).astype(jnp.float32), square)

    steps_down, steps_across = steps_of(limit_down), steps_of(limit_across)
    head_down, head_across = down % GROUP == 0, across % GROUP == 0
    starts = jnp.sum(jnp.where(head_down & (down < across * GROUP), steps_down, 0.0), axis=0, keepdims=True)
    ends = jnp.sum(jnp.where(head_across & (across <= down), steps_across, 0.0), axis=1, keepdims=True)
    group = jnp.concatenate([count(head_down & (ends <= across_f + part * ndoc), 0) for part in range(parts)], axis=1)
    total = jnp.sum(jnp.where(head_down, steps_down, 0.0), axis=0, keepdims=True).astype(jnp.int32)
    rounds = (total + (RING - 1)) // RING
    return order.astype(jnp.int32), starts.astype(jnp.int32), limit_down, group.astype(jnp.int32), rounds, rank_across.astype(jnp.int32)


def seat():
    me = lax.axis_index("docs")
    return me % 2, me // 2


def plan_jobs(pattern_ref, plan_ref, order, shard_rows, count):
    core, chip = seat()
    blocks, columns = pattern_ref.shape
    wide = plan_ref.shape[1]
    job = lax.broadcasted_iota(jnp.int32, (1, wide), 1)
    at, i, b = job >> 2, (job >> 1) & 1, job & 1
    plane = sum(jnp.where(at == k, z, 0) for k, (z, _) in enumerate(order))
    past = sum(jnp.where(at == k, p, 0) for k, (_, p) in enumerate(order))
    there = chip ^ (4 * plane + jnp.where(core == 0, 2 * past + i, past + 2 * i))
    first = (2 * there + core) * shard_rows + lax.axis_index("pb") * count
    block = jnp.right_shift(first, BLOCK.bit_length() - 1)

    column = lax.broadcasted_iota(jnp.int32, (blocks, columns), 1)
    wanted = jnp.where(pattern_ref[...] > 0, 1.0, 0.0)
    own, other = [jnp.sum(jnp.where(column == 2 * chip + (core ^ k), wanted, 0.0), axis=1, keepdims=True) for k in range(2)]
    hit = lax.broadcasted_iota(jnp.int32, (blocks, wide), 0) == block
    active = jnp.sum(jnp.where(hit, jnp.where(b == 0, own, other), 0.0), axis=0, keepdims=True)
    active = jnp.where(job < 4 * len(order), active, 0.0)

    square = (wide, wide)
    down = lax.broadcasted_iota(jnp.int32, square, 0)
    across = lax.broadcasted_iota(jnp.int32, square, 1)
    active_across = jnp.broadcast_to(active, square)
    active_down = active_across.T
    name_down = jnp.broadcast_to((there * JOBS + job).astype(jnp.float32), square).T
    before_down = jnp.sum(jnp.where(across < down, active_across, 0.0), axis=1, keepdims=True)
    chosen = (active_down > 0) & (before_down == across.astype(jnp.float32))
    names = jnp.sum(jnp.where(chosen, name_down, 0.0), axis=0, keepdims=True)
    counts = jnp.sum(jnp.where(down < 4 * across, active_down, 0.0), axis=0, keepdims=True)
    plan_ref[...] = jnp.concatenate([names, counts], axis=0).astype(jnp.int32)


def document_kernel(docs_hbm, length_hbm, *refs, order, shard_rows, count):
    if order:
        pattern_ref, out_ref, rank_ref, steps_ref, plan_ref, *scratch = refs
    else:
        out_ref, rank_ref, steps_ref, *scratch = refs
    turns = docs_hbm.shape[0] // GROUP // SIDE
    if order:
        core, chip = seat()
        column = lax.broadcasted_iota(jnp.int32, pattern_ref.shape, 1)
        hits = (column == 2 * chip + 1 - core) & (pattern_ref[...] > 0)
        turns = jnp.where(jnp.sum(jnp.where(hits, 1.0, 0.0)) > 0, turns, 0)
    pack_block(turns, docs_hbm, length_hbm, out_ref, rank_ref, steps_ref, *scratch)
    if order:
        plan_jobs(pattern_ref, plan_ref, order, shard_rows, count)


def pack_block(turns, docs_hbm, length_hbm, out_ref, rank_ref, steps_ref,
                    docs_ref, rows_ref, limit_ref, length_ref, row_ref, table_ref, docs_sem, length_sem, sem):
    ndoc, slots, _ = docs_hbm.shape
    pitch = rows_ref.shape[1] // GROUP
    length_copy = pltpu.make_async_copy(length_hbm, length_ref, length_sem)
    docs_copy = pltpu.make_async_copy(docs_hbm, docs_ref, docs_sem)
    length_copy.start()
    docs_copy.start()
    length_copy.wait()
    sequence, starts, limit, group, rounds, rank = sort_tables(length_ref[...], steps_ref.shape[1] // ndoc)
    row_ref[0:1, :] = sequence
    row_ref[1:2, :] = starts
    to_scalars = pltpu.make_async_copy(row_ref, table_ref, sem)
    to_scalars.start()
    limit_ref[...] = limit
    steps_ref[0:1, :] = group
    steps_ref[1:2, :] = jnp.concatenate([rounds] * (steps_ref.shape[1] // ndoc), axis=1)
    rank_ref[...] = rank
    to_scalars.wait()
    docs_copy.wait()

    @pl.loop(0, turns)
    def _(turn):
        for side in range(SIDE):
            g = turn * SIDE + side
            for i in range(GROUP):
                doc = table_ref[0, g * GROUP + i]
                rows_ref[side, i * pitch:i * pitch + slots, :] = docs_ref[doc].astype(jnp.float32)
        for side in range(SIDE):
            g = turn * SIDE + side
            limit = limit_ref[pl.ds(pl.multiple_of(g * GROUP, GROUP), GROUP), :].astype(jnp.int32)
            first = rows_ref[side, pl.ds(0, GROUP, stride=pitch), :]
            base = table_ref[1, g] * SUB
            for s in range(0, slots, 2):
                pair = []
                for k in (s, s + 1):
                    tile = rows_ref[side, pl.ds(k, GROUP, stride=pitch), :]
                    pair.append(jnp.where(limit > k, tile, first))
                at = pl.multiple_of(base + s * GROUP, 2 * GROUP)
                out_ref[pl.ds(at, 2 * GROUP), :] = jnp.concatenate(pair, axis=0).astype(out_ref.dtype)


def pack_documents(documents, lengths, space, pattern=None, order=(), shard_rows=0, count=0):
    ndoc, slots, width = documents.shape
    out_shape = [
        jax.ShapeDtypeStruct((ndoc * slots, width), documents.dtype),
        jax.ShapeDtypeStruct((1, ndoc), jnp.int32),
        jax.ShapeDtypeStruct((2, ndoc // GROUP * slots // STEP), jnp.int32),
    ]
    planned = pattern is not None
    if planned:
        out_shape.append(jax.ShapeDtypeStruct((2, ndoc), jnp.int32))
    return pl.pallas_call(
        functools.partial(document_kernel, order=order, shard_rows=shard_rows, count=count),
        out_shape=out_shape,
        in_specs=[space, space] + [VMEM] * planned,
        out_specs=[VMEM, VMEM, VMEM] + [VMEM] * planned,
        scratch_shapes=[
            pltpu.VMEM((ndoc, slots, width), documents.dtype),
            pltpu.VMEM((SIDE, GROUP * (slots + PAD), width), jnp.float32),
            pltpu.VMEM((ndoc, 1), jnp.float32),
            pltpu.VMEM((1, ndoc), jnp.int32),
            pltpu.VMEM((8, ndoc), jnp.int32),
            pltpu.SMEM((8, ndoc), jnp.int32),
            pltpu.SemaphoreType.DMA,
            pltpu.SemaphoreType.DMA,
            pltpu.SemaphoreType.DMA,
        ],
        compiler_params=pltpu.CompilerParams(vmem_limit_bytes=16 << 20),
        cost_estimate=FREE,
        name="pack_documents",
    )(documents, lengths, *([pattern] if planned else []))


def fold(max_ref, step_group, at, best):
    span = slice(at, at + best.shape[1])
    max_ref[step_group, :, span] = jnp.maximum(max_ref[step_group, :, span], best)


def streamed_maxima(b, steps_ref, docs_ref, q_ref, u, max_ref, accs):
    width = q_ref.shape[2]
    rounds = steps_ref[2 * b + 1, 0]
    none_q = jnp.zeros((q_ref.shape[1], 256), q_ref.dtype)
    none_d = jnp.zeros((SUB, q_ref.shape[1]), q_ref.dtype)

    def feed(step, slot, staged):
        rows = docs_ref[pl.ds(pl.multiple_of(step * SUB, SUB), SUB), :]
        rows = jnp.concatenate([rows, none_d], axis=1)
        for unit in range(2):
            pltpu.matmul_acc_lhs(accs[unit][slot], rows, load_staged_rhs=staged)

    def retire(step, slot, pair):
        group = steps_ref[2 * b, step]
        for unit in range(2):
            got = pltpu.matmul_pop(accs[unit][slot])
            best = jnp.max(got.reshape(STEP, GROUP, 256), axis=0)
            fold(max_ref, group, (2 * pair + unit) * 256, best)

    for pair in range(width // 512):
        for unit in range(2):
            at = (2 * pair + unit) * 256
            pltpu.matmul_push_rhs(jnp.concatenate([q_ref[u, :, at:at + 256], none_q], axis=0), pair % 2, unit)
        for slot in range(RING):
            feed(slot, slot, pair % 2 if slot == 0 else None)
            if slot >= LAG:
                retire(slot - LAG, slot - LAG, pair)

        @pl.loop(1, rounds)
        def _(r, pair=pair):
            for slot in range(RING):
                step = r * RING + slot
                feed(step, slot, None)
                retire(step - LAG, (slot - LAG) % RING, pair)

        for k in range(RING - LAG, RING):
            retire((rounds - 1) * RING + k, k, pair)


def plain_maxima(b, steps_ref, docs_ref, q_ref, u, max_ref):
    @pl.loop(0, steps_ref[2 * b + 1, 0] * RING)
    def _(step):
        rows = docs_ref[pl.ds(pl.multiple_of(step * SUB, SUB), SUB), :]
        similar = jnp.dot(rows, q_ref[u], preferred_element_type=jnp.float32)
        fold(max_ref, steps_ref[2 * b, step], 0, jnp.max(similar.reshape(STEP, GROUP, similar.shape[1]), axis=0))


def score_kernel(plan_ref, steps_ref, own_docs, other_docs, own_rank, other_rank, *refs, calls):
    arrays = calls[-1][0]
    sent, refs = refs[:arrays], refs[arrays + 2:]
    own_out, other_out, max_ref, q_ref, score_ref, q_sem, score_sem = refs
    count, ndoc = score_ref.shape[1:]
    width = q_ref.shape[2]
    groups = ndoc // GROUP
    core, _ = seat()
    begin = end = jnp.int32(0)
    for arrived, budget in calls:
        begin, end = end, plan_ref[1, arrived]
        if budget is not None:
            end = jnp.minimum(begin + budget, end)

    def fetch(n):
        job = plan_ref[0, n] % JOBS
        for a in range(arrays):
            @pl.when(job // 4 == a)
            def _(a=a):
                pltpu.make_async_copy(sent[a].at[(job // 2) % 2], q_ref.at[n % 2], q_sem.at[n % 2]).start()

    def written(slot):
        pltpu.make_async_copy(score_ref.at[slot], other_out.at[0], score_sem.at[slot]).wait()

    def scores(b, docs_ref, rank_ref, slot, *flat):
        max_ref[...] = jnp.full(max_ref.shape, LOWEST, jnp.float32)
        if flat:
            streamed_maxima(b, steps_ref, docs_ref, q_ref, slot, max_ref, (flat[:RING], flat[RING:2 * RING]))
        else:
            plain_maxima(b, steps_ref, docs_ref, q_ref, slot, max_ref)
        sums = []
        for g in range(groups):
            total = max_ref[g, :, :128]
            for j in range(1, width // 128):
                total = total + max_ref[g, :, j * 128:(j + 1) * 128]
            sums.append(total)
        turned = jnp.concatenate(sums, axis=0).T
        score = turned[:count]
        for j in range(1, 128 // count):
            score = score + turned[j * count:(j + 1) * count]
        score = jnp.take_along_axis(score, jnp.broadcast_to(rank_ref[...], score.shape), axis=1)
        score_ref[slot] = score

    @pl.when(begin < end)
    def _():
        fetch(begin)

    @pl.loop(begin, end)
    def _(n):
        slot = n % 2
        job, there = plan_ref[0, n] % JOBS, plan_ref[0, n] // JOBS

        @pl.when(n + 1 < end)
        def _():
            fetch(n + 1)

        pltpu.make_async_copy(sent[0].at[0], q_ref.at[slot], q_sem.at[slot]).wait()

        @pl.when(n >= begin + 2)
        def _():
            written(slot)

        for b in range(2):
            @pl.when(job % 2 == b)
            def _(b=b):
                run = functools.partial(scores, b, (own_docs, other_docs)[b], (own_rank, other_rank)[b], slot)
                if width % 512 == 0:
                    pl.run_scoped(
                        run,
                        *[pltpu.ACC(mxu_id=x)((SUB, 256), jnp.float32) for x in range(2) for _ in range(RING)],
                    )
                else:
                    run()
                row = own_out.at[2 * there + core] if b == 0 else other_out.at[there]
                pltpu.make_async_copy(score_ref.at[slot], row, score_sem.at[slot]).start()

    for k in (2, 1):
        @pl.when(end >= begin + k)
        def _(k=k):
            written((end - k) % 2)


def score_jobs(plan, steps, packs, sent, outs, calls, cost):
    width_dim, width = sent[0].shape[1:]
    _, count, ndoc = outs[0].shape
    (own_docs, own_rank), (other_docs, other_rank) = packs
    fixed = 6 + len(sent)
    return pl.pallas_call(
        functools.partial(score_kernel, calls=calls),
        out_shape=[jax.ShapeDtypeStruct(o.shape, o.dtype) for o in outs],
        in_specs=[SMEM] * 2 + [VMEM] * 4 + [ANY] * len(sent) + [HBM] * 2,
        out_specs=[HBM] * 2,
        scratch_shapes=[
            pltpu.VMEM((ndoc // GROUP + 1, GROUP, width), jnp.float32),
            pltpu.VMEM((2, width_dim, width), sent[0].dtype),
            pltpu.VMEM((2, count, ndoc), jnp.float32),
            pltpu.SemaphoreType.DMA((2,)),
            pltpu.SemaphoreType.DMA((2,)),
        ],
        input_output_aliases={fixed: 0, fixed + 1: 1},
        compiler_params=pltpu.CompilerParams(vmem_limit_bytes=16 << 20),
        cost_estimate=cost,
        name="score_jobs",
    )(plan, steps, own_docs, other_docs, own_rank, other_rank, *sent, *outs)


def place_kernel(got_ref, _, out_ref, sem):
    core, _ = seat()
    copies = [pltpu.make_async_copy(got_ref.at[c], out_ref.at[2 * c + 1 - core], sem.at[c]) for c in range(got_ref.shape[0])]
    for copy in copies:
        copy.start()
    for copy in copies:
        copy.wait()


def place_scores(got, out):
    return pl.pallas_call(
        place_kernel,
        out_shape=jax.ShapeDtypeStruct(out.shape, out.dtype),
        in_specs=[ANY, HBM],
        out_specs=HBM,
        scratch_shapes=[pltpu.SemaphoreType.DMA((got.shape[0],))],
        input_output_aliases={1: 0},
        compiler_params=pltpu.CompilerParams(vmem_limit_bytes=4 << 20),
        cost_estimate=FREE,
        name="place_scores",
    )(got, out)


def xor_pairs(devices, even, odd):
    return [(i, ((i // 2) ^ (odd if i % 2 else even)) * 2 + i % 2) for i in range(devices)]


def after(array, *others):
    return lax.optimization_barrier((array, *others))[0]


def local(queries, documents, lengths, pattern):
    devices = lax.axis_size("docs")
    halves = lax.axis_size("pb")
    planes = devices // 8
    shard_rows = queries.shape[0]
    swap = [(i, i ^ 1) for i in range(devices)]

    if halves > 1:
        queries = lax.all_to_all(queries, "pb", split_axis=0, concat_axis=1, tiled=True)
    count = queries.shape[0]

    def send(array, even, odd=None):
        return lax.ppermute(array, "docs", xor_pairs(devices, even, even if odd is None else odd))

    def join(a, b):
        return jnp.concatenate([a, b], axis=0)

    unit = turn_queries(queries)
    crossed = {e: send(unit, 4 * e) for e in range(2, planes, 2)}

    def held(array):
        return pltpu.with_memory_space_constraint(array, pltpu.HBM)

    order = [(0, 0), (0, 1)]
    for z in range(2, planes, 2):
        order += [(z, 0), (z - 1, 0), (z, 1), (z - 1, 1)]
    if planes > 1:
        order += [(planes - 1, 0), (planes - 1, 1)]

    lengths = lengths.reshape(1, -1)
    *own_pack, own_steps = pack_documents(held(documents), held(lengths), HBM)
    *other_pack, other_steps, plan = pack_documents(
        lax.ppermute(documents, "docs", swap), lax.ppermute(lengths, "docs", swap), ANY,
        pattern, tuple(order), shard_rows, count)
    packs = (own_pack, other_pack)
    steps = jnp.concatenate([own_steps, other_steps], axis=0)

    sent, calls = [], []
    outs = [jnp.zeros((n, count, lengths.shape[1]), jnp.float32) for n in (devices, devices // 2)]

    def score(arrays, budget, busy=False):
        sent.extend(arrays)
        calls.append((len(sent), budget))
        outs[:] = score_jobs(plan, steps, packs, sent, outs, tuple(calls), BUSY if busy else FREE)

    def later(*arrays):
        *arrays, outs[1] = lax.optimization_barrier((*arrays, outs[1]))
        return arrays if len(arrays) > 1 else arrays[0]

    def spread(here):
        return join(here, send(here, 1, 2))

    def onward(near, z):
        return send(near, 4) if z + 1 < planes else None, send(near, 2, 1)

    beside = send(unit, 1, 2)
    beside, outs[0], outs[1], _ = lax.optimization_barrier((beside, *outs, own_steps))
    near = join(unit, beside)
    pair, far = onward(near, 0)
    if planes > 2:
        score([near], 1)
        upcoming = spread(later(crossed[2]))
        score([], 1, busy=True)
        ready = [later(far)]
    else:
        score([near], 1)
        score([later(far)], 1 if planes > 1 else None)
        ready = []
    waiting = None
    for z in range(2, planes, 2):
        near = later(upcoming)
        before, (pair, far) = pair, onward(near, z)
        before = after(later(before), near)
        before_far = send(before, 2, 1)
        score(ready + [near, before], 4)
        ready = []
        waiting = [far, before_far]
        if z + 2 < planes:
            upcoming = spread(later(crossed[z + 2]))
            score(later(*waiting), 2)
            waiting = []
    if pair is not None:
        pair = later(pair)
        pair_far = send(pair, 2, 1)
        score((later(*waiting) if waiting else []) + [pair], 4)
        score([later(pair_far)], None)
    own, other = outs
    return place_scores(lax.ppermute(other, "docs", swap), own)


def solution(mesh):
    mapped = jax.shard_map(
        local,
        mesh=mesh,
        in_specs=(P("docs", "pb", None), P("docs", None, None), P("docs"), P()),
        out_specs=P(None, "pb", "docs"),
        check_vma=False,
    )

    def run(*arrays):
        with jax.sharding.use_abstract_mesh(mesh.abstract_mesh):
            return mapped(*arrays)

    return run
```
